32 devices in a mesh: seq: 8 (over z, y), head: 4 (over x, core).
Axes of the slice: x: 2, y: 2, z: 4, core: 2. Of those that a mesh axis runs over, the one named last changes fastest.
Arguments:
- block_in: bfloat16 [4, 2048, 768], P(None, 'seq'), may hold values from -6 to 6
- cotangent: bfloat16 [4, 2048, 768], P(None, 'seq'), may hold values from -6 to 6
- lengths: int32 [4], replicated, may hold values from 512 to 2048, as said below
- norm_gain: float32 [768], replicated, may hold values from 0.5 to 1.5
- in_proj: float32 [768, 4, 838], P(None, 'head'), may hold values from -0.21875 to 0.21875
- conv_params: float32 [5, 4, 448], P(None, 'head'), may hold values from -2 to 2
- head_params: float32 [3, 24], P(None, 'head'), as said below
- gate_gain: float32 [1536], P('head'), may hold values from 0.5 to 1.5
- out_proj: float32 [1536, 768], P('head'), may hold values from -0.15625 to 0.15625
- norm_gain_momentum: float32 [768], replicated, may hold values from -224 to 224
- in_proj_momentum: float32 [768, 4, 838], P(None, 'head'), may hold values from -112 to 112
- conv_momentum: float32 [5, 4, 448], P(None, 'head'), may hold values from -112 to 112
- head_momentum: float32 [3, 24], P(None, 'head'), may hold values from -512 to 512
- gate_gain_momentum: float32 [1536], P('head'), may hold values from -256 to 256
- out_proj_momentum: float32 [1536, 768], P('head'), may hold values from -384 to 384
- norm_gain_average: float32 [768], replicated, may hold values from 0.5 to 1.5
- in_proj_average: float32 [768, 4, 838], P(None, 'head'), may hold values from -0.21875 to 0.21875
- conv_average: float32 [5, 4, 448], P(None, 'head'), may hold values from -2 to 2
- head_average: float32 [3, 24], P(None, 'head'), may hold values from -1 to 1
- gate_gain_average: float32 [1536], P('head'), may hold values from 0.5 to 1.5
- out_proj_average: float32 [1536, 768], P('head'), may hold values from -0.15625 to 0.15625
Outputs:
- block_out: bfloat16 [4, 2048, 768], P(None, 'seq')
- input_grad: float32 [4, 2048, 768], P(None, 'seq')
- norm_gain_new: float32 [768], replicated
- norm_gain_moment: float32 [768], replicated
- norm_gain_mean: float32 [768], replicated
- in_proj_new: float32 [768, 4, 838], P(None, 'head')
- in_proj_moment: float32 [768, 4, 838], P(None, 'head')
- in_proj_mean: float32 [768, 4, 838], P(None, 'head')
- conv_new: float32 [5, 4, 448], P(None, 'head')
- conv_moment: float32 [5, 4, 448], P(None, 'head')
- conv_mean: float32 [5, 4, 448], P(None, 'head')
- head_new: float32 [3, 24], P(None, 'head')
- head_moment: float32 [3, 24], P(None, 'head')
- head_mean: float32 [3, 24], P(None, 'head')
- gate_gain_new: float32 [1536], P('head')
- gate_gain_moment: float32 [1536], P('head')
- gate_gain_mean: float32 [1536], P('head')
- out_proj_new: float32 [1536, 768], P('head')
- out_proj_moment: float32 [1536, 768], P('head')
- out_proj_mean: float32 [1536, 768], P('head')
The draws below stay inside these ranges and needn't reach their ends.
Inputs may be any that keep to these rules, and one draw needn't show every extreme that they name: `lengths`: in every draw one sequence has all 2048 slots real. `head_params`: row 0 lies in -5.1 to -4.1, row 1 (log decay rate) in log(0.3 / (2048 * 0.0165)) to log(2), and row 2 in 0.4 to 2.4.
All inputs are finite; a program needn't handle non-finite values.
Results may differ from the reference program's by a relative error of at most 0.01.
The reference program's roundings to bfloat16 on the way count: a program that leaves them out, or rounds other values in their place, can miss the bound.
Values may be sent and summed in bfloat16 or wider, within the bound.
No kernel may reach another device: no remote copies, remote signals or barrier semaphores. Data moves between devices by JAX's collectives and lax.ppermute only.
A program may use at most 192 MiB of HBM per device.

```python
import math
import jax
import jax.numpy as jnp
from jax import lax

D = 768
HEADS = 24
HDIM = 64
STATE = 128
CONV = 4
BLK = 256
SEQS = 4
INNER = 1536
LEN = 2048
GCOLS = 838
GCONV = 448
N_HEAD = 4


def draw_lengths(key, part):
    key = jax.random.fold_in(key, 11)
    first_key, second_key = jax.random.split(key)
    spread_lengths = jax.random.randint(first_key, (SEQS,), LEN // 4, LEN + 1)
    chosen = jax.random.randint(second_key, (), 0, SEQS)
    return jnp.where(jnp.arange(SEQS) == chosen, LEN, spread_lengths).astype(jnp.int32)


def draw_head_params(key, part):
    key = jax.random.fold_in(key, 23)
    subkeys = jax.random.split(key, 5)
    step_bias = -4.6 + jax.random.uniform(subkeys[0], (HEADS,), minval=-0.5, maxval=0.5)
    fast_share = 0.5
    fast_heads = jax.random.uniform(subkeys[1], (HEADS,)) < fast_share
    slow_rate = jax.random.uniform(subkeys[2], (HEADS,), minval=0.3, maxval=1.5) / (LEN * 0.0165)
    fast_rate = jax.random.uniform(subkeys[3], (HEADS,), minval=1.0, maxval=2.0)
    log_rate = jnp.log(jnp.where(fast_heads, fast_rate, slow_rate))
    skip_level = 0.5 + 1.5 * jnp.arange(HEADS, dtype=jnp.float32) / max(HEADS - 1, 1)
    skip_gain = skip_level * jax.random.uniform(subkeys[4], (HEADS,), minval=0.8, maxval=1.2)
    return jnp.stack([step_bias, log_rate, skip_gain]).astype(jnp.float32)


def steps_of(stream_key, extent, cuts, smallest, largest):
    level, own = 1.0, jax.random.fold_in(stream_key, 6)
    for axis_at, parts in cuts:
        steps = jnp.exp(jax.random.uniform(jax.random.fold_in(own, axis_at), (parts,), jnp.float32, smallest / len(cuts), largest / len(cuts)))
        level = level * jnp.repeat(steps, extent[axis_at] // parts).reshape([-1 if axis == axis_at else 1 for axis in range(len(extent))])
    return level


def gaussian(key, shape, spread, reach, cuts=(), kind=jnp.bfloat16):
    factor_of = steps_of(key, shape, cuts, -0.22, 0.18) if cuts else 1.0
    values = jax.random.normal(key, shape, jnp.float32) * spread * factor_of
    return jnp.minimum(jnp.maximum(values, -reach), reach).astype(kind)


def setup_inputs(seed: int = 0) -> dict:
    streams_of = jax.random.split(jax.random.key(seed), 22)
    return {
        "block_in": gaussian(streams_of[0], (SEQS, LEN, D), 1.0, 6.0, ((1, 8),)),
        "cotangent": gaussian(streams_of[1], (SEQS, LEN, D), 1.0, 6.0, ((1, 8),)),
        "lengths": draw_lengths(jax.random.fold_in(streams_of[21], 71), 0),
        "norm_gain": jnp.clip(1.0 + 0.1 * jax.random.normal(streams_of[3], (D,), jnp.float32), 0.5, 1.5),
        "in_proj": gaussian(streams_of[4], (D, N_HEAD, GCOLS), D ** -0.5, 0.21875, ((1, 4),), jnp.float32),
        "conv_params": gaussian(streams_of[5], (CONV + 1, N_HEAD, GCONV), 0.3, 2.0, ((1, 4),), jnp.float32),
        "head_params": draw_head_params(jax.random.fold_in(streams_of[21], 71), 0),
        "gate_gain": jnp.clip(1.0 + 0.1 * jax.random.normal(streams_of[7], (INNER,), jnp.float32), 0.5, 1.5),
        "out_proj": gaussian(streams_of[8], (INNER, D), INNER ** -0.5, 0.15625, ((0, 4),), jnp.float32),
        "norm_gain_momentum": gaussian(streams_of[9], (D,), (0.4 * (SEQS * LEN) ** 0.5), 224.0, (), jnp.float32),
        "in_proj_momentum": gaussian(streams_of[10], (D, N_HEAD, GCOLS), (0.2 * (SEQS * LEN) ** 0.5), 112.0, ((1, 4),), jnp.float32),
        "conv_momentum": gaussian(streams_of[11], (CONV + 1, N_HEAD, GCONV), (0.2 * (SEQS * LEN) ** 0.5), 112.0, ((1, 4),), jnp.float32),
        "head_momentum": gaussian(streams_of[12], (3, HEADS), (1.0 * (SEQS * LEN) ** 0.5), 512.0, ((1, 4),), jnp.float32),
        "gate_gain_momentum": gaussian(streams_of[13], (INNER,), (0.5 * (SEQS * LEN) ** 0.5), 256.0, ((0, 4),), jnp.float32),
        "out_proj_momentum": gaussian(streams_of[14], (INNER, D), (0.7 * (SEQS * LEN) ** 0.5), 384.0, ((0, 4),), jnp.float32),
        "norm_gain_average": jnp.clip(1.0 + 0.1 * jax.random.normal(streams_of[15], (D,), jnp.float32), 0.5, 1.5),
        "in_proj_average": gaussian(streams_of[16], (D, N_HEAD, GCOLS), D ** -0.5, 0.21875, ((1, 4),), jnp.float32),
        "conv_average": gaussian(streams_of[17], (CONV + 1, N_HEAD, GCONV), 0.3, 2.0, ((1, 4),), jnp.float32),
        "head_average": jnp.clip(jax.random.uniform(streams_of[18], (3, HEADS), jnp.float32, -1.0, 1.0) * steps_of(streams_of[18], (3, HEADS), ((1, 4),), -0.4, 0.0), -1.0, 1.0),
        "gate_gain_average": jnp.clip(1.0 + 0.1 * jax.random.normal(streams_of[19], (INNER,), jnp.float32), 0.5, 1.5),
        "out_proj_average": gaussian(streams_of[20], (INNER, D), INNER ** -0.5, 0.15625, ((0, 4),), jnp.float32),
    }


EPSILON = 1e-05
MOMENTUM = 0.5
AVERAGE = 0.5
RATES = (0.15, 0.1, 0.5, 0.05, 0.15, 0.02)
HIGHEST = lax.Precision.HIGHEST

@jax.custom_vjp
def low(v):
    return lax.optimization_barrier(v.astype(jnp.bfloat16)).astype(jnp.float32)

@jax.custom_vjp
def low_back(v):
    return v

def low_keep(v):
    return (low(v), None)

def low_pass(kept, grad):
    return (grad,)

def back_keep(v):
    return (v, None)

def back_low(kept, grad):
    return (low(grad),)
low.defvjp(low_keep, low_pass)
low_back.defvjp(back_keep, back_low)

def span_parts(x_values, b_rows, c_rows, decays, step_sizes):
    running = jnp.cumsum(decays, axis=0)
    length = running.shape[0]
    places = jnp.arange(length)
    causal = (places[:, None] >= places[None, :])[:, :, None]
    scores = jnp.dot(c_rows, b_rows.T, precision=HIGHEST)
    exponents = jnp.where(causal, running[:, None, :] - running[None, :, :], 0.0)
    weights = jnp.where(causal, jnp.exp(exponents), 0.0) * scores[:, :, None]
    inside = jnp.einsum('tsh,shp->thp', weights, step_sizes[:, :, None] * x_values, precision=HIGHEST)
    ending = running[-1]
    tail_weights = jnp.exp(ending[None, :] - running) * step_sizes
    fresh_state = jnp.einsum('shp,sn->hpn', tail_weights[:, :, None] * x_values, b_rows, precision=HIGHEST)
    return (inside, fresh_state, jnp.exp(ending), running)

def carried_term(c_rows, state_in, running):
    return jnp.einsum('tn,hpn->thp', c_rows, state_in, precision=HIGHEST) * jnp.exp(running)[:, :, None]

def span_step(state, inputs):
    x_values, b_rows, c_rows, decays, step_sizes = inputs
    inside, fresh_state, totals, running = span_parts(x_values, b_rows, c_rows, decays, step_sizes)
    result = inside + carried_term(c_rows, state, running)
    return (totals[:, None, None] * state + fresh_state, result)

def sequence_out(params, block_seq, mask_seq):
    norm_gain, in_low, conv_params, head_params, gate_gain, out_low = params
    groups = in_low.shape[1]
    z_width = INNER // groups
    s_width = STATE // groups
    c_width = z_width + 2 * s_width
    scale = lax.rsqrt(lax.optimization_barrier(jnp.mean(block_seq * block_seq, axis=-1, keepdims=True)) + EPSILON)
    normed = low(block_seq * scale * norm_gain)
    projected = low_back(jnp.dot(normed, in_low.reshape(D, -1), precision=HIGHEST)).reshape(LEN, groups, -1)
    gate_pre = projected[:, :, :z_width].reshape(LEN, INNER)
    mixed = projected[:, :, z_width:z_width + c_width]
    raw_steps = projected[:, :, z_width + c_width:].reshape(LEN, HEADS)
    padded = jnp.concatenate([jnp.zeros((CONV - 1, groups, c_width), jnp.float32), mixed], axis=0)
    summed = conv_params[CONV]
    for offset in range(CONV):
        summed = summed + conv_params[offset] * padded[offset:offset + LEN]
    active = jax.nn.silu(summed)
    x_values = active[:, :, :z_width].reshape(LEN, HEADS, HDIM)
    b_rows = low(active[:, :, z_width:z_width + s_width].reshape(LEN, STATE))
    c_rows = low(active[:, :, z_width + s_width:].reshape(LEN, STATE))
    step_sizes = jax.nn.softplus(raw_steps + head_params[0])
    decays = -jnp.exp(head_params[1]) * step_sizes
    blocks = LEN // BLK
    start_state = jnp.zeros((HEADS, HDIM, STATE), jnp.float32)
    stacked = (x_values.reshape(blocks, BLK, HEADS, HDIM), b_rows.reshape(blocks, BLK, STATE), c_rows.reshape(blocks, BLK, STATE), decays.reshape(blocks, BLK, HEADS), step_sizes.reshape(blocks, BLK, HEADS))
    last_state, mixer_out = lax.scan(jax.checkpoint(span_step), start_state, stacked)
    mixer_out = mixer_out.reshape(LEN, HEADS, HDIM) + head_params[2][:, None] * x_values
    gated = mixer_out.reshape(LEN, INNER) * jax.nn.silu(gate_pre)
    rstd = lax.rsqrt(lax.optimization_barrier(jnp.mean(gated * gated, axis=-1, keepdims=True)) + EPSILON)
    out_in = low(gated * rstd * gate_gain)
    branch = jnp.dot(out_in, out_low, precision=HIGHEST)
    return mask_seq[:, None] * (block_seq + branch)

def advance(weight, gradient, moment, average, rate):
    moment_new = MOMENTUM * moment + gradient
    weight_new = weight - rate * (gradient + MOMENTUM * moment_new)
    average_new = AVERAGE * average + (1.0 - AVERAGE) * weight_new
    return (weight_new, moment_new, average_new)

def reference(block_in, cotangent, lengths, norm_gain, in_proj, conv_params, head_params, gate_gain, out_proj, norm_gain_momentum, in_proj_momentum, conv_momentum, head_momentum, gate_gain_momentum, out_proj_momentum, norm_gain_average, in_proj_average, conv_average, head_average, gate_gain_average, out_proj_average):
    places = jnp.arange(LEN, dtype=jnp.int32)
    live_mask = (places[None, :] < lengths[:, None]).astype(jnp.float32)

    def forward(block_f, gain_n, proj_in, conv_w, heads_w, gain_g, proj_out):
        weights = (gain_n, low(proj_in), conv_w, heads_w, gain_g, low(proj_out))

        def one_sequence(seq_pair):
            return jax.checkpoint(sequence_out)(weights, seq_pair[0], seq_pair[1])
        return lax.map(one_sequence, (block_f, live_mask))
    block_f = block_in.astype(jnp.float32)
    block_out, pull_back = jax.vjp(forward, block_f, norm_gain, in_proj, conv_params, head_params, gate_gain, out_proj)
    gradients = pull_back(cotangent.astype(jnp.float32))
    root = math.sqrt(SEQS * LEN)
    ng_w, ng_m, ng_a = advance(norm_gain, gradients[1], norm_gain_momentum, norm_gain_average, RATES[0] / root)
    ip_w, ip_m, ip_a = advance(in_proj, gradients[2], in_proj_momentum, in_proj_average, RATES[1] / root)
    cv_w, cv_m, cv_a = advance(conv_params, gradients[3], conv_momentum, conv_average, RATES[2] / root)
    hd_w, hd_m, hd_a = advance(head_params, gradients[4], head_momentum, head_average, RATES[3] / root)
    gg_w, gg_m, gg_a = advance(gate_gain, gradients[5], gate_gain_momentum, gate_gain_average, RATES[4] / root)
    op_w, op_m, op_a = advance(out_proj, gradients[6], out_proj_momentum, out_proj_average, RATES[5] / root)
    return (block_out.astype(jnp.bfloat16), gradients[0], ng_w, ng_m, ng_a, ip_w, ip_m, ip_a, cv_w, cv_m, cv_a, hd_w, hd_m, hd_a, gg_w, gg_m, gg_a, op_w, op_m, op_a)
```

```python
import functools
import math

import jax
import jax.numpy as jnp
from jax import lax
from jax.experimental import pallas as pl
from jax.experimental.pallas import tpu as pltpu
from jax.sharding import PartitionSpec as P

HDIM = 64
CONV = 4
INNER = 1536
EPSILON = 1e-05
MOMENTUM = 0.5
AVERAGE = 0.5
RATES = (0.15, 0.1, 0.5, 0.05, 0.15, 0.02)
HIGHEST = lax.Precision.HIGHEST
F32 = jnp.float32
BF16 = jnp.bfloat16
GRP = 4
BLK = 256
HALF = BLK // 2
QUART = BLK // 4
D = 768
ZW = 384
NH = 6
ST = 128
SW = 32
LANES = 128
WCOLS = D // LANES
WROWS = 2 * ZW + 2 * SW
TOK = GRP * BLK
COLS = WROWS + NH
SEG1 = 2 * ZW // GRP
SEG2 = 120
BC_AT, DT_AT, TAP_AT, HD_AT, GG_AT, NG_AT = 384, 448, 456, 464, 472, 473


def nt(a, b, precision=None):
    return lax.dot_general(
        a, b, (((1,), (1,)), ((), ())), preferred_element_type=F32, precision=precision
    )


def nn(a, b, precision=None):
    return lax.dot_general(
        a, b, (((1,), (0,)), ((), ())), preferred_element_type=F32, precision=precision
    )


def tn(a, b, precision=None):
    return lax.dot_general(
        a, b, (((0,), (0,)), ((), ())), preferred_element_type=F32, precision=precision
    )


def iota(shape, dim):
    return lax.broadcasted_iota(jnp.int32, shape, dim)


def spread(kind):
    return (iota((LANES, ZW), 0) == iota((LANES, ZW), 1) // HDIM + 8 * kind).astype(F32)


def gather_heads():
    return (iota((ZW, LANES), 1) == iota((ZW, LANES), 0) // HDIM).astype(F32)


def wide(packed, kind):
    return nn(packed, spread(kind), HIGHEST)


def head_sums(values):
    return nn(values, gather_heads(), HIGHEST)


def lane_mask(which):
    return (iota((1, LANES), 1) // HDIM == which).astype(BF16)


def lower_triangle():
    return (iota((BLK, BLK), 0) >= iota((BLK, BLK), 1)).astype(F32)


def call(kernel, name, grid, ins, in_specs, outs, out_specs, scratch=(), prefetch=None, flops=0, aliases=None):
    params = pltpu.CompilerParams(
        dimension_semantics=("arbitrary",) * len(grid), vmem_limit_bytes=40 << 20
    )
    nbytes = sum(math.prod(a.shape) * a.dtype.itemsize for a in ins)
    nbytes += sum(math.prod(a.shape) * a.dtype.itemsize for a in outs)
    cost = pl.CostEstimate(flops=flops, bytes_accessed=nbytes, transcendentals=0)
    spec = pltpu.PrefetchScalarGridSpec(
        num_scalar_prefetch=0 if prefetch is None else 1,
        grid=grid,
        in_specs=in_specs,
        out_specs=out_specs,
        scratch_shapes=scratch,
    )
    return pl.pallas_call(
        kernel,
        grid_spec=spec,
        out_shape=outs,
        compiler_params=params,
        cost_estimate=cost,
        input_output_aliases=aliases or {},
        name=name,
    )(*(() if prefetch is None else (prefetch,)), *ins)


def sds(shape, dtype=F32):
    return jax.ShapeDtypeStruct(shape, dtype)


def whole(shape):
    return pl.BlockSpec(shape, lambda *_: (0,) * len(shape))


def rows(width, height=BLK):
    return pl.BlockSpec((height, width), lambda i, *_: (i, 0))


def rows_back(width, height=BLK):
    return pl.BlockSpec((height, width), lambda i, *_: (GRP - 1 - i, 0))


def slot(height, width=D):
    return pl.BlockSpec((1, height, width), lambda i, at: (i ^ at[0], 0, 0))


def pick_kernel(at, *refs):
    for source, goal in zip(refs[:GRP], refs[GRP : 2 * GRP]):
        goal[...] = source[0]


def pick(at, array, after=()):
    def half_of(b):
        return pl.BlockSpec((1, HALF, D), lambda i, at: (at[0] ^ b, at[1], 0))

    def kernel(at, *refs):
        pick_kernel(at, *refs[:GRP], *refs[GRP + len(after) :])

    tokens = [pl.BlockSpec(memory_space=pl.ANY)] * len(after)
    return call(
        kernel, "pick", (1,), (array,) * GRP + tuple(after), [half_of(b) for b in range(GRP)] + tokens,
        [sds((HALF, D), BF16)] * GRP, [whole((HALF, D))] * GRP, prefetch=at,
    )


def prep_kernel(win, wout, taps, w_ref, wdt_ref, low_ref, send_ref, wide_w, sem):
    copy = pltpu.make_async_copy(win.at[:, 0, :], wide_w, sem)
    copy.start()
    low_ref[...] = wout[...].astype(BF16)
    copy.wait()
    w_ref[...] = wide_w[0:WROWS, :].astype(BF16)
    last = jnp.concatenate([wide_w[WROWS:, :], jnp.zeros((8 - NH, D), F32)], axis=0)
    wdt_ref[...] = jnp.concatenate([last] * 16, axis=0).astype(BF16)
    send_ref[0 : 2 * SW, :] = w_ref[2 * ZW : WROWS, :]
    own = taps[:, 0, :][:, ZW:]
    high = own.astype(BF16).astype(F32)
    mid = (own - high).astype(BF16).astype(F32)
    low = own - high - mid
    parts = jnp.concatenate([high, mid, low, jnp.zeros((1, 2 * SW), F32)], axis=0)
    send_ref[2 * SW :, :] = jnp.zeros((16, D), BF16)
    send_ref[2 * SW :, 0 : 2 * SW] = parts.astype(BF16)


def chunk_of(own_ref, oth_ref, core):
    own, oth = own_ref[0], oth_ref[0]
    first = core == 0
    return jnp.concatenate([jnp.where(first, own, oth), jnp.where(first, oth, own)], axis=0)


def normalise(x, gain):
    u = x.astype(F32)
    scale = lax.rsqrt(jnp.mean(u * u, axis=-1, keepdims=True) + EPSILON)
    return (u * scale * gain).astype(BF16)


def first_kernel(at, own, oth, gain, wz, wdt, hp, nrm_ref, z_ref, info_ref, row_ref, tot_ref, cum):
    step = pl.program_id(0)

    @pl.when(step == 0)
    def _():
        cum[...] = jnp.zeros_like(cum)

    normed = normalise(chunk_of(own, oth, at[1]), gain[...])
    nrm_ref[...] = normed
    z_ref[...] = nt(normed, wz[...])
    biased = nt(normed, wdt[...]) + hp[0:1, :]
    steps = jax.nn.softplus(biased)
    decays = -jnp.exp(hp[1:2, :]) * steps
    c = nn(lower_triangle(), decays, HIGHEST)
    base = cum[0:1, :]
    group = iota((BLK, LANES), 1) // 8
    info = jnp.where(group == 0, c, jnp.where(group == 1, steps, biased))
    info_ref[...] = jnp.where(group == 3, base + c, info)
    row_ref[...] = jnp.transpose(c)[0:8, :]
    cum[0:1, :] = base + c[BLK - 1 : BLK, :]
    tot_ref[...] = jnp.broadcast_to(cum[0:1, :], (8, LANES))


def mix_kernel(
    nrm, halo, gain, wx, wo, bc0, bc1, bc2, bc3, taps, info,
    mx_ref, px_ref, xa_ref, xdt_ref, mo_ref, po_ref, b_ref, c_ref, h_ref, s_ref,
    wbc, tbc, ext, exto, state,
):
    step = pl.program_id(0)
    tap = taps[:, 0, :]

    @pl.when(step == 0)
    def _():
        place = jnp.zeros((16, 2 * ST), F32)
        for b, buf in enumerate((bc0, bc1, bc2, bc3)):
            wbc[SW * b : SW * (b + 1), :] = buf[0:SW, :]
            wbc[ST + SW * b : ST + SW * (b + 1), :] = buf[SW : 2 * SW, :]
            at_row, at_col = iota((2 * SW, 2 * ST), 0), iota((2 * SW, 2 * ST), 1)
            goal = jnp.where(at_row < SW, SW * b + at_row, ST + SW * b + at_row - SW)
            put = (at_col == goal).astype(BF16)
            place = place + nn(buf[2 * SW :, 0 : 2 * SW], put)
        tbc[0:5, :] = place[0:5] + place[5:10] + place[10:15]
        before = normalise(halo[...], gain[...])
        ext[0:8, 0:ZW] = nt(before, wx[...])[8:16]
        ext[0:8, ZW:] = nt(before, wbc[...])[8:16]
        exto[0:8, :] = nt(before, wo[...])[8:16]
        state[...] = jnp.zeros_like(state)

    normed = nrm[...]
    mixed = nt(normed, wx[...])
    mx_ref[...] = mixed
    ext[8:, 0:ZW] = mixed
    ext[8:, ZW:] = nt(normed, wbc[...])
    own = nt(normed, wo[...])
    mo_ref[...] = own
    exto[8:, :] = own
    pre = tap[4:5, 0:ZW]
    pre_bc = tbc[4:5, :]
    pre_o = tap[4:5, ZW:]
    for k in range(CONV):
        pre = pre + tap[k : k + 1, 0:ZW] * ext[5 + k : 5 + k + BLK, 0:ZW]
        pre_bc = pre_bc + tbc[k : k + 1, :] * ext[5 + k : 5 + k + BLK, ZW:]
        pre_o = pre_o + tap[k : k + 1, ZW:] * exto[5 + k : 5 + k + BLK, :]
    px_ref[...] = pre
    po_ref[...] = pre_o
    x = pre * jax.nn.sigmoid(pre)
    xa_ref[...] = x
    bc = (pre_bc * jax.nn.sigmoid(pre_bc)).astype(BF16)
    b_ref[...] = bc[:, 0:ST]
    c_ref[...] = bc[:, ST:]
    ext[0:8, :] = ext[BLK:, :]
    exto[0:8, :] = exto[BLK:, :]

    packed = info[...]
    c = packed[:, 0:LANES]
    keep = iota((BLK, LANES), 1) < 8
    tail = jnp.where(keep, jnp.exp(jnp.where(keep, c[BLK - 1 : BLK, :] - c, 0.0)), 0.0)
    xdt = x * wide(packed, 1)
    xdt_ref[...] = xdt.astype(BF16)
    fresh = tn((xdt * wide(tail, 0)).astype(BF16), bc[:, 0:ST])
    h_ref[0] = state[...]
    for h in range(NH):
        decay = jnp.exp(packed[BLK - 1 : BLK, h : h + 1])
        at = pl.ds(HDIM * h, HDIM)
        state[at, :] = decay * state[at, :] + fresh[HDIM * h : HDIM * (h + 1), :]
    s_ref[...] = state[...].astype(BF16)


def weights_of(h, packed, row, causal):
    diff = packed[:, h : h + 1] - row[h : h + 1, :]
    return jnp.where(causal, jnp.exp(jnp.where(causal, diff, 0.0)), 0.0)


def local_kernel(
    at, xdt, xa, b, c, info, row, hloc, own, oth, low, skip, yl_ref, dyn_ref, w_ref
):
    step = pl.program_id(0)
    packed = info[...]
    rowc = row[...]
    causal = iota((BLK, BLK), 0) >= iota((BLK, BLK), 1)
    scores = nt(c[...], b[...])
    c_exp = jnp.exp(jnp.where(iota((BLK, LANES), 1) < 8, packed, 0.0))
    carried = nt(c[...], hloc[0].astype(BF16)) * wide(c_exp, 0)
    carried = carried + skip[0:1, :] * xa[...]
    for p in range(NH // 2):
        x = xdt[:, LANES * p : LANES * (p + 1)]
        total = carried[:, LANES * p : LANES * (p + 1)]
        for q in range(2):
            weights = (weights_of(2 * p + q, packed, rowc, causal) * scores).astype(BF16)
            total = total + nn(weights, x * lane_mask(q))
        yl_ref[:, LANES * p : LANES * (p + 1)] = total
    place = (at[2] * GRP + step) * BLK + iota((BLK, 1), 0)
    live = place < at[3]
    w = jnp.where(live, chunk_of(own, oth, at[1]), 0.0).astype(BF16)
    w_ref[...] = w
    dyn_ref[...] = nt(w, low[...])


def gate_kernel(yl, c, info, hin, z, dyn, gg, y_ref, sum_ref):
    packed = info[...]
    lane = iota((BLK, LANES), 1)
    cum = jnp.where(lane // 8 == 3, jnp.exp(jnp.where(lane // 8 == 3, packed, 0.0)), 0.0)
    y = yl[...] + nt(c[...], hin[...]) * wide(cum, 3)
    y_ref[...] = y
    gate = z[...]
    g = y * (gate * jax.nn.sigmoid(gate))
    squares = jnp.sum(g * g, axis=-1, keepdims=True)
    inner = jnp.sum(dyn[...] * gg[...] * g, axis=-1, keepdims=True)
    both = jnp.where(lane == 0, squares, jnp.where(lane == 1, inner, 0.0))
    sum_ref[...] = jnp.transpose(both)[0:8, :]


def ungate_kernel(
    y, z, dyn, s0, s1, s2, s3, info, c, gg, dy_ref, dz_ref, yn_ref, p_ref, gg_ref, acc
):
    step = pl.program_id(0)

    @pl.when(step == 0)
    def _():
        acc[...] = jnp.zeros_like(acc)
        gg_ref[...] = jnp.zeros_like(gg_ref)

    sums = s0[...] + s1[...] + s2[...] + s3[...]
    sums = jnp.transpose(jnp.concatenate([sums, jnp.zeros((LANES - 8, BLK), F32)], axis=0))
    q = lax.rsqrt(sums[:, 0:1] / INNER + EPSILON)
    mean = sums[:, 1:2] * q / INNER
    gate = z[...]
    sigma = jax.nn.sigmoid(gate)
    silu = gate * sigma
    out = y[...]
    g = out * silu
    n = g * q
    d = dyn[...]
    d_g = q * (d * gg[...] - n * mean)
    d_y = d_g * silu
    dy_ref[...] = d_y
    dz_ref[...] = (d_g * out * sigma * (1.0 + gate * (1.0 - sigma))).astype(BF16)
    yn_ref[...] = (n * gg[...]).astype(BF16)
    gg_ref[0:1, :] += jnp.sum(d * n, axis=0, keepdims=True)
    packed = info[...]
    lane = iota((BLK, LANES), 1)
    cum = jnp.where(lane // 8 == 3, jnp.exp(jnp.where(lane // 8 == 3, packed, 0.0)), 0.0)
    acc[...] += tn((d_y * wide(cum, 3)).astype(BF16), c[...])
    p_ref[...] = acc[...].astype(BF16)


def halves(value, core, keep_ref, send_ref):
    low, high = value[0:HALF], value[HALF:]
    first = core == 0
    keep_ref[0] = jnp.where(first, low, high)
    send_ref[0] = jnp.where(first, high, low)


def out_kernel(
    at, yn, w, low, nrm, dz, keep_ref, send_ref, g0, g1, g2, g3, acc
):
    step = pl.program_id(0)

    @pl.when(step == 0)
    def _():
        acc[...] = jnp.zeros_like(acc)

    halves(nn(yn[...], low[...]).astype(BF16), at[1], keep_ref, send_ref)
    acc[0:ZW, :] += tn(dz[...], nrm[...])
    acc[ZW:, :] += tn(yn[...], w[...])

    @pl.when(step == GRP - 1)
    def _():
        for b, ref in enumerate((g0, g1, g2, g3)):
            start = pl.multiple_of((at[0] ^ b) * SEG1, SEG1)
            ref[...] = acc[pl.ds(start, SEG1), :].astype(BF16)


def inner_kernel(
    xdt, b, c, info, row, dy, hloc, hin, token, dxi_ref, dbi_ref, dci_ref, dcum_ref, hall_ref
):
    packed = info[...]
    rowc = row[...]
    lane = iota((BLK, LANES), 1)
    causal = iota((BLK, BLK), 0) >= iota((BLK, BLK), 1)
    bb, cc = b[...], c[...]
    scores = nt(cc, bb)
    d_scores = jnp.zeros((BLK, BLK), F32)
    d_cum = jnp.zeros((BLK, LANES), F32)
    columns = []
    dyv = dy[...]
    for p in range(NH // 2):
        x = xdt[:, LANES * p : LANES * (p + 1)]
        d = dyv[:, LANES * p : LANES * (p + 1)].astype(BF16)
        total = jnp.zeros((BLK, LANES), F32)
        for q in range(2):
            h = 2 * p + q
            spans = weights_of(h, packed, rowc, causal)
            d_h = d * lane_mask(q)
            d_spans = nt(d_h, x) * spans
            d_scores = d_scores + d_spans
            both = d_spans * scores
            d_cum = d_cum + jnp.where(lane == h, jnp.sum(both, axis=1, keepdims=True), 0.0)
            columns.append(jnp.sum(both, axis=0, keepdims=True))
            total = total + tn((spans * scores).astype(BF16), d_h)
        dxi_ref[:, LANES * p : LANES * (p + 1)] = total
    columns = jnp.concatenate(columns + [jnp.zeros((LANES - NH, BLK), F32)], axis=0)
    d_cum = d_cum - jnp.transpose(columns)
    low_scores = d_scores.astype(BF16)
    c_exp = jnp.exp(jnp.where(lane < 8, packed, 0.0))
    c_wide = wide(c_exp, 0)
    base = packed[0:1, 24:32] - packed[0:1, 0:8]
    for h in range(NH):
        at = pl.ds(HDIM * h, HDIM)
        grown = jnp.exp(base[:, h : h + 1]) * hin[at, :].astype(F32)
        hall_ref[0, at, :] = hloc[0, at, :] + grown
    entering = hall_ref[0].astype(BF16)
    carried = nt(cc, entering) * c_wide
    d_cum = d_cum + head_sums(dyv * carried)
    dcum_ref[...] = d_cum
    dci_ref[...] = nn(low_scores, bb) + nn((dyv * c_wide).astype(BF16), entering)
    dbi_ref[...] = tn(low_scores, cc)


def back_kernel(
    after, dxi, dbi, dci, dcum, hall, xa, px, b, c, info, dy, hp, skip,
    dpx_ref, o0, o1, o2, o3, draw_ref, hg_ref, state,
):
    step = pl.program_id(0)

    @pl.when(step == 0)
    def _():
        state[...] = after[...].astype(F32)
        hg_ref[...] = jnp.zeros_like(hg_ref)

    packed = info[...]
    lane = iota((BLK, LANES), 1)
    first = lane < 8
    c_last = packed[BLK - 1 : BLK, :]
    tail = jnp.where(first, jnp.exp(jnp.where(first, c_last - packed, 0.0)), 0.0)
    c_exp = jnp.exp(jnp.where(first, packed, 0.0))
    tail_wide, c_wide, dt_wide = wide(tail, 0), wide(c_exp, 0), wide(packed, 1)
    x = xa[...]
    xdt = x * dt_wide
    d_y = dy[...]
    bb, cc = b[...], c[...]
    low_state = state[...].astype(BF16)
    d_tail = nt(bb, low_state) * tail_wide
    tails = head_sums(xdt * d_tail)
    d_xdt = dxi[...] + d_tail
    d_b = dbi[...] + nn((xdt * tail_wide).astype(BF16), low_state)
    d_c = dci[...]
    ending = jnp.sum(tails, axis=0, keepdims=True)
    lane1 = iota((1, LANES), 1)
    for h in range(NH):
        at = pl.ds(HDIM * h, HDIM)
        inner = jnp.sum(state[at, :] * hall[0, at, :], axis=(0, 1), keepdims=True)
        ending = ending + jnp.where(lane1 == h, inner * jnp.exp(c_last[:, h : h + 1]), 0.0)
    d_cum = dcum[...] - tails
    d_cum = d_cum + jnp.where(iota((BLK, LANES), 0) == BLK - 1, ending, 0.0)
    d_a = tn(lower_triangle(), d_cum, HIGHEST)
    fresh = tn((d_y * c_wide).astype(BF16), cc)
    for h in range(NH):
        at = pl.ds(HDIM * h, HDIM)
        decay = jnp.exp(c_last[:, h : h + 1])
        state[at, :] = decay * state[at, :] + fresh[HDIM * h : HDIM * (h + 1), :]
    rate = -jnp.exp(hp[1:2, :])
    d_dt = head_sums(x * d_xdt) + rate * d_a
    biased = pltpu.roll(packed, LANES - 16, 1)
    steps = pltpu.roll(packed, LANES - 8, 1)
    used = lane < NH
    d_raw = jnp.where(used, d_dt * jax.nn.sigmoid(jnp.where(used, biased, 0.0)), 0.0)
    draw_ref[...] = d_raw.astype(BF16)
    hg_ref[0:1, :] += jnp.sum(d_raw, axis=0, keepdims=True)
    g_rate = jnp.where(used, d_a * rate * jnp.where(used, steps, 0.0), 0.0)
    hg_ref[1:2, :] += jnp.sum(g_rate, axis=0, keepdims=True)
    hg_ref[2:3, :] += jnp.sum(head_sums(d_y * x), axis=0, keepdims=True)
    d_x = d_xdt * dt_wide + skip[0:1, :] * d_y
    pre = px[...]
    sigma = jax.nn.sigmoid(pre)
    dpx_ref[...] = d_x * sigma * (1.0 + pre * (1.0 - sigma))
    for s, ref in enumerate((o0, o1, o2, o3)):
        ref[:, 0:SW] = d_b[:, SW * s : SW * (s + 1)].astype(BF16)
        ref[:, SW:] = d_c[:, SW * s : SW * (s + 1)].astype(BF16)


def edge_kernel(o0, r1, r2, r3, po, dpx, dpo_ref, halo_ref):
    d = o0[...].astype(F32) + r1[...].astype(F32) + r2[...].astype(F32) + r3[...].astype(F32)
    pre = po[...]
    sigma = jax.nn.sigmoid(pre)
    d = d * sigma * (1.0 + pre * (1.0 - sigma))
    dpo_ref[...] = d

    @pl.when(pl.program_id(0) == 0)
    def _():
        halo_ref[:, 0:ZW] = dpx[0:8, :]
        halo_ref[:, ZW:] = jnp.zeros((8, LANES), F32)
        halo_ref[:, ZW : ZW + 2 * SW] = d[0:8, :]


def last_kernel(
    at, dpx, dpo, halo, mx, mo, taps, dz, draw, nrm, w, wdt, gain, gg, hg,
    keep_ref, send_ref, g0, g1, g2, g3,
    ext, exto, acc, acc_t, acc_n, tap_x, tap_o,
):
    step = pl.program_id(0)
    tap = taps[:, 0, :]

    @pl.when(step == 0)
    def _():
        ext[BLK:, :] = halo[:, 0:ZW]
        exto[BLK:, :] = halo[:, ZW : ZW + 2 * SW]
        for ref in (acc, acc_t, acc_n, tap_x, tap_o):
            ref[...] = jnp.zeros_like(ref)

    d_x, d_o = dpx[...], dpo[...]
    ext[0:BLK, :] = d_x
    exto[0:BLK, :] = d_o
    d_mx = jnp.zeros((BLK, ZW), F32)
    d_mo = jnp.zeros((BLK, 2 * SW), F32)
    for k in range(CONV):
        d_mx = d_mx + tap[k : k + 1, 0:ZW] * ext[3 - k : 3 - k + BLK, :]
        d_mo = d_mo + tap[k : k + 1, ZW:] * exto[3 - k : 3 - k + BLK, :]
    v_x, v_o = mx[...], mo[...]
    for k in range(CONV):
        tap_x[k : k + 1, :] += jnp.sum(v_x * ext[3 - k : 3 - k + BLK, :], axis=0, keepdims=True)
        tap_o[k : k + 1, :] += jnp.sum(v_o * exto[3 - k : 3 - k + BLK, :], axis=0, keepdims=True)
    tap_x[4:5, :] += jnp.sum(d_x, axis=0, keepdims=True)
    tap_o[4:5, :] += jnp.sum(d_o, axis=0, keepdims=True)
    ext[BLK:, :] = d_x[0:8]
    exto[BLK:, :] = d_o[0:8]
    p_x, p_o = d_mx.astype(BF16), d_mo.astype(BF16)
    p_z, p_t = dz[...], draw[...]
    back = nn(p_z, w[0:ZW, :]) + nn(p_x, w[ZW : 2 * ZW, :])
    back = back + nn(p_o, w[2 * ZW : WROWS, :]) + nn(p_t, wdt[...])
    halves(back.astype(BF16), at[1], keep_ref, send_ref)
    normed = nrm[...]
    acc_n[0:1, :] += jnp.sum(back * normed.astype(F32), axis=0, keepdims=True)
    acc[0:ZW, :] += tn(p_x, normed)
    acc[BC_AT:DT_AT, :] += tn(p_o, normed)
    acc_t[...] += tn(p_t, normed)

    @pl.when(step == GRP - 1)
    def _():
        acc[DT_AT:, :] = jnp.zeros((GRP * SEG2 - DT_AT, D), F32)
        acc[DT_AT : DT_AT + NH, :] = acc_t[0:NH, :]
        acc[TAP_AT : TAP_AT + 5, 0:ZW] = tap_x[0:5, :]
        acc[TAP_AT : TAP_AT + 5, ZW : ZW + 2 * SW] = tap_o[0:5, :]
        acc[HD_AT : HD_AT + 8, 0:LANES] = hg[...]
        acc[GG_AT : GG_AT + 1, 0:ZW] = gg[0:1, :]
        acc[NG_AT : NG_AT + 1, :] = acc_n[0:1, :] / gain[...]
        for b, ref in enumerate((g0, g1, g2, g3)):
            start = pl.multiple_of((at[0] ^ b) * SEG2, 8)
            ref[...] = acc[pl.ds(start, SEG2), :].astype(BF16)


def split_kernel(at, keep, other, keep_ref, send_ref):
    value = keep[0].astype(F32) + other[0].astype(F32)
    low, high = value[0:QUART], value[QUART:]
    first = at[4] == 0
    keep_ref[0] = jnp.where(first, low, high)
    send_ref[0] = jnp.where(first, high, low).astype(BF16)


def add_kernel(keep, other, r0, r1, r2, r3):
    for b, ref in enumerate((r0, r1, r2, r3)):
        ref[...] = (keep[b] + other[b].astype(F32)).astype(BF16)


def sum_kernel(*refs):
    total = refs[0][...].astype(F32)
    for ref in refs[1:-1]:
        total = total + ref[...].astype(F32)
    refs[-1][...] = total.astype(refs[-1].dtype)


def place_quarters(at, b, parts, scr):
    core, xbit = at[1], at[4]
    for n, ref in enumerate(parts):
        half = core if n < 2 else 1 - core
        quarter = xbit if n % 2 == 0 else 1 - xbit
        start = pl.multiple_of(half * HALF + quarter * QUART, QUART)
        scr[pl.ds(start, QUART), :] = ref[0]


def home_out_kernel(at, lens, block, a, x, ac, xc, out_ref, scr):
    step = pl.program_id(0)
    place_quarters(at, step, (a, x, ac, xc), scr)
    place = (at[2] * GRP + at[0]) * BLK + iota((BLK, 1), 0)
    live = place < lens[step]
    total = block[0].astype(F32) + scr[...].astype(F32)
    out_ref[0] = jnp.where(live, total, 0.0).astype(BF16)


def home_grad_kernel(at, lens, block, cot, gain, a, x, ac, xc, out_ref, scr):
    step = pl.program_id(0)
    place_quarters(at, step, (a, x, ac, xc), scr)
    place = (at[2] * GRP + at[0]) * BLK + iota((BLK, 1), 0)
    live = place < lens[step]
    u = block[0].astype(F32)
    scale = lax.rsqrt(jnp.mean(u * u, axis=-1, keepdims=True) + EPSILON)
    m = u * scale
    f = scr[...].astype(F32) * gain[...]
    inner = jnp.mean(f * m, axis=-1, keepdims=True)
    out_ref[0] = scale * (f - m * inner) + jnp.where(live, cot[0].astype(F32), 0.0)


def home(kernel, name, at, lens, arrays, specs, parts, dtype):
    full = pl.BlockSpec((1, BLK, D), lambda i, *_: (i, 0, 0))
    part = pl.BlockSpec((1, QUART, D), lambda i, at, lens: (i ^ at[0], 0, 0))
    specs = [full if s is None else whole(s) for s in specs]
    spec = pltpu.PrefetchScalarGridSpec(
        num_scalar_prefetch=2,
        grid=(GRP,),
        in_specs=specs + [part] * 4,
        out_specs=full,
        scratch_shapes=[pltpu.VMEM((BLK, D), BF16)],
    )
    return pl.pallas_call(
        kernel,
        grid_spec=spec,
        out_shape=sds((GRP, BLK, D), dtype),
        cost_estimate=pl.CostEstimate(flops=0, bytes_accessed=8 << 20, transcendentals=0),
        name=name,
    )(at, lens, *arrays, *parts)


def advance(weight, gradient, moment, average, rate):
    moment_new = MOMENTUM * moment + gradient
    weight_new = weight - rate * (gradient + MOMENTUM * moment_new)
    average_new = AVERAGE * average + (1.0 - AVERAGE) * weight_new
    return (weight_new, moment_new, average_new)


def stepped(grad_of, weights, outs, blocks, buffers, sems, rate):
    ins, done = buffers[:3], buffers[3:]

    def reads(n):
        start, size = blocks[n]
        return [
            pltpu.make_async_copy(
                w.at[pl.ds(start, size), 0, :], buf.at[pl.ds(start, size), :], sems.at[n, j]
            )
            for j, (w, buf) in enumerate(zip(weights, ins))
        ]

    def writes(n):
        start, size = blocks[n]
        return [
            pltpu.make_async_copy(
                buf.at[pl.ds(start, size), :], o.at[pl.ds(start, size), 0, :], sems.at[n, 3 + j]
            )
            for j, (o, buf) in enumerate(zip(outs, done))
        ]

    for n in range(len(blocks)):
        for copy in reads(n):
            copy.start()
    for n, (start, size) in enumerate(blocks):
        for copy in reads(n):
            copy.wait()
        here = pl.ds(start, size)
        new = advance(ins[0][here, :], grad_of(n), ins[1][here, :], ins[2][here, :], rate)
        for buf, value in zip(done, new):
            buf[here, :] = value
        for copy in writes(n):
            copy.start()
    for n in range(len(blocks)):
        for copy in writes(n):
            copy.wait()


Z_BLOCKS = tuple((96 * n, 96) for n in range(4))
X_BLOCKS = tuple((ZW + 96 * n, 96) for n in range(4)) + ((2 * ZW, COLS - 2 * ZW),)


def update_a_kernel(
    at, g0, g1, g2, g3, w, m, a, wi, mi, ai, w_ref, m_ref, a_ref, wo, mo, ao,
    grad, b0, b1, b2, b3, b4, b5, sems, *, rate, rate_in,
):
    for b, ref in enumerate((g0, g1, g2, g3)):
        grad[pl.ds(pl.multiple_of((at[0] ^ b) * SEG1, SEG1), SEG1), :] = ref[...].astype(F32)
    stepped(
        lambda n: grad[96 * n : 96 * (n + 1), :], (wi, mi, ai), (wo, mo, ao), Z_BLOCKS,
        (b0, b1, b2, b3, b4, b5), sems, rate_in,
    )
    w_ref[...], m_ref[...], a_ref[...] = advance(w[...], grad[ZW:, :], m[...], a[...], rate)


def update_b_kernel(
    at, g0, g1, g2, g3, wi, mi, ai, x0, x1, x2, wo, mo, ao, small_ref,
    grad, b0, b1, b2, b3, b4, b5, sems, *, rate,
):
    for b, ref in enumerate((g0, g1, g2, g3)):
        start = pl.multiple_of((at[0] ^ b) * SEG2, 8)
        grad[pl.ds(start, SEG2), :] = ref[...].astype(F32)
    stepped(
        lambda n: grad[96 * n : min(96 * (n + 1), COLS - ZW), :], (wi, mi, ai), (wo, mo, ao), X_BLOCKS,
        (b0, b1, b2, b3, b4, b5), sems, rate,
    )
    small_ref[...] = grad[TAP_AT : TAP_AT + 24, :]


def trade(axis, flip):
    count = lax.axis_size(axis)
    pairs = [(i, i ^ flip) for i in range(count)]
    return lambda array: lax.ppermute(array, axis, pairs)


def moved(array, by):
    count = lax.axis_size("seq")
    pairs = [(i, i + by) for i in range(count) if 0 <= i + by < count]
    return lax.ppermute(array, "seq", pairs)


def grow(decay, state):
    return jnp.repeat(decay[0, 0:NH], HDIM)[:, None] * state


def pieces_before(state, logs, way):
    count = lax.axis_size("seq") // GRP
    found = moved(state, way * GRP)
    by = 1
    if count > 2:
        there = lax.axis_index("seq") // GRP
        decay = moved(jnp.exp(logs), way * GRP)
        total = found.astype(F32)
        while by < count - 1:
            inside = (there >= by) if way > 0 else (there + by < count)
            earlier = moved(total.astype(BF16), way * GRP * by).astype(F32)
            total = jnp.where(inside, grow(decay, earlier) + total, total)
            decay = decay * moved(decay, way * GRP * by)
            by *= 2
        found = total.astype(BF16)
    return found


def summed_over_seq(parts, height):
    got = [trade("seq", b)(parts[b]) for b in (1, 2, 3)]
    spec = whole((height, D))

    def add(*arrays):
        specs = [spec] * len(arrays)
        out = [sds((height, D), BF16)]
        return call(sum_kernel, "sum", (1,), arrays, specs, out, [spec])[0]

    mine = add(parts[0], *got)
    by = GRP
    while by < lax.axis_size("seq"):
        mine = add(mine, trade("seq", by)(mine))
        by *= 2
    return [mine] + [trade("seq", b)(mine) for b in (1, 2, 3)]


def returned(at, keep, send):
    slot3 = lambda height: pl.BlockSpec((1, height, D), lambda i, at: (i, 0, 0))
    other = trade("head", 1)(send)
    keep2, send2 = call(
        split_kernel, "split", (GRP,), (keep, other), [slot3(HALF)] * 2,
        [sds((GRP, QUART, D)), sds((GRP, QUART, D), BF16)], [slot3(QUART)] * 2, prefetch=at,
    )
    other2 = trade("head", 2)(send2)
    every = whole((GRP, QUART, D))
    parts = call(
        add_kernel, "add", (1,), (keep2, other2), [every] * 2,
        [sds((QUART, D), BF16)] * 4, [whole((QUART, D))] * 4,
    )
    got = [parts[0]] + [trade("seq", b)(parts[b]) for b in (1, 2, 3)]
    a = jnp.stack(got)
    x = trade("head", 2)(a)
    return a, x, trade("head", 1)(a), trade("head", 1)(x)


def shards(
    block_in, cotangent, lengths,
    norm_gain, in_proj, conv_params, head_params, gate_gain, out_proj,
    norm_gain_momentum, in_proj_momentum, conv_momentum, head_momentum, gate_gain_momentum,
    out_proj_momentum,
    norm_gain_average, in_proj_average, conv_average, head_average, gate_gain_average,
    out_proj_average,
):
    seq_at, head_at = lax.axis_index("seq"), lax.axis_index("head")
    place = seq_at % GRP
    at = jnp.stack([place, head_at % 2, seq_at // GRP, lengths[place], head_at // 2])
    at = at.astype(jnp.int32)
    gain = norm_gain.reshape(1, D)
    ggain = gate_gain.reshape(1, ZW)
    hp = jnp.tile(jnp.pad(head_params, ((0, 5), (0, 2))), (1, 16))
    skip = jnp.repeat(head_params[2], HDIM).reshape(1, ZW)

    def turned(array):
        return jnp.transpose(array, (2, 1, 0))

    anyspec = pl.BlockSpec(memory_space=pl.ANY)
    picked = pick(at, block_in)
    got = [picked[0]] + [trade("seq", b)(picked[b]) for b in (1, 2, 3)]
    w, wdt, low, send_bc = call(
        prep_kernel, "prep", (1,), (turned(in_proj), out_proj, conv_params),
        [anyspec, whole((ZW, D)), whole((5, 1, 448))],
        [sds((WROWS, D), BF16), sds((LANES, D), BF16), sds((ZW, D), BF16), sds((80, D), BF16)],
        [whole((WROWS, D)), whole((LANES, D)), whole((ZW, D)), whole((80, D))],
        scratch=[pltpu.VMEM((COLS, D), F32), pltpu.SemaphoreType.DMA],
    )
    bcs = [send_bc] + [trade("head", b)(send_bc) for b in (1, 2, 3)]
    own = jnp.stack(got)
    oth = trade("head", 1)(own)
    high = jnp.where(head_at % 2 == 1, own[:, HALF - 16 :], oth[:, HALF - 16 :])
    edge = lax.dynamic_index_in_dim(high, place ^ (GRP - 1), 0, False)
    halo = moved(edge, GRP)
    cot_picked = pick(at, cotangent, (own,))
    cot_got = [cot_picked[0]] + [trade("seq", b)(cot_picked[b]) for b in (1, 2, 3)]
    cot_own = jnp.stack(cot_got)
    cot_oth = trade("head", 1)(cot_own)

    def wblock(n, height):
        return pl.BlockSpec((height, D), lambda i, *_: (n, 0))

    nrm, z, info, rowc, logs = call(
        first_kernel, "first", (GRP,), (own, oth, gain, w, wdt, hp),
        [slot(HALF), slot(HALF), whole((1, D)), wblock(0, ZW), whole((LANES, D)), whole((8, LANES))],
        [sds((TOK, D), BF16), sds((TOK, ZW)), sds((TOK, LANES)), sds((8, TOK)), sds((8, LANES))],
        [rows(D), rows(ZW), rows(LANES), pl.BlockSpec((8, BLK), lambda i, *_: (0, i)), whole((8, LANES))],
        scratch=[pltpu.VMEM((8, LANES), F32)], prefetch=at, flops=2 * TOK * D * 512,
    )
    hspec = pl.BlockSpec((1, ZW, ST), lambda i, *_: (i, 0, 0))
    rowspec = pl.BlockSpec((8, BLK), lambda i, *_: (0, i))
    mx, px, xa, xdt, mo, po, bb, cc, hloc, fresh = call(
        mix_kernel, "mix", (GRP,), (nrm, halo, gain, w, w, *bcs, conv_params, info),
        [rows(D), whole((16, D)), whole((1, D)), wblock(1, ZW), wblock(12, 2 * SW)]
        + [whole((80, D))] * 4 + [whole((5, 1, 448)), rows(LANES)],
        [sds((TOK, ZW)), sds((TOK, ZW)), sds((TOK, ZW)), sds((TOK, ZW), BF16), sds((TOK, 2 * SW)),
         sds((TOK, 2 * SW)), sds((TOK, ST), BF16), sds((TOK, ST), BF16), sds((GRP, ZW, ST)),
         sds((ZW, ST), BF16)],
        [rows(ZW), rows(ZW), rows(ZW), rows(ZW), rows(2 * SW), rows(2 * SW), rows(ST), rows(ST),
         hspec, whole((ZW, ST))],
        scratch=[pltpu.VMEM((2 * ST, D), BF16), pltpu.VMEM((8, 2 * ST), F32),
                 pltpu.VMEM((BLK + 8, ZW + 2 * ST), F32), pltpu.VMEM((BLK + 8, 2 * SW), F32),
                 pltpu.VMEM((ZW, ST), F32)],
        flops=2 * TOK * D * 704,
    )
    hin = pieces_before(fresh, logs, 1)
    yl, dyn, w_live = call(
        local_kernel, "local", (GRP,),
        (xdt, xa, bb, cc, info, rowc, hloc, cot_own, cot_oth, low, skip),
        [rows(ZW), rows(ZW), rows(ST), rows(ST), rows(LANES), rowspec, hspec, slot(HALF),
         slot(HALF), whole((ZW, D)), whole((1, ZW))],
        [sds((TOK, ZW)), sds((TOK, ZW)), sds((TOK, D), BF16)], [rows(ZW), rows(ZW), rows(D)],
        prefetch=at, flops=2 * TOK * (D * ZW + 4 * BLK * ZW),
    )
    y, sums = call(
        gate_kernel, "gate", (GRP,), (yl, cc, info, hin, z, dyn, ggain),
        [rows(ZW), rows(ST), rows(LANES), whole((ZW, ST)), rows(ZW), rows(ZW), whole((1, ZW))],
        [sds((TOK, ZW)), sds((8, TOK))], [rows(ZW), rowspec], flops=2 * TOK * ST * ZW,
    )
    all_sums = [sums] + [trade("head", b)(sums) for b in (1, 2, 3)]
    dy, dz, yn, pulled, g_gate = call(
        ungate_kernel, "ungate", (GRP,), (y, z, dyn, *all_sums, info, cc, ggain),
        [rows(ZW)] * 3 + [rowspec] * 4 + [rows(LANES), rows(ST), whole((1, ZW))],
        [sds((TOK, ZW)), sds((TOK, ZW), BF16), sds((TOK, ZW), BF16), sds((ZW, ST), BF16), sds((8, ZW))],
        [rows(ZW), rows(ZW), rows(ZW), whole((ZW, ST)), whole((8, ZW))],
        scratch=[pltpu.VMEM((ZW, ST), F32)], flops=2 * TOK * ST * ZW,
    )
    after = pieces_before(pulled, logs, -1)
    half_slot = pl.BlockSpec((1, HALF, D), lambda i, at: (i ^ at[0], 0, 0))
    keep, send, *grads1 = call(
        out_kernel, "out", (GRP,), (yn, w_live, low, nrm, dz),
        [rows(ZW), rows(D), whole((ZW, D)), rows(D), rows(ZW)],
        [sds((GRP, HALF, D), BF16)] * 2 + [sds((SEG1, D), BF16)] * 4,
        [half_slot] * 2 + [whole((SEG1, D))] * 4,
        scratch=[pltpu.VMEM((2 * ZW, D), F32)],
        prefetch=at, flops=6 * TOK * D * ZW,
    )
    dxi, dbi, dci, dcum, hall = call(
        inner_kernel, "inner", (GRP,), (xdt, bb, cc, info, rowc, dy, hloc, hin, grads1[0]),
        [rows(ZW), rows(ST), rows(ST), rows(LANES), rowspec, rows(ZW), hspec, whole((ZW, ST)), anyspec],
        [sds((TOK, ZW)), sds((TOK, ST)), sds((TOK, ST)), sds((TOK, LANES)), sds((GRP, ZW, ST))],
        [rows(ZW), rows(ST), rows(ST), rows(LANES), hspec], flops=2 * TOK * 8 * BLK * ZW,
    )
    hback = pl.BlockSpec((1, ZW, ST), lambda i, *_: (GRP - 1 - i, 0, 0))
    dpx, *dbc, draw, g_head = call(
        back_kernel, "back", (GRP,),
        (after, dxi, dbi, dci, dcum, hall, xa, px, bb, cc, info, dy, hp, skip),
        [whole((ZW, ST)), rows_back(ZW), rows_back(ST), rows_back(ST), rows_back(LANES), hback,
         rows_back(ZW), rows_back(ZW), rows_back(ST), rows_back(ST), rows_back(LANES),
         rows_back(ZW), whole((8, LANES)), whole((1, ZW))],
        [sds((TOK, ZW))] + [sds((TOK, 2 * SW), BF16)] * 4 + [sds((TOK, LANES), BF16), sds((8, LANES))],
        [rows_back(ZW)] + [rows_back(2 * SW)] * 4 + [rows_back(LANES), whole((8, LANES))],
        scratch=[pltpu.VMEM((ZW, ST), F32)], flops=2 * TOK * 4 * ST * ZW,
    )
    bc_got = [trade("head", b)(dbc[b]) for b in (1, 2, 3)]
    dpo, edge_back = call(
        edge_kernel, "edge", (GRP,), (dbc[0], *bc_got, po, dpx),
        [rows(2 * SW)] * 5 + [pl.BlockSpec((8, ZW), lambda i: (0, 0))],
        [sds((TOK, 2 * SW)), sds((8, ZW + LANES))], [rows(2 * SW), whole((8, ZW + LANES))],
    )
    halo_back = moved(edge_back, -GRP)
    keep_b, send_b, *grads2 = call(
        last_kernel, "last", (GRP,),
        (dpx, dpo, halo_back, mx, mo, conv_params, dz, draw, nrm, w, wdt, gain, g_gate, g_head),
        [rows_back(ZW), rows_back(2 * SW), whole((8, ZW + LANES)), rows_back(ZW), rows_back(2 * SW),
         whole((5, 1, 448)), rows_back(ZW),
         rows_back(LANES), rows_back(D), whole((WROWS, D)), whole((LANES, D)), whole((1, D)),
         whole((8, ZW)), whole((8, LANES))],
        [sds((GRP, HALF, D), BF16)] * 2 + [sds((SEG2, D), BF16)] * 4,
        [pl.BlockSpec((1, HALF, D), lambda i, at: ((GRP - 1 - i) ^ at[0], 0, 0))] * 2
        + [whole((SEG2, D))] * 4,
        scratch=[pltpu.VMEM((BLK + 8, ZW), F32), pltpu.VMEM((BLK + 8, 2 * SW), F32),
                 pltpu.VMEM((GRP * SEG2, D), F32), pltpu.VMEM((LANES, D), F32),
                 pltpu.VMEM((8, D), F32), pltpu.VMEM((8, ZW), F32), pltpu.VMEM((8, 2 * SW), F32)],
        prefetch=at, flops=4 * TOK * D * 960,
    )

    out_parts = returned(at, keep, send)
    block_out = home(home_out_kernel, "home_out", at, lengths, (block_in,), (None,), out_parts, BF16)
    grad_parts = returned(at, keep_b, send_b)
    input_grad = home(
        home_grad_kernel, "home_grad", at, lengths, (block_in, cotangent, gain),
        (None, None, (1, D)), grad_parts, F32,
    )

    root = math.sqrt(TOK * lax.axis_size("seq"))
    sums1 = summed_over_seq(grads1, SEG1)
    mat = whole((ZW, D))
    turned3 = [turned(p) for p in (in_proj, in_proj_momentum, in_proj_average)]
    turned_shape = [sds((COLS, 1, D))] * 3
    buffers = [pltpu.VMEM((COLS, D), F32)] * 6 + [pltpu.SemaphoreType.DMA((5, 6))]
    out_w, out_m, out_a, *in_half = call(
        functools.partial(update_a_kernel, rate=RATES[5] / root, rate_in=RATES[1] / root), "update_a", (1,),
        (*sums1, out_proj, out_proj_momentum, out_proj_average, *turned3),
        [whole((SEG1, D))] * 4 + [mat] * 3 + [anyspec] * 3, [sds((ZW, D))] * 3 + turned_shape,
        [mat] * 3 + [anyspec] * 3, scratch=[pltpu.VMEM((2 * ZW, D), F32)] + buffers, prefetch=at,
    )
    sums2 = summed_over_seq(grads2, SEG2)
    *in_new, small = call(
        functools.partial(update_b_kernel, rate=RATES[1] / root), "update_b", (1,),
        (*sums2, *turned3, *in_half), [whole((SEG2, D))] * 4 + [anyspec] * 6,
        turned_shape + [sds((24, D))], [anyspec] * 3 + [whole((24, D))],
        scratch=[pltpu.VMEM((GRP * SEG2, D), F32)] + buffers, prefetch=at, aliases={8: 0, 9: 1, 10: 2},
    )
    hd, gg, ng = HD_AT - TAP_AT, GG_AT - TAP_AT, NG_AT - TAP_AT
    g_taps = small[0:5, 0:448].reshape(5, 1, 448)
    g_heads = small[hd : hd + 3, 0:NH]
    g_ggain = small[gg, 0:ZW]
    own_norm = small[ng]
    g_norm = own_norm
    for b in (1, 2, 3):
        g_norm = g_norm + trade("head", b)(own_norm)
    ng3 = advance(norm_gain, g_norm, norm_gain_momentum, norm_gain_average, RATES[0] / root)
    cv3 = advance(conv_params, g_taps, conv_momentum, conv_average, RATES[2] / root)
    hd3 = advance(head_params, g_heads, head_momentum, head_average, RATES[3] / root)
    gg3 = advance(gate_gain, g_ggain, gate_gain_momentum, gate_gain_average, RATES[4] / root)
    in3 = tuple(turned(a) for a in in_new)
    return (block_out, input_grad, *ng3, *in3, *cv3, *hd3, *gg3, out_w, out_m, out_a)


def solution(mesh):
    act, vec, mat = P(None, "seq", None), P(), P(None, "head", None)
    weights = (vec, mat, mat, P(None, "head"), P("head"), P("head", None))
    outs = tuple(spec for spec in weights for _ in range(3))
    return jax.shard_map(
        shards,
        mesh=mesh,
        in_specs=(act, act, P(), *weights, *weights, *weights),
        out_specs=(act, act, *outs),
        check_vma=False,
    )
```

```python
import functools
import math

import jax
import jax.numpy as jnp
from jax import lax
from jax.experimental import pallas as pl
from jax.experimental.pallas import tpu as pltpu
from jax.sharding import PartitionSpec as P

HDIM = 64
CONV = 4
INNER = 1536
EPSILON = 1e-05
MOMENTUM = 0.5
AVERAGE = 0.5
RATES = (0.15, 0.1, 0.5, 0.05, 0.15, 0.02)
HIGHEST = lax.Precision.HIGHEST
F32 = jnp.float32
BF16 = jnp.bfloat16
VMEM = 14
GRP = 4
BLK = 256
HALF = BLK // 2
QUART = BLK // 4
D = 768
ZW = 384
NH = 6
ST = 128
SW = 32
LANES = 128
WCOLS = D // LANES
WROWS = 2 * ZW + 2 * SW
TOK = GRP * BLK
COLS = WROWS + NH
SEG1 = 2 * ZW // GRP
SEG2 = 120
BC_AT, DT_AT, TAP_AT, HD_AT, GG_AT, NG_AT = 384, 448, 456, 464, 472, 473


def nt(a, b, precision=None):
    return lax.dot_general(
        a, b, (((1,), (1,)), ((), ())), preferred_element_type=F32, precision=precision
    )


def nn(a, b, precision=None):
    return lax.dot_general(
        a, b, (((1,), (0,)), ((), ())), preferred_element_type=F32, precision=precision
    )


def tn(a, b, precision=None):
    return lax.dot_general(
        a, b, (((0,), (0,)), ((), ())), preferred_element_type=F32, precision=precision
    )


def iota(shape, dim):
    return lax.broadcasted_iota(jnp.int32, shape, dim)


def split3(value):
    high = value.astype(BF16).astype(F32)
    rest = value - high
    mid = rest.astype(BF16).astype(F32)
    return high, mid, rest - mid


def side_by_side(value, used):
    high, mid, low = split3(jnp.where(iota(value.shape, 1) < used, value, 0.0))
    return (high + pltpu.roll(mid, used, 1) + pltpu.roll(low, 2 * used, 1)).astype(BF16)


def widen(packed, kinds):
    lane, col = iota((LANES, ZW), 0), iota((LANES, ZW), 1)
    goals = [((lane % 32 == col // HDIM + 8 * k) & (lane < 96)).astype(BF16) for k in kinds]
    parts = side_by_side(packed, 32)
    return [nn(parts, goal) for goal in goals]


def head_sums(values):
    goal = (iota((ZW, LANES), 1) == iota((ZW, LANES), 0) // HDIM).astype(BF16)
    high = values.astype(BF16)
    return nn(high, goal) + nn((values - high.astype(F32)).astype(BF16), goal)


def running_sums(triangle, values):
    total = nn(triangle, side_by_side(values, 8))
    total = total + pltpu.roll(total, LANES - 8, 1) + pltpu.roll(total, LANES - 16, 1)
    return jnp.where(iota(total.shape, 1) < 8, total, 0.0)


def lane_mask(which):
    return (iota((1, LANES), 1) // HDIM == which).astype(BF16)


def triangle(lower):
    row, col = iota((BLK, BLK), 0), iota((BLK, BLK), 1)
    return (row >= col if lower else row <= col).astype(BF16)


def call(
    kernel, name, grid, ins, in_specs, outs, out_specs, scratch=(), prefetch=None, flops=0,
    aliases=None, after=(), vmem=VMEM, light=False, token=False,
):
    count = len(ins) + (prefetch is not None)
    results = len(outs)

    def body(*refs):
        rest = refs[count + len(after) :]
        if token:
            rest[results][...] = jnp.zeros((8, LANES), F32)
            rest = rest[:results] + rest[results + 1 :]
        kernel(*refs[:count], *rest)

    outs, out_specs = list(outs), list(out_specs)
    if token:
        outs.append(sds((8, LANES)))
        out_specs.append(whole((8, LANES)))
    nbytes = sum(math.prod(a.shape) * a.dtype.itemsize for a in (*ins, *outs))
    if light:
        flops, nbytes = 1024, 1024
    spec = pltpu.PrefetchScalarGridSpec(
        num_scalar_prefetch=0 if prefetch is None else 1,
        grid=grid,
        in_specs=list(in_specs) + [pl.BlockSpec(memory_space=pl.ANY)] * len(after),
        out_specs=out_specs,
        scratch_shapes=scratch,
    )
    return pl.pallas_call(
        body,
        grid_spec=spec,
        out_shape=outs,
        compiler_params=pltpu.CompilerParams(
            dimension_semantics=("arbitrary",) * len(grid), vmem_limit_bytes=vmem << 20
        ),
        cost_estimate=pl.CostEstimate(flops=flops, bytes_accessed=nbytes, transcendentals=0),
        input_output_aliases=aliases or {},
        name=name,
    )(*(() if prefetch is None else (prefetch,)), *ins, *after)


def sds(shape, dtype=F32):
    return jax.ShapeDtypeStruct(shape, dtype)


def whole(shape):
    return pl.BlockSpec(shape, lambda *_: (0,) * len(shape))


def rows(width, height=BLK):
    return pl.BlockSpec((height, width), lambda i, *_: (i, 0))


def rows_back(width, height=BLK):
    return pl.BlockSpec((height, width), lambda i, *_: (GRP - 1 - i, 0))


def slot(height, width=D):
    return pl.BlockSpec((1, height, width), lambda i, at: (i ^ at[0], 0, 0))


def pick_kernel(at, *refs):
    for n, goal in enumerate(refs[2 * GRP :]):
        goal[0:HALF, :] = refs[n][0]
        if goal.shape[0] > HALF:
            goal[HALF:, :] = refs[GRP + n][0]


def pick(at, array, edge, after=()):
    def half_of(b):
        return pl.BlockSpec((1, HALF, D), lambda i, at: (at[0] ^ b, at[1], 0))

    def edge_of(b):
        return pl.BlockSpec((1, 16, D), lambda i, at: (at[0] ^ b, BLK // 16 - 1, 0))

    size = HALF + 16 * edge
    specs = [half_of(b) for b in range(GRP)] + [edge_of(b) for b in range(GRP)]
    return call(
        pick_kernel, "pick", (1,), (array,) * (2 * GRP), specs,
        [sds((size, D), BF16)] * GRP, [whole((size, D))] * GRP, prefetch=at, after=after,
    )


def stack_kernel(at, r0, r1, r2, r3, out_ref, *edge):
    refs = (r0, r1, r2, r3)
    for b, ref in enumerate(refs):
        out_ref[b] = ref[0:HALF, :]
    for goal in edge:
        for b, ref in enumerate(refs):

            @pl.when(at[0] ^ b == GRP - 1)
            def _():
                goal[...] = ref[HALF:, :]


def stack(at, parts, after=()):
    size = parts[0].shape[0]
    outs, specs = [sds((GRP, HALF, D), BF16)], [whole((GRP, HALF, D))]
    if size > HALF:
        outs, specs = outs + [sds((16, D), BF16)], specs + [whole((16, D))]
    return call(
        stack_kernel, "stack", (1,), parts, [whole((size, D))] * GRP, outs, specs, prefetch=at, after=after
    )


def prep_kernel(
    win, wout, taps, heads, ng, gg,
    w_ref, wdt_ref, low_ref, send_ref, hp_ref, vec_ref, wide_w, scr, sem,
):
    copy = pltpu.make_async_copy(win.at[:, 0, :], wide_w, sem)
    copy.start()
    low_ref[...] = wout[...].astype(BF16)
    scr[...] = jnp.zeros_like(scr)
    scr[0:3, 0:NH] = heads[...]
    lanes = scr[...]
    for by in (8, 16, 32, 64):
        lanes = lanes + pltpu.roll(lanes, by, 1)
    hp_ref[...] = lanes
    vec_ref[...] = jnp.zeros_like(vec_ref)
    vec_ref[0:1, :] = ng[...].reshape(1, D)
    vec_ref[1:2, 0:ZW] = gg[...].reshape(1, ZW)
    vec_ref[2:3, 0:ZW] = widen(lanes, (0,))[0][2:3, :]
    copy.wait()
    w_ref[...] = wide_w[0:WROWS, :].astype(BF16)
    last = jnp.concatenate([wide_w[WROWS:, :], jnp.zeros((8 - NH, D), F32)], axis=0)
    wdt_ref[...] = jnp.concatenate([last] * 16, axis=0).astype(BF16)
    send_ref[0 : 2 * SW, :] = w_ref[2 * ZW : WROWS, :]
    own = taps[:, 0, :][:, ZW:]
    high = own.astype(BF16).astype(F32)
    mid = (own - high).astype(BF16).astype(F32)
    low = own - high - mid
    parts = jnp.concatenate([high, mid, low, jnp.zeros((1, 2 * SW), F32)], axis=0)
    send_ref[2 * SW :, :] = jnp.zeros((16, D), BF16)
    send_ref[2 * SW :, 0 : 2 * SW] = parts.astype(BF16)


def chunk_of(own_ref, oth_ref, core):
    own, oth = own_ref[0], oth_ref[0]
    first = core == 0
    return jnp.concatenate([jnp.where(first, own, oth), jnp.where(first, oth, own)], axis=0)


def normalise(x, gain):
    u = x.astype(F32)
    scale = lax.rsqrt(jnp.mean(u * u, axis=-1, keepdims=True) + EPSILON)
    return (u * scale * gain).astype(BF16)


def first_kernel(at, own, oth, vecs, wz, wdt, hp, nrm_ref, z_ref, info_ref, row_ref, tot_ref, cum):
    step = pl.program_id(0)

    @pl.when(step == 0)
    def _():
        cum[...] = jnp.zeros_like(cum)

    normed = normalise(chunk_of(own, oth, at[1]), vecs[0:1, :])
    nrm_ref[...] = normed
    z_ref[...] = nt(normed, wz[...])
    biased = nt(normed, wdt[...]) + hp[0:1, :]
    steps = jax.nn.softplus(biased)
    decays = -jnp.exp(hp[1:2, :]) * steps
    c = running_sums(triangle(True), decays)
    group = iota((BLK, LANES), 1) // 8
    info = jnp.where(group == 0, c, jnp.where(group == 1, steps, biased))
    moved_c = pltpu.roll(c, 24, 1) + cum[0:1, :]
    info_ref[...] = jnp.where(group == 3, moved_c, info)
    row_ref[...] = jnp.transpose(c)[0:8, :]
    cum[0:1, :] = moved_c[BLK - 1 : BLK, :]
    tot_ref[...] = jnp.broadcast_to(cum[0:1, :], (8, LANES))


def mix_kernel(
    at, nrm, halo, vecs, wx, wo, bc0, bc1, bc2, bc3, taps, info,
    mx_ref, px_ref, xa_ref, xdt_ref, mo_ref, po_ref, b_ref, c_ref, h_ref, s_ref,
    wbc, tbc, ext, exto, state,
):
    step = pl.program_id(0)
    tap = taps[:, 0, :]

    @pl.when(step == 0)
    def _():
        place = jnp.zeros((16, 2 * ST), F32)
        for b, buf in enumerate((bc0, bc1, bc2, bc3)):
            wbc[SW * b : SW * (b + 1), :] = buf[0:SW, :]
            wbc[ST + SW * b : ST + SW * (b + 1), :] = buf[SW : 2 * SW, :]
            at_row, at_col = iota((2 * SW, 2 * ST), 0), iota((2 * SW, 2 * ST), 1)
            goal = jnp.where(at_row < SW, SW * b + at_row, ST + SW * b + at_row - SW)
            put = (at_col == goal).astype(BF16)
            place = place + nn(buf[2 * SW :, 0 : 2 * SW], put)
        tbc[0:5, :] = place[0:5] + place[5:10] + place[10:15]
        before = normalise(jnp.where(at[5] > 0, halo[...], 0.0).astype(BF16), vecs[0:1, :])
        ext[0:8, 0:ZW] = nt(before, wx[...])[8:16]
        ext[0:8, ZW:] = nt(before, wbc[...])[8:16]
        exto[0:8, :] = nt(before, wo[...])[8:16]
        state[...] = jnp.zeros_like(state)

    normed = nrm[...]
    mixed = nt(normed, wx[...])
    mx_ref[...] = mixed
    ext[8:, 0:ZW] = mixed
    ext[8:, ZW:] = nt(normed, wbc[...])
    own = nt(normed, wo[...])
    mo_ref[...] = own
    exto[8:, :] = own
    pre = tap[4:5, 0:ZW]
    pre_bc = tbc[4:5, :]
    pre_o = tap[4:5, ZW:]
    for k in range(CONV):
        pre = pre + tap[k : k + 1, 0:ZW] * ext[5 + k : 5 + k + BLK, 0:ZW]
        pre_bc = pre_bc + tbc[k : k + 1, :] * ext[5 + k : 5 + k + BLK, ZW:]
        pre_o = pre_o + tap[k : k + 1, ZW:] * exto[5 + k : 5 + k + BLK, :]
    px_ref[...] = pre
    po_ref[...] = pre_o
    x = pre * jax.nn.sigmoid(pre)
    xa_ref[...] = x
    bc = (pre_bc * jax.nn.sigmoid(pre_bc)).astype(BF16)
    b_ref[...] = bc[:, 0:ST]
    c_ref[...] = bc[:, ST:]
    ext[0:8, :] = ext[BLK:, :]
    exto[0:8, :] = exto[BLK:, :]

    packed = info[...]
    c = packed[:, 0:LANES]
    keep = iota((BLK, LANES), 1) < 8
    tail = jnp.where(keep, jnp.exp(jnp.where(keep, c[BLK - 1 : BLK, :] - c, 0.0)), 0.0)
    tail_wide, dt_wide = widen(jnp.where(keep, tail, packed), (0, 1))
    xdt = x * dt_wide
    xdt_ref[...] = xdt.astype(BF16)
    fresh = tn((xdt * tail_wide).astype(BF16), bc[:, 0:ST])
    h_ref[0] = state[...]
    for h in range(NH):
        decay = jnp.exp(packed[BLK - 1 : BLK, h : h + 1])
        at = pl.ds(HDIM * h, HDIM)
        state[at, :] = decay * state[at, :] + fresh[HDIM * h : HDIM * (h + 1), :]
    s_ref[...] = state[...].astype(BF16)


def weights_of(h, packed, row, causal):
    diff = packed[:, h : h + 1] - row[h : h + 1, :]
    return jnp.where(causal, jnp.exp(jnp.where(causal, diff, 0.0)), 0.0)


def local_kernel(
    at, xdt, xa, b, c, info, row, hloc, own, oth, low, vecs, yl_ref, dyn_ref, w_ref
):
    step = pl.program_id(0)
    packed = info[...]
    rowc = row[...]
    causal = iota((BLK, BLK), 0) >= iota((BLK, BLK), 1)
    scores = nt(c[...], b[...])
    c_exp = jnp.exp(jnp.where(iota((BLK, LANES), 1) < 8, packed, 0.0))
    carried = nt(c[...], hloc[0].astype(BF16)) * widen(c_exp, (0,))[0]
    carried = carried + vecs[2:3, 0:ZW] * xa[...]
    for p in range(NH // 2):
        x = xdt[:, LANES * p : LANES * (p + 1)]
        total = carried[:, LANES * p : LANES * (p + 1)]
        for q in range(2):
            weights = (weights_of(2 * p + q, packed, rowc, causal) * scores).astype(BF16)
            total = total + nn(weights, x * lane_mask(q))
        yl_ref[:, LANES * p : LANES * (p + 1)] = total
    place = (at[2] * GRP + step) * BLK + iota((BLK, 1), 0)
    live = place < at[7 + at[0]]
    w = jnp.where(live, chunk_of(own, oth, at[1]), 0.0).astype(BF16)
    w_ref[...] = w
    dyn_ref[...] = nt(w, low[...])


def gate_kernel(at, yl, c, info, hin, z, dyn, vecs, y_ref, sum_ref):
    packed = info[...]
    lane = iota((BLK, LANES), 1)
    cum = jnp.where(lane // 8 == 3, jnp.exp(jnp.where(lane // 8 == 3, packed, 0.0)), 0.0)
    entering = jnp.where(at[5] > 0, hin[...], 0.0).astype(BF16)
    y = yl[...] + nt(c[...], entering) * widen(cum, (3,))[0]
    y_ref[...] = y
    gate = z[...]
    g = y * (gate * jax.nn.sigmoid(gate))
    squares = jnp.sum(g * g, axis=-1, keepdims=True)
    inner = jnp.sum(dyn[...] * vecs[1:2, 0:ZW] * g, axis=-1, keepdims=True)
    both = jnp.where(lane == 0, squares, jnp.where(lane == 1, inner, 0.0))
    sum_ref[...] = jnp.transpose(both)[0:8, :]


def ungate_kernel(
    at, y, z, dyn, s0, s1, s2, s3, info, c, vecs, low,
    dy_ref, dz_ref, yn_ref, p_ref, gg_ref, keep_ref, send_ref, acc,
):
    step = pl.program_id(0)

    @pl.when(step == 0)
    def _():
        acc[...] = jnp.zeros_like(acc)
        gg_ref[...] = jnp.zeros_like(gg_ref)

    sums = s0[...] + s1[...] + s2[...] + s3[...]
    sums = jnp.transpose(jnp.concatenate([sums, jnp.zeros((LANES - 8, BLK), F32)], axis=0))
    q = lax.rsqrt(sums[:, 0:1] / INNER + EPSILON)
    mean = sums[:, 1:2] * q / INNER
    gate = z[...]
    sigma = jax.nn.sigmoid(gate)
    silu = gate * sigma
    out = y[...]
    g = out * silu
    n = g * q
    d = dyn[...]
    gg = vecs[1:2, 0:ZW]
    d_g = q * (d * gg - n * mean)
    d_y = d_g * silu
    dy_ref[...] = d_y
    dz_ref[...] = (d_g * out * sigma * (1.0 + gate * (1.0 - sigma))).astype(BF16)
    yn = (n * gg).astype(BF16)
    yn_ref[...] = yn
    halves(nn(yn, low[...]).astype(BF16), at[1], keep_ref, send_ref)
    gg_ref[0:1, :] += jnp.sum(d * n, axis=0, keepdims=True)
    packed = info[...]
    lane = iota((BLK, LANES), 1)
    cum = jnp.where(lane // 8 == 3, jnp.exp(jnp.where(lane // 8 == 3, packed, 0.0)), 0.0)
    acc[...] += tn((d_y * widen(cum, (3,))[0]).astype(BF16), c[...])
    p_ref[...] = acc[...].astype(BF16)


def halves(value, core, keep_ref, send_ref):
    low, high = value[0:HALF], value[HALF:]
    first = core == 0
    keep_ref[0] = jnp.where(first, low, high)
    send_ref[0] = jnp.where(first, high, low)


def out_kernel(
    at, yn, w, nrm, dz, g0, g1, g2, g3, acc
):
    step = pl.program_id(0)

    @pl.when(step == 0)
    def _():
        acc[...] = jnp.zeros_like(acc)

    acc[0:ZW, :] += tn(dz[...], nrm[...])
    acc[ZW:, :] += tn(yn[...], w[...])

    @pl.when(step == GRP - 1)
    def _():
        for b, ref in enumerate((g0, g1, g2, g3)):
            start = pl.multiple_of((at[0] ^ b) * SEG1, SEG1)
            ref[...] = acc[pl.ds(start, SEG1), :].astype(BF16)


def inner_kernel(
    at, xdt, b, c, info, row, dy, hloc, hin, dxi_ref, dbi_ref, dci_ref, dcum_ref, hall_ref
):
    packed = info[...]
    rowc = row[...]
    lane = iota((BLK, LANES), 1)
    causal = iota((BLK, BLK), 0) >= iota((BLK, BLK), 1)
    bb, cc = b[...], c[...]
    scores = nt(cc, bb)
    d_scores = jnp.zeros((BLK, BLK), F32)
    d_cum = jnp.zeros((BLK, LANES), F32)
    columns = []
    dyv = dy[...]
    for p in range(NH // 2):
        x = xdt[:, LANES * p : LANES * (p + 1)]
        d = dyv[:, LANES * p : LANES * (p + 1)].astype(BF16)
        total = jnp.zeros((BLK, LANES), F32)
        for q in range(2):
            h = 2 * p + q
            spans = weights_of(h, packed, rowc, causal)
            d_h = d * lane_mask(q)
            d_spans = nt(d_h, x) * spans
            d_scores = d_scores + d_spans
            both = d_spans * scores
            d_cum = d_cum + jnp.where(lane == h, jnp.sum(both, axis=1, keepdims=True), 0.0)
            columns.append(jnp.sum(both, axis=0, keepdims=True))
            total = total + tn((spans * scores).astype(BF16), d_h)
        dxi_ref[:, LANES * p : LANES * (p + 1)] = total
    columns = jnp.concatenate(columns + [jnp.zeros((LANES - NH, BLK), F32)], axis=0)
    d_cum = d_cum - jnp.transpose(columns)
    low_scores = d_scores.astype(BF16)
    c_exp = jnp.exp(jnp.where(lane < 8, packed, 0.0))
    c_wide = widen(c_exp, (0,))[0]
    base = packed[0:1, 24:32] - packed[0:1, 0:8]
    for h in range(NH):
        here = pl.ds(HDIM * h, HDIM)
        grown = jnp.exp(base[:, h : h + 1]) * hin[here, :].astype(F32)
        grown = jnp.where(at[5] > 0, grown, 0.0)
        hall_ref[0, here, :] = hloc[0, here, :] + grown
    entering = hall_ref[0].astype(BF16)
    carried = nt(cc, entering) * c_wide
    d_cum = d_cum + head_sums(dyv * carried)
    dcum_ref[...] = d_cum
    dci_ref[...] = nn(low_scores, bb) + nn((dyv * c_wide).astype(BF16), entering)
    dbi_ref[...] = tn(low_scores, cc)


def back_kernel(
    at, after, dxi, dbi, dci, dcum, hall, xa, px, b, c, info, dy, hp, vecs,
    dpx_ref, halo_ref, o0, o1, o2, o3, draw_ref, hg_ref, state,
):
    step = pl.program_id(0)

    @pl.when(step == 0)
    def _():
        state[...] = jnp.where(at[6] > 0, after[...].astype(F32), 0.0)
        hg_ref[...] = jnp.zeros_like(hg_ref)

    packed = info[...]
    lane = iota((BLK, LANES), 1)
    first = lane < 8
    c_last = packed[BLK - 1 : BLK, :]
    tail = jnp.where(first, jnp.exp(jnp.where(first, c_last - packed, 0.0)), 0.0)
    c_exp = jnp.where(first, jnp.exp(jnp.where(first, packed, 0.0)), 0.0)
    mixed = jnp.where(first, tail, jnp.where(lane < 16, packed, pltpu.roll(c_exp, 16, 1)))
    tail_wide, dt_wide, c_wide = widen(mixed, (0, 1, 2))
    x = xa[...]
    xdt = x * dt_wide
    d_y = dy[...]
    bb, cc = b[...], c[...]
    low_state = state[...].astype(BF16)
    d_tail = nt(bb, low_state) * tail_wide
    tails = head_sums(xdt * d_tail)
    d_xdt = dxi[...] + d_tail
    d_b = dbi[...] + nn((xdt * tail_wide).astype(BF16), low_state)
    d_c = dci[...]
    ending = jnp.sum(tails, axis=0, keepdims=True)
    lane1 = iota((1, LANES), 1)
    for h in range(NH):
        here = pl.ds(HDIM * h, HDIM)
        inner = jnp.sum(state[here, :] * hall[0, here, :], axis=(0, 1), keepdims=True)
        ending = ending + jnp.where(lane1 == h, inner * jnp.exp(c_last[:, h : h + 1]), 0.0)
    d_cum = dcum[...] - tails
    d_cum = d_cum + jnp.where(iota((BLK, LANES), 0) == BLK - 1, ending, 0.0)
    d_a = running_sums(triangle(False), d_cum)
    fresh = tn((d_y * c_wide).astype(BF16), cc)
    for h in range(NH):
        here = pl.ds(HDIM * h, HDIM)
        decay = jnp.exp(c_last[:, h : h + 1])
        state[here, :] = decay * state[here, :] + fresh[HDIM * h : HDIM * (h + 1), :]
    rate = -jnp.exp(hp[1:2, :])
    d_dt = head_sums(x * d_xdt) + rate * d_a
    biased = pltpu.roll(packed, LANES - 16, 1)
    steps = pltpu.roll(packed, LANES - 8, 1)
    used = lane < NH
    d_raw = jnp.where(used, d_dt * jax.nn.sigmoid(jnp.where(used, biased, 0.0)), 0.0)
    draw_ref[...] = d_raw.astype(BF16)
    hg_ref[0:1, :] += jnp.sum(d_raw, axis=0, keepdims=True)
    g_rate = jnp.where(used, d_a * rate * jnp.where(used, steps, 0.0), 0.0)
    hg_ref[1:2, :] += jnp.sum(g_rate, axis=0, keepdims=True)
    hg_ref[2:3, :] += jnp.sum(head_sums(d_y * x), axis=0, keepdims=True)
    d_x = d_xdt * dt_wide + vecs[2:3, 0:ZW] * d_y
    pre = px[...]
    sigma = jax.nn.sigmoid(pre)
    d_pre = d_x * sigma * (1.0 + pre * (1.0 - sigma))
    dpx_ref[...] = d_pre
    halo_ref[...] = d_pre[0:8]
    for s, ref in enumerate((o0, o1, o2, o3)):
        for n, value in enumerate((d_b, d_c)):
            mine = value[:, SW * s : SW * (s + 1)].astype(BF16)
            ref[:, SW * n : SW * (n + 1)] = mine[0:HALF]
            ref[:, SW * (n + 2) : SW * (n + 3)] = mine[HALF:]


def edge_kernel(o0, r1, r2, r3, po, dpo_ref, halo_ref):
    d = o0[...].astype(F32) + r1[...].astype(F32) + r2[...].astype(F32) + r3[...].astype(F32)
    d = jnp.concatenate([d[:, 0 : 2 * SW], d[:, 2 * SW :]], axis=0)
    pre = po[...]
    sigma = jax.nn.sigmoid(pre)
    d = d * sigma * (1.0 + pre * (1.0 - sigma))
    dpo_ref[...] = d

    @pl.when(pl.program_id(0) == 0)
    def _():
        halo_ref[...] = d[0:8]


def unconvolve(acc, ext, d_pre, follows, values, tap, lanes):
    ext[0:BLK, :] = d_pre
    ext[BLK:, :] = follows
    total = jnp.zeros(d_pre.shape, F32)
    for k in range(CONV):
        shifted = ext[3 - k : 3 - k + BLK, :]
        total = total + tap[k : k + 1, lanes] * shifted
        acc[TAP_AT + k : TAP_AT + k + 1, lanes] += jnp.sum(values * shifted, axis=0, keepdims=True)
    acc[TAP_AT + CONV : TAP_AT + CONV + 1, lanes] += jnp.sum(d_pre, axis=0, keepdims=True)
    return total.astype(BF16)


X_LANES, O_LANES = slice(0, ZW), slice(ZW, ZW + 2 * SW)


def last_x_kernel(
    at, dpx, nx, halo, mx, taps, dz, draw, nrm, w, wdt, pb_ref, acc, ext
):
    step = pl.program_id(0)

    @pl.when(step == 0)
    def _():
        acc[...] = jnp.zeros_like(acc)

    follows = jnp.where(step < GRP - 1, nx[...], jnp.where(at[6] > 0, halo[...], 0.0))
    p_x = unconvolve(acc, ext, dpx[...], follows, mx[...], taps[:, 0, :], X_LANES)
    p_t = draw[...]
    pb_ref[...] = nn(dz[...], w[0:ZW, :]) + nn(p_x, w[ZW:, :]) + nn(p_t, wdt[...])
    normed = nrm[...]
    acc[0:ZW, :] += tn(p_x, normed)
    acc[DT_AT : DT_AT + 8, :] += tn(p_t, normed)[0:8]


def last_o_kernel(
    at, dpo, no, halo, mo, taps, nrm, w, pb, vecs, gg, hg, acc_in,
    keep_ref, send_ref, g0, g1, g2, g3, ext, acc,
):
    step = pl.program_id(0)

    @pl.when(step == 0)
    def _():
        acc[...] = acc_in[...]
        acc[HD_AT : HD_AT + 8, 0:LANES] = hg[...]
        acc[GG_AT : GG_AT + 1, 0:ZW] = gg[0:1, :]

    follows = jnp.where(step < GRP - 1, no[...], jnp.where(at[6] > 0, halo[...], 0.0))
    p_o = unconvolve(acc, ext, dpo[...], follows, mo[...], taps[:, 0, :], O_LANES)
    back = pb[...] + nn(p_o, w[...])
    halves(back.astype(BF16), at[1], keep_ref, send_ref)
    normed = nrm[...]
    acc[NG_AT : NG_AT + 1, :] += jnp.sum(back * normed.astype(F32), axis=0, keepdims=True)
    acc[BC_AT:DT_AT, :] += tn(p_o, normed)

    @pl.when(step == GRP - 1)
    def _():
        acc[NG_AT : NG_AT + 1, :] = acc[NG_AT : NG_AT + 1, :] / vecs[0:1, :]
        for b, ref in enumerate((g0, g1, g2, g3)):
            start = pl.multiple_of((at[0] ^ b) * SEG2, 8)
            ref[...] = acc[pl.ds(start, SEG2), :].astype(BF16)


def split_kernel(at, keep, other, keep_ref, send_ref):
    value = keep[0].astype(F32) + other[0].astype(F32)
    low, high = value[0:QUART], value[QUART:]
    first = at[4] == 0
    keep_ref[0] = jnp.where(first, low, high)
    send_ref[0] = jnp.where(first, high, low).astype(BF16)


def add_kernel(keep, other, r0, r1, r2, r3):
    for b, ref in enumerate((r0, r1, r2, r3)):
        ref[...] = (keep[b] + other[b].astype(F32)).astype(BF16)


def sum_kernel(*refs):
    total = refs[0][...].astype(F32)
    for ref in refs[1:-1]:
        total = total + ref[...].astype(F32)
    refs[-1][...] = total.astype(refs[-1].dtype)


def place_quarters(at, b, parts, scr):
    core, xbit = at[1], at[4]
    for n, ref in enumerate(parts):
        half = core if n < 2 else 1 - core
        quarter = xbit if n % 2 == 0 else 1 - xbit
        start = pl.multiple_of(half * HALF + quarter * QUART, QUART)
        scr[pl.ds(start, QUART), :] = ref[0]


def home_out_kernel(at, block, a, x, ac, xc, out_ref, scr):
    step = pl.program_id(0)
    place_quarters(at, step, (a, x, ac, xc), scr)
    place = (at[2] * GRP + at[0]) * BLK + iota((BLK, 1), 0)
    live = place < at[7 + step]
    total = block[0].astype(F32) + scr[...].astype(F32)
    out_ref[0] = jnp.where(live, total, 0.0).astype(BF16)


def home_grad_kernel(at, block, cot, vecs, a, x, ac, xc, out_ref, scr):
    step = pl.program_id(0)
    place_quarters(at, step, (a, x, ac, xc), scr)
    place = (at[2] * GRP + at[0]) * BLK + iota((BLK, 1), 0)
    live = place < at[7 + step]
    u = block[0].astype(F32)
    scale = lax.rsqrt(jnp.mean(u * u, axis=-1, keepdims=True) + EPSILON)
    m = u * scale
    f = scr[...].astype(F32) * vecs[0:1, :]
    inner = jnp.mean(f * m, axis=-1, keepdims=True)
    out_ref[0] = scale * (f - m * inner) + jnp.where(live, cot[0].astype(F32), 0.0)


def home(kernel, name, at, arrays, specs, parts, dtype, after=()):
    full = pl.BlockSpec((1, BLK, D), lambda i, *_: (i, 0, 0))
    part = pl.BlockSpec((1, QUART, D), lambda i, at: (i ^ at[0], 0, 0))
    specs = [full if s is None else whole(s) for s in specs]
    return call(
        kernel, name, (GRP,), (*arrays, *parts), specs + [part] * 4, [sds((GRP, BLK, D), dtype)],
        [full], scratch=[pltpu.VMEM((BLK, D), BF16)], prefetch=at, after=after, token=True,
    )


def advance(weight, gradient, moment, average, rate):
    moment_new = MOMENTUM * moment + gradient
    weight_new = weight - rate * (gradient + MOMENTUM * moment_new)
    average_new = AVERAGE * average + (1.0 - AVERAGE) * weight_new
    return (weight_new, moment_new, average_new)


def stepped(grad_of, weights, outs, blocks, buffers, sems, rate):
    ins, done = buffers[:3], buffers[3:]

    def reads(n):
        start, size = blocks[n]
        return [
            pltpu.make_async_copy(
                w.at[pl.ds(start, size), 0, :], buf.at[pl.ds(start, size), :], sems.at[n, j]
            )
            for j, (w, buf) in enumerate(zip(weights, ins))
        ]

    def writes(n):
        start, size = blocks[n]
        return [
            pltpu.make_async_copy(
                buf.at[pl.ds(start, size), :], o.at[pl.ds(start, size), 0, :], sems.at[n, 3 + j]
            )
            for j, (o, buf) in enumerate(zip(outs, done))
        ]

    for n in range(len(blocks)):
        for copy in reads(n):
            copy.start()
    for n, (start, size) in enumerate(blocks):
        for copy in reads(n):
            copy.wait()
        here = pl.ds(start, size)
        new = advance(ins[0][here, :], grad_of(n), ins[1][here, :], ins[2][here, :], rate)
        for buf, value in zip(done, new):
            buf[here, :] = value
        for copy in writes(n):
            copy.start()
    for n in range(len(blocks)):
        for copy in writes(n):
            copy.wait()


Z_BLOCKS = tuple((96 * n, 96) for n in range(4))
X_BLOCKS = tuple((ZW + 96 * n, 96) for n in range(4)) + ((2 * ZW, COLS - 2 * ZW),)


def update_a_kernel(
    at, g0, g1, g2, g3, w, m, a, wi, mi, ai, w_ref, m_ref, a_ref, wo, mo, ao,
    grad, b0, b1, b2, b3, b4, b5, sems, *, rate, rate_in,
):
    for b, ref in enumerate((g0, g1, g2, g3)):
        grad[pl.ds(pl.multiple_of((at[0] ^ b) * SEG1, SEG1), SEG1), :] = ref[0:SEG1, :].astype(F32)
    stepped(
        lambda n: grad[96 * n : 96 * (n + 1), :], (wi, mi, ai), (wo, mo, ao), Z_BLOCKS,
        (b0, b1, b2, b3, b4, b5), sems, rate_in,
    )
    w_ref[...], m_ref[...], a_ref[...] = advance(w[...], grad[ZW:, :], m[...], a[...], rate)


def update_b_kernel(
    at, g0, g1, g2, g3, wi, mi, ai, x0, x1, x2, wo, mo, ao,
    grad, b0, b1, b2, b3, b4, b5, sems, *, rate,
):
    for b, ref in enumerate((g0, g1, g2, g3)):
        start = pl.multiple_of((at[0] ^ b) * SEG2, 8)
        grad[pl.ds(start, SEG2), :] = ref[...].astype(F32)
    stepped(
        lambda n: grad[96 * n : min(96 * (n + 1), COLS - ZW), :], (wi, mi, ai), (wo, mo, ao), X_BLOCKS,
        (b0, b1, b2, b3, b4, b5), sems, rate,
    )


SMALL = GRP * SEG2 - TAP_AT


def small_kernel(at, g0, g1, g2, g3, small_ref, norm_ref):
    for b, ref in enumerate((g0, g1, g2, g3)):

        @pl.when(at[0] ^ b == GRP - 1)
        def _():
            small_ref[...] = ref[SEG2 - SMALL :, :].astype(F32)
            norm_ref[...] = ref[SEG2 - 8 :, :].astype(F32)


def update_small_kernel(
    small, n0, n1, n2, n3, ng, ngm, nga, cv, cvm, cva, hd, hdm, hda, gg, ggm, gga, *outs, rates
):
    ng_o, cv_o, hd_o, gg_o = (outs[3 * n : 3 * n + 3] for n in range(4))
    at_norm = NG_AT - TAP_AT - (SMALL - 8)
    norms = [n[at_norm : at_norm + 1, :] for n in (n0, n1, n2, n3)]
    grad = (norms[0] + norms[1] + norms[2] + norms[3]).reshape(D)
    for ref, new in zip(ng_o, advance(ng[...], grad, ngm[...], nga[...], rates[0])):
        ref[...] = new
    grad = small[0:5, 0 : ZW + 2 * SW]
    old = [a[:, 0, :] for a in (cv, cvm, cva)]
    for ref, new in zip(cv_o, advance(old[0], grad, old[1], old[2], rates[2])):
        ref[:, 0, :] = new
    at_head = HD_AT - TAP_AT
    grad = small[at_head : at_head + 3, 0:NH]
    for ref, new in zip(hd_o, advance(hd[...], grad, hdm[...], hda[...], rates[3])):
        ref[...] = new
    at_gate = GG_AT - TAP_AT
    grad = small[at_gate : at_gate + 1, 0:ZW].reshape(ZW)
    for ref, new in zip(gg_o, advance(gg[...], grad, ggm[...], gga[...], rates[4])):
        ref[...] = new


def trade(axis, flip):
    count = lax.axis_size(axis)
    pairs = [(i, i ^ flip) for i in range(count)]
    return lambda array: lax.ppermute(array, axis, pairs)


def moved(array, by):
    count = lax.axis_size("seq")
    if count == 2 * abs(by):
        return trade("seq", abs(by))(array)
    pairs = [(i, i + by) for i in range(count) if 0 <= i + by < count]
    return lax.ppermute(array, "seq", pairs)


def grow(decay, state):
    return jnp.repeat(decay[0, 24 : 24 + NH], HDIM)[:, None] * state


def pieces_before(state, logs, way):
    count = lax.axis_size("seq") // GRP
    found = moved(state, way * GRP)
    by = 1
    if count > 2:
        there = lax.axis_index("seq") // GRP
        decay = moved(jnp.exp(logs), way * GRP)
        total = found.astype(F32)
        while by < count - 1:
            inside = (there >= by) if way > 0 else (there + by < count)
            earlier = moved(total.astype(BF16), way * GRP * by).astype(F32)
            total = jnp.where(inside, grow(decay, earlier) + total, total)
            decay = decay * moved(decay, way * GRP * by)
            by *= 2
        found = total.astype(BF16)
    return found


def group_sum(parts, height, after=()):
    return add_rows(height, [parts[0]] + [trade("seq", b)(parts[b]) for b in (1, 2, 3)], after)


def add_rows(height, arrays, after=()):
    spec = whole((height, D))
    out = [sds((height, D), BF16)]
    return call(sum_kernel, "sum", (1,), arrays, [spec] * len(arrays), out, [spec], after=after)[0]


def across_groups(mine, height, after=()):
    by = GRP
    while by < lax.axis_size("seq"):
        mine = add_rows(height, [mine, trade("seq", by)(mine)], after)
        by *= 2
    return mine


def all_quarters(mine):
    return [mine] + [trade("seq", b)(mine) for b in (1, 2, 3)]


def slot_of(height):
    return pl.BlockSpec((1, height, D), lambda i, at: (i, 0, 0))


def split_sum(at, keep, send, after=()):
    other = trade("head", 1)(send)
    return call(
        split_kernel, "split", (GRP,), (keep, other), [slot_of(HALF)] * 2,
        [sds((GRP, QUART, D)), sds((GRP, QUART, D), BF16)], [slot_of(QUART)] * 2,
        prefetch=at, after=after,
    )


def quarter_sum(keep, send, after=()):
    other = trade("head", 2)(send)
    every = whole((GRP, QUART, D))
    return call(
        add_kernel, "add", (1,), (keep, other), [every] * 2,
        [sds((QUART, D), BF16)] * 4, [whole((QUART, D))] * 4, after=after,
    )


def join_kernel(r0, r1, r2, r3, out_ref):
    for b, ref in enumerate((r0, r1, r2, r3)):
        out_ref[b] = ref[ref.shape[0] - QUART :, :]


def quarter_home(parts, after=()):
    return join([parts[0]] + [trade("seq", b)(parts[b]) for b in (1, 2, 3)], after)


def join(got, after=()):
    return call(
        join_kernel, "join", (1,), got, [whole(a.shape) for a in got],
        [sds((GRP, QUART, D), BF16)], [whole((GRP, QUART, D))], after=after,
    )[0]


def all_home(a):
    x = trade("head", 2)(a)
    return a, x, trade("head", 1)(a), trade("head", 1)(x)


def shards(
    block_in, cotangent, lengths,
    norm_gain, in_proj, conv_params, head_params, gate_gain, out_proj,
    norm_gain_momentum, in_proj_momentum, conv_momentum, head_momentum, gate_gain_momentum,
    out_proj_momentum,
    norm_gain_average, in_proj_average, conv_average, head_average, gate_gain_average,
    out_proj_average,
):
    seq_at, head_at = lax.axis_index("seq"), lax.axis_index("head")
    place = seq_at % GRP
    groups = lax.axis_size("seq") // GRP
    group = seq_at // GRP
    at = [place, head_at % 2, group, 0, head_at // 2, group > 0, group < groups - 1]
    at = jnp.concatenate([jnp.stack([jnp.asarray(v, jnp.int32) for v in at]), lengths])

    def turned(array):
        return jnp.transpose(array, (2, 1, 0))

    anyspec = pl.BlockSpec(memory_space=pl.ANY)
    picked = pick(at, block_in, True)
    got = [picked[0]] + [trade("seq", b)(picked[b]) for b in (1, 2, 3)]
    w, wdt, low, send_bc, hp, vecs = call(
        prep_kernel, "prep", (1,),
        (turned(in_proj), out_proj, conv_params, head_params, norm_gain, gate_gain),
        [anyspec, whole((ZW, D)), whole((5, 1, 448)), whole((3, NH)), whole((D,)), whole((ZW,))],
        [sds((WROWS, D), BF16), sds((LANES, D), BF16), sds((ZW, D), BF16), sds((80, D), BF16),
         sds((8, LANES)), sds((8, D))],
        [whole((WROWS, D)), whole((LANES, D)), whole((ZW, D)), whole((80, D)), whole((8, LANES)), whole((8, D))],
        scratch=[pltpu.VMEM((COLS, D), F32), pltpu.VMEM((8, LANES), F32), pltpu.SemaphoreType.DMA],
        after=(picked[0],),
    )
    bcs = [send_bc] + [trade("head", b)(send_bc) for b in (1, 2, 3)]
    own, edge = stack(at, got, (w, *bcs[1:]))
    oth = trade("head", 1)(own)
    halo = moved(edge, GRP)
    cot_picked = pick(at, cotangent, False, (w,))
    cot_got = [cot_picked[0]] + [trade("seq", b)(cot_picked[b]) for b in (1, 2, 3)]

    def wblock(n, height):
        return pl.BlockSpec((height, D), lambda i, *_: (n, 0))

    nrm, z, info, rowc, logs = call(
        first_kernel, "first", (GRP,), (own, oth, vecs, w, wdt, hp),
        [slot(HALF), slot(HALF), whole((8, D)), wblock(0, ZW), whole((LANES, D)), whole((8, LANES))],
        [sds((TOK, D), BF16), sds((TOK, ZW)), sds((TOK, LANES)), sds((8, TOK)), sds((8, LANES))],
        [rows(D), rows(ZW), rows(LANES), pl.BlockSpec((8, BLK), lambda i, *_: (0, i)), whole((8, LANES))],
        scratch=[pltpu.VMEM((8, LANES), F32)], prefetch=at, flops=2 * TOK * D * 512, after=(halo,),
    )
    hspec = pl.BlockSpec((1, ZW, ST), lambda i, *_: (i, 0, 0))
    rowspec = pl.BlockSpec((8, BLK), lambda i, *_: (0, i))
    mx, px, xa, xdt, mo, po, bb, cc, hloc, fresh = call(
        mix_kernel, "mix", (GRP,), (nrm, halo, vecs, w, w, *bcs, conv_params, info),
        [rows(D), whole((16, D)), whole((8, D)), wblock(1, ZW), wblock(12, 2 * SW)]
        + [whole((80, D))] * 4 + [whole((5, 1, 448)), rows(LANES)],
        [sds((TOK, ZW)), sds((TOK, ZW)), sds((TOK, ZW)), sds((TOK, ZW), BF16), sds((TOK, 2 * SW)),
         sds((TOK, 2 * SW)), sds((TOK, ST), BF16), sds((TOK, ST), BF16), sds((GRP, ZW, ST)),
         sds((ZW, ST), BF16)],
        [rows(ZW), rows(ZW), rows(ZW), rows(ZW), rows(2 * SW), rows(2 * SW), rows(ST), rows(ST),
         hspec, whole((ZW, ST))],
        scratch=[pltpu.VMEM((2 * ST, D), BF16), pltpu.VMEM((8, 2 * ST), F32),
                 pltpu.VMEM((BLK + 8, ZW + 2 * ST), F32), pltpu.VMEM((BLK + 8, 2 * SW), F32),
                 pltpu.VMEM((ZW, ST), F32)],
        flops=2 * TOK * D * 704, prefetch=at,
    )
    hin = pieces_before(fresh, logs, 1)
    cot_own = stack(at, cot_got, (fresh,))[0]
    cot_oth = trade("head", 1)(cot_own)
    yl, dyn, w_live = call(
        local_kernel, "local", (GRP,),
        (xdt, xa, bb, cc, info, rowc, hloc, cot_own, cot_oth, low, vecs),
        [rows(ZW), rows(ZW), rows(ST), rows(ST), rows(LANES), rowspec, hspec, slot(HALF),
         slot(HALF), whole((ZW, D)), whole((8, D))],
        [sds((TOK, ZW)), sds((TOK, ZW)), sds((TOK, D), BF16)], [rows(ZW), rows(ZW), rows(D)],
        prefetch=at, flops=2 * TOK * (D * ZW + 4 * BLK * ZW),
    )
    y, sums = call(
        gate_kernel, "gate", (GRP,), (yl, cc, info, hin, z, dyn, vecs),
        [rows(ZW), rows(ST), rows(LANES), whole((ZW, ST)), rows(ZW), rows(ZW), whole((8, D))],
        [sds((TOK, ZW)), sds((8, TOK))], [rows(ZW), rowspec], prefetch=at, flops=2 * TOK * ST * ZW,
    )
    all_sums = [sums] + [trade("head", b)(sums) for b in (1, 2, 3)]
    half_slot = pl.BlockSpec((1, HALF, D), lambda i, at: (i ^ at[0], 0, 0))
    dy, dz, yn, pulled, g_gate, keep, send = call(
        ungate_kernel, "ungate", (GRP,), (y, z, dyn, *all_sums, info, cc, vecs, low),
        [rows(ZW)] * 3 + [rowspec] * 4 + [rows(LANES), rows(ST), whole((8, D)), whole((ZW, D))],
        [sds((TOK, ZW)), sds((TOK, ZW), BF16), sds((TOK, ZW), BF16), sds((ZW, ST), BF16), sds((8, ZW))]
        + [sds((GRP, HALF, D), BF16)] * 2,
        [rows(ZW), rows(ZW), rows(ZW), whole((ZW, ST)), whole((8, ZW))] + [half_slot] * 2,
        scratch=[pltpu.VMEM((ZW, ST), F32)], flops=2 * TOK * (ST + D) * ZW, prefetch=at,
    )
    after = pieces_before(pulled, logs, -1)
    grads1 = call(
        out_kernel, "out", (GRP,), (yn, w_live, nrm, dz),
        [rows(ZW), rows(D), rows(D), rows(ZW)],
        [sds((SEG1, D), BF16)] * 4, [whole((SEG1, D))] * 4,
        scratch=[pltpu.VMEM((2 * ZW, D), F32)], prefetch=at, flops=4 * TOK * D * ZW,
    )
    keep2, send2 = split_sum(at, keep, send, (grads1[0],))
    dxi, dbi, dci, dcum, hall = call(
        inner_kernel, "inner", (GRP,), (xdt, bb, cc, info, rowc, dy, hloc, hin),
        [rows(ZW), rows(ST), rows(ST), rows(LANES), rowspec, rows(ZW), hspec, whole((ZW, ST))],
        [sds((TOK, ZW)), sds((TOK, ST)), sds((TOK, ST)), sds((TOK, LANES)), sds((GRP, ZW, ST))],
        [rows(ZW), rows(ST), rows(ST), rows(LANES), hspec], prefetch=at, after=(send2,), light=True,
    )
    hback = pl.BlockSpec((1, ZW, ST), lambda i, *_: (GRP - 1 - i, 0, 0))
    dpx, halo_x, *dbc, draw, g_head = call(
        back_kernel, "back", (GRP,),
        (after, dxi, dbi, dci, dcum, hall, xa, px, bb, cc, info, dy, hp, vecs),
        [whole((ZW, ST)), rows_back(ZW), rows_back(ST), rows_back(ST), rows_back(LANES), hback,
         rows_back(ZW), rows_back(ZW), rows_back(ST), rows_back(ST), rows_back(LANES),
         rows_back(ZW), whole((8, LANES)), whole((8, D))],
        [sds((TOK, ZW)), sds((8, ZW))] + [sds((TOK // 2, LANES), BF16)] * 4 + [sds((TOK, LANES), BF16), sds((8, LANES))],
        [rows_back(ZW), whole((8, ZW))] + [rows_back(LANES, HALF)] * 4 + [rows_back(LANES), whole((8, LANES))],
        scratch=[pltpu.VMEM((ZW, ST), F32)], flops=2 * TOK * 4 * ST * ZW, prefetch=at,
    )
    bc_got = [trade("head", b)(dbc[b]) for b in (1, 2, 3)]
    halo_x = moved(halo_x, -GRP)
    quarters = quarter_sum(keep2, send2, (draw,))
    mine1 = group_sum(grads1, SEG1, (draw,))

    def after_rows(width):
        last = TOK // 8 - 1
        return pl.BlockSpec((8, width), lambda i, *_: (jnp.minimum((i + 1) * (BLK // 8), last), 0))

    final = GRP * SEG2
    pb, acc = call(
        last_x_kernel, "last_x", (GRP,),
        (dpx, dpx, halo_x, mx, conv_params, dz, draw, nrm, w, wdt),
        [rows(ZW), after_rows(ZW), whole((8, ZW)), rows(ZW), whole((5, 1, 448)), rows(ZW), rows(LANES),
         rows(D), whole((2 * ZW, D)), whole((LANES, D))],
        [sds((TOK, D)), sds((final, D))], [rows(D), whole((final, D))],
        scratch=[pltpu.VMEM((BLK + 8, ZW), F32)], prefetch=at, flops=4 * TOK * D * 2 * ZW, after=(mine1,),
    )
    dpo, halo_o = call(
        edge_kernel, "edge", (GRP,), (dbc[0], *bc_got, po),
        [rows(LANES, HALF)] * 4 + [rows(2 * SW)],
        [sds((TOK, 2 * SW)), sds((8, 2 * SW))], [rows(2 * SW), whole((8, 2 * SW))], after=(acc,),
    )
    halo_o = moved(halo_o, -GRP)
    half_rows = pl.BlockSpec((1, HALF, D), lambda i, at: (i ^ at[0], 0, 0))
    keep_b, send_b, *grads2 = call(
        last_o_kernel, "last_o", (GRP,),
        (dpo, dpo, halo_o, mo, conv_params, nrm, w, pb, vecs, g_gate, g_head, acc),
        [rows(2 * SW), after_rows(2 * SW), whole((8, 2 * SW)), rows(2 * SW), whole((5, 1, 448)), rows(D),
         wblock(12, 2 * SW), rows(D), whole((8, D)), whole((8, ZW)), whole((8, LANES)), whole((final, D))],
        [sds((GRP, HALF, D), BF16)] * 2 + [sds((SEG2, D), BF16)] * 4,
        [half_rows] * 2 + [whole((SEG2, D))] * 4,
        scratch=[pltpu.VMEM((BLK + 8, 2 * SW), F32), pltpu.VMEM((final, D), F32)],
        prefetch=at, flops=4 * TOK * D * 2 * SW, after=(quarters[0],),
    )

    root = math.sqrt(TOK * lax.axis_size("seq"))
    mat = whole((ZW, D))
    turned3 = [turned(p) for p in (in_proj, in_proj_momentum, in_proj_average)]
    turned_shape = [sds((COLS, 1, D))] * 3
    buffers = [pltpu.VMEM((COLS, D), F32)] * 6 + [pltpu.SemaphoreType.DMA((5, 6))]
    keep3, send3 = split_sum(at, keep_b, send_b)
    total1 = across_groups(mine1, SEG1, (send3,))
    quarters_b = quarter_sum(keep3, send3, (total1,))
    mine2 = group_sum(grads2, SEG2, (quarters_b[0],))
    own_out = quarter_home(quarters, (mine2,))
    out_parts = all_home(own_out)
    own_grad = quarter_home(quarters_b, (own_out,))
    grad_parts = all_home(own_grad)
    total2 = across_groups(mine2, SEG2, (own_grad,))
    sums2 = all_quarters(total2)
    sums1 = all_quarters(total1)
    block_out, done_out = home(
        home_out_kernel, "home_out", at, (block_in,), (None,), out_parts, BF16, (total2,)
    )
    out_w, out_m, out_a, *in_half, done_a = call(
        functools.partial(update_a_kernel, rate=RATES[5] / root, rate_in=RATES[1] / root), "update_a", (1,),
        (*sums1, out_proj, out_proj_momentum, out_proj_average, *turned3),
        [whole((SEG1, D))] * 4 + [mat] * 3 + [anyspec] * 3, [sds((ZW, D))] * 3 + turned_shape,
        [mat] * 3 + [anyspec] * 3, scratch=[pltpu.VMEM((2 * ZW, D), F32)] + buffers, prefetch=at,
        after=(done_out,), vmem=32, token=True,
    )
    input_grad, done_grad = home(
        home_grad_kernel, "home_grad", at, (block_in, cotangent, vecs), (None, None, (8, D)),
        grad_parts, F32, (done_a,),
    )
    quarter = whole((SEG2, D))
    small, norm = call(
        small_kernel, "small", (1,), sums2, [quarter] * 4, [sds((SMALL, D)), sds((8, D))],
        [whole((SMALL, D)), whole((8, D))], prefetch=at, after=(done_grad,),
    )
    norms = [norm] + [trade("head", b)(norm) for b in (1, 2, 3)]
    *in_new, done_b = call(
        functools.partial(update_b_kernel, rate=RATES[1] / root), "update_b", (1,),
        (*sums2, *turned3, *in_half), [quarter] * 4 + [anyspec] * 6, turned_shape, [anyspec] * 3,
        scratch=[pltpu.VMEM((GRP * SEG2, D), F32)] + buffers, prefetch=at, aliases={8: 0, 9: 1, 10: 2},
        after=(norm,), vmem=24, token=True,
    )
    groups_of = (
        (norm_gain, norm_gain_momentum, norm_gain_average),
        (conv_params, conv_momentum, conv_average),
        (head_params, head_momentum, head_average),
        (gate_gain, gate_gain_momentum, gate_gain_average),
    )
    arrays = [a for three in groups_of for a in three]
    specs = [whole(a.shape) for a in arrays]
    new = call(
        functools.partial(update_small_kernel, rates=[r / root for r in RATES]), "update_small", (1,),
        (small, *norms, *arrays), [whole((SMALL, D))] + [whole((8, D))] * 4 + specs,
        [sds(a.shape) for a in arrays], specs, after=(done_b,),
    )
    ng3, cv3, hd3, gg3 = (tuple(new[3 * n : 3 * n + 3]) for n in range(4))
    in3 = tuple(turned(a) for a in in_new)
    return (block_out, input_grad, *ng3, *in3, *cv3, *hd3, *gg3, out_w, out_m, out_a)


def solution(mesh):
    act, vec, mat = P(None, "seq", None), P(), P(None, "head", None)
    weights = (vec, mat, mat, P(None, "head"), P("head"), P("head", None))
    outs = tuple(spec for spec in weights for _ in range(3))
    return jax.shard_map(
        shards,
        mesh=mesh,
        in_specs=(act, act, P(), *weights, *weights, *weights),
        out_specs=(act, act, *outs),
        check_vma=False,
    )
```

```python
import functools
import math

import jax
import jax.numpy as jnp
from jax import lax
from jax.experimental import pallas as pl
from jax.experimental.pallas import tpu as pltpu
from jax.sharding import PartitionSpec as P

HDIM = 64
CONV = 4
INNER = 1536
EPSILON = 1e-05
MOMENTUM = 0.5
AVERAGE = 0.5
RATES = (0.15, 0.1, 0.5, 0.05, 0.15, 0.02)
HIGHEST = lax.Precision.HIGHEST
F32 = jnp.float32
BF16 = jnp.bfloat16
VMEM = 14
GRP = 4
BLK = 256
HALF = BLK // 2
QUART = BLK // 4
D = 768
ZW = 384
NH = 6
ST = 128
SW = 32
LANES = 128
WCOLS = D // LANES
WROWS = 2 * ZW + 2 * SW
TOK = GRP * BLK
COLS = WROWS + NH
SEG1 = 2 * ZW // GRP
SEG2 = 120
BC_AT, DT_AT, TAP_AT, HD_AT, GG_AT, NG_AT = 384, 448, 456, 464, 472, 473


def nt(a, b, precision=None):
    return lax.dot_general(
        a, b, (((1,), (1,)), ((), ())), preferred_element_type=F32, precision=precision
    )


def nn(a, b, precision=None):
    return lax.dot_general(
        a, b, (((1,), (0,)), ((), ())), preferred_element_type=F32, precision=precision
    )


def tn(a, b, precision=None):
    return lax.dot_general(
        a, b, (((0,), (0,)), ((), ())), preferred_element_type=F32, precision=precision
    )


def iota(shape, dim):
    return lax.broadcasted_iota(jnp.int32, shape, dim)


def split3(value):
    high = value.astype(BF16).astype(F32)
    rest = value - high
    mid = rest.astype(BF16).astype(F32)
    return high, mid, rest - mid


def side_by_side(value, used):
    high, mid, low = split3(jnp.where(iota(value.shape, 1) < used, value, 0.0))
    return (high + pltpu.roll(mid, used, 1) + pltpu.roll(low, 2 * used, 1)).astype(BF16)


def widen(packed, kinds):
    lane, col = iota((LANES, ZW), 0), iota((LANES, ZW), 1)
    goals = [((lane % 32 == col // HDIM + 8 * k) & (lane < 96)).astype(BF16) for k in kinds]
    parts = side_by_side(packed, 32)
    return [nn(parts, goal) for goal in goals]


def head_sums(values):
    goal = (iota((ZW, LANES), 1) == iota((ZW, LANES), 0) // HDIM).astype(BF16)
    high = values.astype(BF16)
    return nn(high, goal) + nn((values - high.astype(F32)).astype(BF16), goal)


def running_sums(triangle, values):
    total = nn(triangle, side_by_side(values, 8))
    total = total + pltpu.roll(total, LANES - 8, 1) + pltpu.roll(total, LANES - 16, 1)
    return jnp.where(iota(total.shape, 1) < 8, total, 0.0)


def lane_mask(which):
    return (iota((1, LANES), 1) // HDIM == which).astype(BF16)


def triangle(lower):
    row, col = iota((BLK, BLK), 0), iota((BLK, BLK), 1)
    return (row >= col if lower else row <= col).astype(BF16)


def call(
    kernel, name, grid, ins, in_specs, outs, out_specs, scratch=(), prefetch=None, flops=0,
    aliases=None, after=(), vmem=VMEM, light=False, token=False,
):
    count = len(ins) + (prefetch is not None)
    results = len(outs)
    if grid == (GRP,) and name not in STREAMED:
        plain, pre, cuts = kernel, count - len(ins), list(in_specs) + list(out_specs)
        used = pre + len(cuts)

        def kernel(*refs):
            at = refs[:pre]
            for i in range(GRP):
                views = [part_of(r, c, i, at) for r, c in zip(refs[pre:used], cuts)]
                STEP.append(i)
                plain(*at, *views, *refs[used:])
                STEP.pop()

        grid = (1,)
        in_specs, out_specs = [whole(a.shape) for a in ins], [whole(a.shape) for a in outs]

    def body(*refs):
        rest = refs[count + len(after) :]
        if token:
            rest[results][...] = jnp.zeros((8, LANES), F32)
            rest = rest[:results] + rest[results + 1 :]
        kernel(*refs[:count], *rest)

    outs, out_specs = list(outs), list(out_specs)
    if token:
        outs.append(sds((8, LANES)))
        out_specs.append(whole((8, LANES)))
    nbytes = sum(math.prod(a.shape) * a.dtype.itemsize for a in (*ins, *outs))
    if light:
        flops, nbytes = 1024, 1024
    spec = pltpu.PrefetchScalarGridSpec(
        num_scalar_prefetch=0 if prefetch is None else 1,
        grid=grid,
        in_specs=list(in_specs) + [pl.BlockSpec(memory_space=pl.ANY)] * len(after),
        out_specs=out_specs,
        scratch_shapes=scratch,
    )
    return pl.pallas_call(
        body,
        grid_spec=spec,
        out_shape=outs,
        compiler_params=pltpu.CompilerParams(
            dimension_semantics=("arbitrary",) * len(grid), vmem_limit_bytes=vmem << 20
        ),
        cost_estimate=pl.CostEstimate(flops=flops, bytes_accessed=nbytes, transcendentals=0),
        input_output_aliases=aliases or {},
        name=name,
    )(*(() if prefetch is None else (prefetch,)), *ins, *after)


STEP = []
STREAMED = ("home_out", "home_grad", "split", "gate", "inner", "edge", "last_x", "local", "back", )


def step_now():
    return STEP[-1] if STEP else pl.program_id(0)


def when(condition):
    if isinstance(condition, bool):
        return lambda body: body() if condition else None
    return pl.when(condition)


def part_of(ref, spec, i, at):
    size = spec.block_shape
    if size is None or tuple(size) == tuple(ref.shape):
        return ref
    cut = []
    for n, length, full in zip(spec.index_map(i, *at), size, ref.shape):
        if length == full:
            cut.append(slice(None))
        elif isinstance(n, int):
            cut.append(pl.ds(n * length, length))
        else:
            cut.append(pl.ds(pl.multiple_of(n * length, length), length))
    return ref.at[tuple(cut)]


def sds(shape, dtype=F32):
    return jax.ShapeDtypeStruct(shape, dtype)


def whole(shape):
    return pl.BlockSpec(shape, lambda *_: (0,) * len(shape))


def rows(width, height=BLK):
    return pl.BlockSpec((height, width), lambda i, *_: (i, 0))


def rows_back(width, height=BLK):
    return pl.BlockSpec((height, width), lambda i, *_: (GRP - 1 - i, 0))


def slot(height, width=D):
    return pl.BlockSpec((1, height, width), lambda i, at: (i ^ at[0], 0, 0))


def pick_kernel(at, *refs):
    for n, goal in enumerate(refs[2 * GRP :]):
        goal[0:HALF, :] = refs[n][0]
        if goal.shape[0] > HALF:
            goal[HALF:, :] = refs[GRP + n][0]


def pick(at, array, edge, after=()):
    def half_of(b):
        return pl.BlockSpec((1, HALF, D), lambda i, at: (at[0] ^ b, at[1], 0))

    def edge_of(b):
        return pl.BlockSpec((1, 16, D), lambda i, at: (at[0] ^ b, BLK // 16 - 1, 0))

    size = HALF + 16 * edge
    specs = [half_of(b) for b in range(GRP)] + [edge_of(b) for b in range(GRP)]
    return call(
        pick_kernel, "pick", (1,), (array,) * (2 * GRP), specs,
        [sds((size, D), BF16)] * GRP, [whole((size, D))] * GRP, prefetch=at, after=after,
    )


def stack_kernel(at, r0, r1, r2, r3, out_ref, *edge):
    refs = (r0, r1, r2, r3)
    for b, ref in enumerate(refs):
        out_ref[b] = ref[0:HALF, :]
    for goal in edge:
        for b, ref in enumerate(refs):

            @when(at[0] ^ b == GRP - 1)
            def _():
                goal[...] = ref[HALF:, :]


def stack(at, parts, after=()):
    size = parts[0].shape[0]
    outs, specs = [sds((GRP, HALF, D), BF16)], [whole((GRP, HALF, D))]
    if size > HALF:
        outs, specs = outs + [sds((16, D), BF16)], specs + [whole((16, D))]
    return call(
        stack_kernel, "stack", (1,), parts, [whole((size, D))] * GRP, outs, specs, prefetch=at, after=after
    )


def prep_kernel(
    win, wout, taps, heads, ng, gg,
    w_ref, wdt_ref, low_ref, send_ref, hp_ref, vec_ref, wide_w, scr, sem,
):
    copy = pltpu.make_async_copy(win.at[:, 0, :], wide_w, sem)
    copy.start()
    low_ref[...] = wout[...].astype(BF16)
    scr[...] = jnp.zeros_like(scr)
    scr[0:3, 0:NH] = heads[...]
    lanes = scr[...]
    for by in (8, 16, 32, 64):
        lanes = lanes + pltpu.roll(lanes, by, 1)
    hp_ref[...] = lanes
    vec_ref[...] = jnp.zeros_like(vec_ref)
    vec_ref[0:1, :] = ng[...].reshape(1, D)
    vec_ref[1:2, 0:ZW] = gg[...].reshape(1, ZW)
    vec_ref[2:3, 0:ZW] = widen(lanes, (0,))[0][2:3, :]
    copy.wait()
    w_ref[...] = wide_w[0:WROWS, :].astype(BF16)
    last = jnp.concatenate([wide_w[WROWS:, :], jnp.zeros((8 - NH, D), F32)], axis=0)
    wdt_ref[...] = jnp.concatenate([last] * 16, axis=0).astype(BF16)
    send_ref[0 : 2 * SW, :] = w_ref[2 * ZW : WROWS, :]
    own = taps[:, 0, :][:, ZW:]
    high = own.astype(BF16).astype(F32)
    mid = (own - high).astype(BF16).astype(F32)
    low = own - high - mid
    parts = jnp.concatenate([high, mid, low, jnp.zeros((1, 2 * SW), F32)], axis=0)
    send_ref[2 * SW :, :] = jnp.zeros((16, D), BF16)
    send_ref[2 * SW :, 0 : 2 * SW] = parts.astype(BF16)


def chunk_of(own_ref, oth_ref, core):
    own, oth = own_ref[0], oth_ref[0]
    first = core == 0
    return jnp.concatenate([jnp.where(first, own, oth), jnp.where(first, oth, own)], axis=0)


def normalise(x, gain):
    u = x.astype(F32)
    scale = lax.rsqrt(jnp.mean(u * u, axis=-1, keepdims=True) + EPSILON)
    return (u * scale * gain).astype(BF16)


def first_kernel(at, own, oth, vecs, wz, wdt, hp, nrm_ref, z_ref, info_ref, row_ref, tot_ref, cum):
    step = step_now()

    @when(step == 0)
    def _():
        cum[...] = jnp.zeros_like(cum)

    normed = normalise(chunk_of(own, oth, at[1]), vecs[0:1, :])
    nrm_ref[...] = normed
    z_ref[...] = nt(normed, wz[...])
    biased = nt(normed, wdt[...]) + hp[0:1, :]
    steps = jax.nn.softplus(biased)
    decays = -jnp.exp(hp[1:2, :]) * steps
    c = running_sums(triangle(True), decays)
    group = iota((BLK, LANES), 1) // 8
    info = jnp.where(group == 0, c, jnp.where(group == 1, steps, biased))
    moved_c = pltpu.roll(c, 24, 1) + cum[0:1, :]
    info_ref[...] = jnp.where(group == 3, moved_c, info)
    row_ref[...] = jnp.transpose(c)[0:8, :]
    cum[0:1, :] = moved_c[BLK - 1 : BLK, :]
    tot_ref[...] = jnp.broadcast_to(cum[0:1, :], (8, LANES))


def mix_kernel(
    at, nrm, halo, vecs, wx, wo, bc0, bc1, bc2, bc3, taps, info,
    mx_ref, px_ref, xa_ref, xdt_ref, mo_ref, po_ref, b_ref, c_ref, h_ref, s_ref,
    wbc, tbc, ext, exto, state,
):
    step = step_now()
    tap = taps[:, 0, :]

    @when(step == 0)
    def _():
        place = jnp.zeros((16, 2 * ST), F32)
        for b, buf in enumerate((bc0, bc1, bc2, bc3)):
            wbc[SW * b : SW * (b + 1), :] = buf[0:SW, :]
            wbc[ST + SW * b : ST + SW * (b + 1), :] = buf[SW : 2 * SW, :]
            at_row, at_col = iota((2 * SW, 2 * ST), 0), iota((2 * SW, 2 * ST), 1)
            goal = jnp.where(at_row < SW, SW * b + at_row, ST + SW * b + at_row - SW)
            put = (at_col == goal).astype(BF16)
            place = place + nn(buf[2 * SW :, 0 : 2 * SW], put)
        tbc[0:5, :] = place[0:5] + place[5:10] + place[10:15]
        before = normalise(jnp.where(at[5] > 0, halo[...], 0.0).astype(BF16), vecs[0:1, :])
        ext[0:8, 0:ZW] = nt(before, wx[...])[8:16]
        ext[0:8, ZW:] = nt(before, wbc[...])[8:16]
        exto[0:8, :] = nt(before, wo[...])[8:16]
        state[...] = jnp.zeros_like(state)

    normed = nrm[...]
    mixed = nt(normed, wx[...])
    mx_ref[...] = mixed
    ext[8:, 0:ZW] = mixed
    ext[8:, ZW:] = nt(normed, wbc[...])
    own = nt(normed, wo[...])
    mo_ref[...] = own
    exto[8:, :] = own
    pre = tap[4:5, 0:ZW]
    pre_bc = tbc[4:5, :]
    pre_o = tap[4:5, ZW:]
    for k in range(CONV):
        pre = pre + tap[k : k + 1, 0:ZW] * ext[5 + k : 5 + k + BLK, 0:ZW]
        pre_bc = pre_bc + tbc[k : k + 1, :] * ext[5 + k : 5 + k + BLK, ZW:]
        pre_o = pre_o + tap[k : k + 1, ZW:] * exto[5 + k : 5 + k + BLK, :]
    px_ref[...] = pre
    po_ref[...] = pre_o
    x = pre * jax.nn.sigmoid(pre)
    xa_ref[...] = x
    bc = (pre_bc * jax.nn.sigmoid(pre_bc)).astype(BF16)
    b_ref[...] = bc[:, 0:ST]
    c_ref[...] = bc[:, ST:]
    ext[0:8, :] = ext[BLK:, :]
    exto[0:8, :] = exto[BLK:, :]

    packed = info[...]
    c = packed[:, 0:LANES]
    keep = iota((BLK, LANES), 1) < 8
    tail = jnp.where(keep, jnp.exp(jnp.where(keep, c[BLK - 1 : BLK, :] - c, 0.0)), 0.0)
    tail_wide, dt_wide = widen(jnp.where(keep, tail, packed), (0, 1))
    xdt = x * dt_wide
    xdt_ref[...] = xdt.astype(BF16)
    fresh = tn((xdt * tail_wide).astype(BF16), bc[:, 0:ST])
    h_ref[0] = state[...]
    for h in range(NH):
        decay = jnp.exp(packed[BLK - 1 : BLK, h : h + 1])
        at = pl.ds(HDIM * h, HDIM)
        state[at, :] = decay * state[at, :] + fresh[HDIM * h : HDIM * (h + 1), :]
    s_ref[...] = state[...].astype(BF16)


def weights_of(h, packed, row, causal):
    diff = packed[:, h : h + 1] - row[h : h + 1, :]
    return jnp.where(causal, jnp.exp(jnp.where(causal, diff, 0.0)), 0.0)


def local_kernel(
    at, xdt, xa, b, c, info, row, hloc, own, oth, low, vecs, yl_ref, dyn_ref, w_ref
):
    step = step_now()
    packed = info[...]
    rowc = row[...]
    causal = iota((BLK, BLK), 0) >= iota((BLK, BLK), 1)
    scores = nt(c[...], b[...])
    c_exp = jnp.exp(jnp.where(iota((BLK, LANES), 1) < 8, packed, 0.0))
    carried = nt(c[...], hloc[0].astype(BF16)) * widen(c_exp, (0,))[0]
    carried = carried + vecs[2:3, 0:ZW] * xa[...]
    for p in range(NH // 2):
        x = xdt[:, LANES * p : LANES * (p + 1)]
        total = carried[:, LANES * p : LANES * (p + 1)]
        for q in range(2):
            weights = (weights_of(2 * p + q, packed, rowc, causal) * scores).astype(BF16)
            total = total + nn(weights, x * lane_mask(q))
        yl_ref[:, LANES * p : LANES * (p + 1)] = total
    place = (at[2] * GRP + step) * BLK + iota((BLK, 1), 0)
    live = place < at[7 + at[0]]
    w = jnp.where(live, chunk_of(own, oth, at[1]), 0.0).astype(BF16)
    w_ref[...] = w
    dyn_ref[...] = nt(w, low[...])


def gate_kernel(at, yl, c, info, hin, z, dyn, vecs, y_ref, sum_ref):
    packed = info[...]
    lane = iota((BLK, LANES), 1)
    cum = jnp.where(lane // 8 == 3, jnp.exp(jnp.where(lane // 8 == 3, packed, 0.0)), 0.0)
    entering = jnp.where(at[5] > 0, hin[...], 0.0).astype(BF16)
    y = yl[...] + nt(c[...], entering) * widen(cum, (3,))[0]
    y_ref[...] = y
    gate = z[...]
    g = y * (gate * jax.nn.sigmoid(gate))
    squares = jnp.sum(g * g, axis=-1, keepdims=True)
    inner = jnp.sum(dyn[...] * vecs[1:2, 0:ZW] * g, axis=-1, keepdims=True)
    both = jnp.where(lane == 0, squares, jnp.where(lane == 1, inner, 0.0))
    sum_ref[...] = jnp.transpose(both)[0:8, :]


def ungate_kernel(
    at, y, z, dyn, s0, s1, s2, s3, info, c, vecs, low,
    dy_ref, dz_ref, yn_ref, p_ref, gg_ref, keep_ref, send_ref, acc,
):
    step = step_now()

    @when(step == 0)
    def _():
        acc[...] = jnp.zeros_like(acc)
        gg_ref[...] = jnp.zeros_like(gg_ref)

    sums = s0[...] + s1[...] + s2[...] + s3[...]
    sums = jnp.transpose(jnp.concatenate([sums, jnp.zeros((LANES - 8, BLK), F32)], axis=0))
    q = lax.rsqrt(sums[:, 0:1] / INNER + EPSILON)
    mean = sums[:, 1:2] * q / INNER
    gate = z[...]
    sigma = jax.nn.sigmoid(gate)
    silu = gate * sigma
    out = y[...]
    g = out * silu
    n = g * q
    d = dyn[...]
    gg = vecs[1:2, 0:ZW]
    d_g = q * (d * gg - n * mean)
    d_y = d_g * silu
    dy_ref[...] = d_y
    dz_ref[...] = (d_g * out * sigma * (1.0 + gate * (1.0 - sigma))).astype(BF16)
    yn = (n * gg).astype(BF16)
    yn_ref[...] = yn
    halves(nn(yn, low[...]).astype(BF16), at[1], keep_ref, send_ref)
    gg_ref[0:1, :] += jnp.sum(d * n, axis=0, keepdims=True)
    packed = info[...]
    lane = iota((BLK, LANES), 1)
    cum = jnp.where(lane // 8 == 3, jnp.exp(jnp.where(lane // 8 == 3, packed, 0.0)), 0.0)
    acc[...] += tn((d_y * widen(cum, (3,))[0]).astype(BF16), c[...])
    p_ref[...] = acc[...].astype(BF16)


def halves(value, core, keep_ref, send_ref):
    low, high = value[0:HALF], value[HALF:]
    first = core == 0
    keep_ref[0] = jnp.where(first, low, high)
    send_ref[0] = jnp.where(first, high, low)


def out_kernel(
    at, yn, w, nrm, dz, g0, g1, g2, g3, acc
):
    step = step_now()

    @when(step == 0)
    def _():
        acc[...] = jnp.zeros_like(acc)

    acc[0:ZW, :] += tn(dz[...], nrm[...])
    acc[ZW:, :] += tn(yn[...], w[...])

    @when(step == GRP - 1)
    def _():
        for b, ref in enumerate((g0, g1, g2, g3)):
            start = pl.multiple_of((at[0] ^ b) * SEG1, SEG1)
            ref[...] = acc[pl.ds(start, SEG1), :].astype(BF16)


def inner_kernel(
    at, xdt, b, c, info, row, dy, hloc, hin, dxi_ref, dbi_ref, dci_ref, dcum_ref, hall_ref
):
    packed = info[...]
    rowc = row[...]
    lane = iota((BLK, LANES), 1)
    causal = iota((BLK, BLK), 0) >= iota((BLK, BLK), 1)
    bb, cc = b[...], c[...]
    scores = nt(cc, bb)
    d_scores = jnp.zeros((BLK, BLK), F32)
    d_cum = jnp.zeros((BLK, LANES), F32)
    columns = []
    dyv = dy[...]
    for p in range(NH // 2):
        x = xdt[:, LANES * p : LANES * (p + 1)]
        d = dyv[:, LANES * p : LANES * (p + 1)].astype(BF16)
        total = jnp.zeros((BLK, LANES), F32)
        for q in range(2):
            h = 2 * p + q
            spans = weights_of(h, packed, rowc, causal)
            d_h = d * lane_mask(q)
            d_spans = nt(d_h, x) * spans
            d_scores = d_scores + d_spans
            both = d_spans * scores
            d_cum = d_cum + jnp.where(lane == h, jnp.sum(both, axis=1, keepdims=True), 0.0)
            columns.append(jnp.sum(both, axis=0, keepdims=True))
            total = total + tn((spans * scores).astype(BF16), d_h)
        dxi_ref[:, LANES * p : LANES * (p + 1)] = total
    columns = jnp.concatenate(columns + [jnp.zeros((LANES - NH, BLK), F32)], axis=0)
    d_cum = d_cum - jnp.transpose(columns)
    low_scores = d_scores.astype(BF16)
    c_exp = jnp.exp(jnp.where(lane < 8, packed, 0.0))
    c_wide = widen(c_exp, (0,))[0]
    base = packed[0:1, 24:32] - packed[0:1, 0:8]
    for h in range(NH):
        here = pl.ds(HDIM * h, HDIM)
        grown = jnp.exp(base[:, h : h + 1]) * hin[here, :].astype(F32)
        grown = jnp.where(at[5] > 0, grown, 0.0)
        hall_ref[0, here, :] = hloc[0, here, :] + grown
    entering = hall_ref[0].astype(BF16)
    carried = nt(cc, entering) * c_wide
    d_cum = d_cum + head_sums(dyv * carried)
    dcum_ref[...] = d_cum
    dci_ref[...] = nn(low_scores, bb) + nn((dyv * c_wide).astype(BF16), entering)
    dbi_ref[...] = tn(low_scores, cc)


def back_kernel(
    at, after, dxi, dbi, dci, dcum, hall, xa, px, b, c, info, dy, hp, vecs,
    dpx_ref, halo_ref, o0, o1, o2, o3, draw_ref, hg_ref, state,
):
    step = step_now()

    @when(step == 0)
    def _():
        state[...] = jnp.where(at[6] > 0, after[...].astype(F32), 0.0)
        hg_ref[...] = jnp.zeros_like(hg_ref)

    packed = info[...]
    lane = iota((BLK, LANES), 1)
    first = lane < 8
    c_last = packed[BLK - 1 : BLK, :]
    tail = jnp.where(first, jnp.exp(jnp.where(first, c_last - packed, 0.0)), 0.0)
    c_exp = jnp.where(first, jnp.exp(jnp.where(first, packed, 0.0)), 0.0)
    mixed = jnp.where(first, tail, jnp.where(lane < 16, packed, pltpu.roll(c_exp, 16, 1)))
    tail_wide, dt_wide, c_wide = widen(mixed, (0, 1, 2))
    x = xa[...]
    xdt = x * dt_wide
    d_y = dy[...]
    bb, cc = b[...], c[...]
    low_state = state[...].astype(BF16)
    d_tail = nt(bb, low_state) * tail_wide
    tails = head_sums(xdt * d_tail)
    d_xdt = dxi[...] + d_tail
    d_b = dbi[...] + nn((xdt * tail_wide).astype(BF16), low_state)
    d_c = dci[...]
    ending = jnp.sum(tails, axis=0, keepdims=True)
    lane1 = iota((1, LANES), 1)
    for h in range(NH):
        here = pl.ds(HDIM * h, HDIM)
        inner = jnp.sum(state[here, :] * hall[0, here, :], axis=(0, 1), keepdims=True)
        ending = ending + jnp.where(lane1 == h, inner * jnp.exp(c_last[:, h : h + 1]), 0.0)
    d_cum = dcum[...] - tails
    d_cum = d_cum + jnp.where(iota((BLK, LANES), 0) == BLK - 1, ending, 0.0)
    d_a = running_sums(triangle(False), d_cum)
    fresh = tn((d_y * c_wide).astype(BF16), cc)
    for h in range(NH):
        here = pl.ds(HDIM * h, HDIM)
        decay = jnp.exp(c_last[:, h : h + 1])
        state[here, :] = decay * state[here, :] + fresh[HDIM * h : HDIM * (h + 1), :]
    rate = -jnp.exp(hp[1:2, :])
    d_dt = head_sums(x * d_xdt) + rate * d_a
    biased = pltpu.roll(packed, LANES - 16, 1)
    steps = pltpu.roll(packed, LANES - 8, 1)
    used = lane < NH
    d_raw = jnp.where(used, d_dt * jax.nn.sigmoid(jnp.where(used, biased, 0.0)), 0.0)
    draw_ref[...] = d_raw.astype(BF16)
    hg_ref[0:1, :] += jnp.sum(d_raw, axis=0, keepdims=True)
    g_rate = jnp.where(used, d_a * rate * jnp.where(used, steps, 0.0), 0.0)
    hg_ref[1:2, :] += jnp.sum(g_rate, axis=0, keepdims=True)
    hg_ref[2:3, :] += jnp.sum(head_sums(d_y * x), axis=0, keepdims=True)
    d_x = d_xdt * dt_wide + vecs[2:3, 0:ZW] * d_y
    pre = px[...]
    sigma = jax.nn.sigmoid(pre)
    d_pre = d_x * sigma * (1.0 + pre * (1.0 - sigma))
    dpx_ref[...] = d_pre
    halo_ref[...] = d_pre[0:8]
    for s, ref in enumerate((o0, o1, o2, o3)):
        for n, value in enumerate((d_b, d_c)):
            mine = value[:, SW * s : SW * (s + 1)].astype(BF16)
            ref[:, SW * n : SW * (n + 1)] = mine[0:HALF]
            ref[:, SW * (n + 2) : SW * (n + 3)] = mine[HALF:]


def edge_kernel(o0, r1, r2, r3, po, halo_x, dpo_ref, halo_ref):
    d = o0[...].astype(F32) + r1[...].astype(F32) + r2[...].astype(F32) + r3[...].astype(F32)
    d = jnp.concatenate([d[:, 0 : 2 * SW], d[:, 2 * SW :]], axis=0)
    pre = po[...]
    sigma = jax.nn.sigmoid(pre)
    d = d * sigma * (1.0 + pre * (1.0 - sigma))
    dpo_ref[...] = d

    @when(step_now() == 0)
    def _():
        halo_ref[:, X_LANES] = halo_x[...]
        halo_ref[:, ZW:] = jnp.zeros((8, LANES), F32)
        halo_ref[:, O_LANES] = d[0:8]


def unconvolve(acc, ext, d_pre, follows, values, tap, lanes):
    ext[0:BLK, :] = d_pre
    ext[BLK:, :] = follows
    total = jnp.zeros(d_pre.shape, F32)
    for k in range(CONV):
        shifted = ext[3 - k : 3 - k + BLK, :]
        total = total + tap[k : k + 1, lanes] * shifted
        acc[TAP_AT + k : TAP_AT + k + 1, lanes] += jnp.sum(values * shifted, axis=0, keepdims=True)
    acc[TAP_AT + CONV : TAP_AT + CONV + 1, lanes] += jnp.sum(d_pre, axis=0, keepdims=True)
    return total


X_LANES, O_LANES = slice(0, ZW), slice(ZW, ZW + 2 * SW)


END = 16


def last_x_kernel(
    at, dpx, nx, mx, taps, dz, draw, nrm, w, wdt, pb_ref, end_ref, acc, ext
):
    step = step_now()

    @when(step == 0)
    def _():
        acc[...] = jnp.zeros_like(acc)

    follows = jnp.where(step < GRP - 1, nx[...], 0.0)
    d_mx = unconvolve(acc, ext, dpx[...], follows, mx[...], taps[:, 0, :], X_LANES)
    end_ref[...] = d_mx[BLK - END :, :]
    late = (step == GRP - 1) & (iota((BLK, 1), 0) >= BLK - END)
    p_x = jnp.where(late, 0.0, d_mx).astype(BF16)
    p_t = draw[...]
    pb_ref[...] = nn(dz[...], w[0:ZW, :]) + nn(p_x, w[ZW:, :]) + nn(p_t, wdt[...])
    normed = nrm[...]
    acc[0:ZW, :] += tn(p_x, normed)
    acc[DT_AT : DT_AT + 8, :] += tn(p_t, normed)[0:8]


def last_o_kernel(
    at, dpo, no, halo, mo, taps, nrm, w, wx, pb, vecs, gg, hg, acc_in, end, mxe,
    keep_ref, send_ref, g0, g1, g2, g3, ext, acc, wide_pb,
):
    step = step_now()

    @when(step == 0)
    def _():
        acc[...] = acc_in[...]
        acc[HD_AT : HD_AT + 8, 0:LANES] = hg[...]
        acc[GG_AT : GG_AT + 1, 0:ZW] = gg[0:1, :]

    after = jnp.where(at[6] > 0, halo[...], 0.0)
    follows = jnp.where(step < GRP - 1, no[...], after[:, O_LANES])
    p_o = unconvolve(acc, ext, dpo[...], follows, mo[...], taps[:, 0, :], O_LANES).astype(BF16)
    wide_pb[...] = pb[...] + nn(p_o, w[...])
    normed = nrm[...]

    @when(step == GRP - 1)
    def _():
        rows_after = jnp.concatenate([jnp.zeros((END, ZW), F32), after[:, X_LANES]], axis=0)
        total = end[...]
        for k in range(CONV):
            shifted = rows_after[3 - k : 3 - k + END, :]
            total = total + taps[k : k + 1, 0, X_LANES] * shifted
            grad = jnp.sum(mxe[...] * shifted, axis=0, keepdims=True)
            acc[TAP_AT + k : TAP_AT + k + 1, X_LANES] += grad
        p_x = total.astype(BF16)
        wide_pb[BLK - END :, :] += nn(p_x, wx[...])
        acc[0:ZW, :] += tn(p_x, normed[BLK - END :, :])

    back = wide_pb[...]
    halves(back.astype(BF16), at[1], keep_ref, send_ref)
    acc[NG_AT : NG_AT + 1, :] += jnp.sum(back * normed.astype(F32), axis=0, keepdims=True)
    acc[BC_AT:DT_AT, :] += tn(p_o, normed)

    @when(step == GRP - 1)
    def _():
        acc[NG_AT : NG_AT + 1, :] = acc[NG_AT : NG_AT + 1, :] / vecs[0:1, :]
        for b, ref in enumerate((g0, g1, g2, g3)):
            start = pl.multiple_of((at[0] ^ b) * SEG2, 8)
            ref[...] = acc[pl.ds(start, SEG2), :].astype(BF16)


def split_kernel(at, keep, other, keep_ref, send_ref):
    value = keep[0].astype(F32) + other[0].astype(F32)
    low, high = value[0:QUART], value[QUART:]
    first = at[4] == 0
    keep_ref[0] = jnp.where(first, low, high)
    send_ref[0] = jnp.where(first, high, low).astype(BF16)


def add_kernel(keep, other, r0, r1, r2, r3):
    for b, ref in enumerate((r0, r1, r2, r3)):
        ref[...] = (keep[b] + other[b].astype(F32)).astype(BF16)


def sum_kernel(*refs):
    total = refs[0][...].astype(F32)
    for ref in refs[1:-1]:
        total = total + ref[...].astype(F32)
    refs[-1][...] = total.astype(refs[-1].dtype)


def place_quarters(at, b, parts, scr):
    core, xbit = at[1], at[4]
    for n, ref in enumerate(parts):
        half = core if n < 2 else 1 - core
        quarter = xbit if n % 2 == 0 else 1 - xbit
        start = pl.multiple_of(half * HALF + quarter * QUART, QUART)
        scr[pl.ds(start, QUART), :] = ref[0]


def home_out_kernel(at, block, a, x, ac, xc, out_ref, scr):
    step = step_now()
    place_quarters(at, step, (a, x, ac, xc), scr)
    place = (at[2] * GRP + at[0]) * BLK + iota((BLK, 1), 0)
    live = place < at[7 + step]
    total = block[0].astype(F32) + scr[...].astype(F32)
    out_ref[0] = jnp.where(live, total, 0.0).astype(BF16)


def home_grad_kernel(at, block, cot, vecs, a, x, ac, xc, out_ref, scr):
    step = step_now()
    place_quarters(at, step, (a, x, ac, xc), scr)
    place = (at[2] * GRP + at[0]) * BLK + iota((BLK, 1), 0)
    live = place < at[7 + step]
    u = block[0].astype(F32)
    scale = lax.rsqrt(jnp.mean(u * u, axis=-1, keepdims=True) + EPSILON)
    m = u * scale
    f = scr[...].astype(F32) * vecs[0:1, :]
    inner = jnp.mean(f * m, axis=-1, keepdims=True)
    out_ref[0] = scale * (f - m * inner) + jnp.where(live, cot[0].astype(F32), 0.0)


def home(kernel, name, at, arrays, specs, parts, dtype, after=()):
    full = pl.BlockSpec((1, BLK, D), lambda i, *_: (i, 0, 0))
    part = pl.BlockSpec((1, QUART, D), lambda i, at: (i ^ at[0], 0, 0))
    specs = [full if s is None else whole(s) for s in specs]
    return call(
        kernel, name, (GRP,), (*arrays, *parts), specs + [part] * 4, [sds((GRP, BLK, D), dtype)],
        [full], scratch=[pltpu.VMEM((BLK, D), BF16)], prefetch=at, after=after, token=True,
    )


def advance(weight, gradient, moment, average, rate):
    moment_new = MOMENTUM * moment + gradient
    weight_new = weight - rate * (gradient + MOMENTUM * moment_new)
    average_new = AVERAGE * average + (1.0 - AVERAGE) * weight_new
    return (weight_new, moment_new, average_new)


def stepped(grad_of, weights, outs, blocks, buffers, sems, rate):
    ins, done = buffers[:3], buffers[3:]

    def reads(n):
        start, size = blocks[n]
        return [
            pltpu.make_async_copy(
                w.at[pl.ds(start, size), 0, :], buf.at[pl.ds(start, size), :], sems.at[n, j]
            )
            for j, (w, buf) in enumerate(zip(weights, ins))
        ]

    def writes(n):
        start, size = blocks[n]
        return [
            pltpu.make_async_copy(
                buf.at[pl.ds(start, size), :], o.at[pl.ds(start, size), 0, :], sems.at[n, 3 + j]
            )
            for j, (o, buf) in enumerate(zip(outs, done))
        ]

    for n in range(len(blocks)):
        for copy in reads(n):
            copy.start()
    for n, (start, size) in enumerate(blocks):
        for copy in reads(n):
            copy.wait()
        here = pl.ds(start, size)
        new = advance(ins[0][here, :], grad_of(n), ins[1][here, :], ins[2][here, :], rate)
        for buf, value in zip(done, new):
            buf[here, :] = value
        for copy in writes(n):
            copy.start()
    for n in range(len(blocks)):
        for copy in writes(n):
            copy.wait()


Z_BLOCKS = tuple((96 * n, 96) for n in range(4))
X_BLOCKS = tuple((ZW + 96 * n, 96) for n in range(4)) + ((2 * ZW, COLS - 2 * ZW),)


def update_a_kernel(
    at, g0, g1, g2, g3, w, m, a, wi, mi, ai, x0, x1, x2, w_ref, m_ref, a_ref, wo, mo, ao,
    grad, b0, b1, b2, b3, b4, b5, sems, *, rate, rate_in,
):
    for b, ref in enumerate((g0, g1, g2, g3)):
        grad[pl.ds(pl.multiple_of((at[0] ^ b) * SEG1, SEG1), SEG1), :] = ref[0:SEG1, :].astype(F32)
    stepped(
        lambda n: grad[96 * n : 96 * (n + 1), :], (wi, mi, ai), (wo, mo, ao), Z_BLOCKS,
        (b0, b1, b2, b3, b4, b5), sems, rate_in,
    )
    w_ref[...], m_ref[...], a_ref[...] = advance(w[...], grad[ZW:, :], m[...], a[...], rate)


def update_b_kernel(
    at, g0, g1, g2, g3, wi, mi, ai, wo, mo, ao,
    grad, b0, b1, b2, b3, b4, b5, sems, *, rate,
):
    for b, ref in enumerate((g0, g1, g2, g3)):
        start = pl.multiple_of((at[0] ^ b) * SEG2, 8)
        grad[pl.ds(start, SEG2), :] = ref[...].astype(F32)
    stepped(
        lambda n: grad[96 * n : min(96 * (n + 1), COLS - ZW), :], (wi, mi, ai), (wo, mo, ao), X_BLOCKS,
        (b0, b1, b2, b3, b4, b5), sems, rate,
    )


SMALL = GRP * SEG2 - TAP_AT


def small_kernel(at, g0, g1, g2, g3, small_ref, norm_ref):
    for b, ref in enumerate((g0, g1, g2, g3)):

        @when(at[0] ^ b == GRP - 1)
        def _():
            small_ref[...] = ref[SEG2 - SMALL :, :].astype(F32)
            norm_ref[...] = ref[SEG2 - 8 :, :].astype(F32)


def add_small_kernel(a, b, out_ref):
    out_ref[...] = a[...] + b[...]


def update_small_kernel(
    small, n0, n1, ng, ngm, nga, cv, cvm, cva, hd, hdm, hda, gg, ggm, gga, *outs, rates
):
    ng_o, cv_o, hd_o, gg_o = (outs[3 * n : 3 * n + 3] for n in range(4))
    at_norm = NG_AT - TAP_AT - (SMALL - 8)
    norms = [n[at_norm : at_norm + 1, :] for n in (n0, n1)]
    grad = (norms[0] + norms[1]).reshape(D)
    for ref, new in zip(ng_o, advance(ng[...], grad, ngm[...], nga[...], rates[0])):
        ref[...] = new
    grad = small[0:5, 0 : ZW + 2 * SW]
    old = [a[:, 0, :] for a in (cv, cvm, cva)]
    for ref, new in zip(cv_o, advance(old[0], grad, old[1], old[2], rates[2])):
        ref[:, 0, :] = new
    at_head = HD_AT - TAP_AT
    grad = small[at_head : at_head + 3, 0:NH]
    for ref, new in zip(hd_o, advance(hd[...], grad, hdm[...], hda[...], rates[3])):
        ref[...] = new
    at_gate = GG_AT - TAP_AT
    grad = small[at_gate : at_gate + 1, 0:ZW].reshape(ZW)
    for ref, new in zip(gg_o, advance(gg[...], grad, ggm[...], gga[...], rates[4])):
        ref[...] = new


def trade(axis, flip):
    count = lax.axis_size(axis)
    pairs = [(i, i ^ flip) for i in range(count)]
    return lambda array: lax.ppermute(array, axis, pairs)


def moved(array, by):
    count = lax.axis_size("seq")
    if count == 2 * abs(by):
        return trade("seq", abs(by))(array)
    pairs = [(i, i + by) for i in range(count) if 0 <= i + by < count]
    return lax.ppermute(array, "seq", pairs)


def grow(decay, state):
    return jnp.repeat(decay[0, 24 : 24 + NH], HDIM)[:, None] * state


def pieces_before(state, logs, way):
    count = lax.axis_size("seq") // GRP
    found = moved(state, way * GRP)
    by = 1
    if count > 2:
        there = lax.axis_index("seq") // GRP
        decay = moved(jnp.exp(logs), way * GRP)
        total = found.astype(F32)
        while by < count - 1:
            inside = (there >= by) if way > 0 else (there + by < count)
            earlier = moved(total.astype(BF16), way * GRP * by).astype(F32)
            total = jnp.where(inside, grow(decay, earlier) + total, total)
            decay = decay * moved(decay, way * GRP * by)
            by *= 2
        found = total.astype(BF16)
    return found


def group_sum(parts, height, after=()):
    return add_rows(height, [parts[0]] + [trade("seq", b)(parts[b]) for b in (1, 2, 3)], after)


def add_rows(height, arrays, after=()):
    spec = whole((height, D))
    out = [sds((height, D), BF16)]
    return call(sum_kernel, "sum", (1,), arrays, [spec] * len(arrays), out, [spec], after=after)[0]


def across_groups(mine, height, after=()):
    by = GRP
    while by < lax.axis_size("seq"):
        mine = add_rows(height, [mine, trade("seq", by)(mine)], after)
        by *= 2
    return mine


def all_quarters(mine):
    return [mine] + [trade("seq", b)(mine) for b in (1, 2, 3)]


def slot_of(height):
    return pl.BlockSpec((1, height, D), lambda i, at: (i, 0, 0))


def split_both(at, keep, other, after=()):
    return call(
        split_kernel, "split", (GRP,), (keep, other), [slot_of(HALF)] * 2,
        [sds((GRP, QUART, D)), sds((GRP, QUART, D), BF16)], [slot_of(QUART)] * 2,
        prefetch=at, after=after,
    )


def quarter_add(keep, other, after=()):
    every = whole((GRP, QUART, D))
    return call(
        add_kernel, "add", (1,), (keep, other), [every] * 2,
        [sds((QUART, D), BF16)] * 4, [whole((QUART, D))] * 4, after=after,
    )


def join_kernel(r0, r1, r2, r3, out_ref):
    for b, ref in enumerate((r0, r1, r2, r3)):
        out_ref[b] = ref[ref.shape[0] - QUART :, :]


def quarter_home(parts, after=()):
    return join([parts[0]] + [trade("seq", b)(parts[b]) for b in (1, 2, 3)], after)


def join(got, after=()):
    return call(
        join_kernel, "join", (1,), got, [whole(a.shape) for a in got],
        [sds((GRP, QUART, D), BF16)], [whole((GRP, QUART, D))], after=after,
    )[0]


def all_home(a):
    x = trade("head", 2)(a)
    return a, x, trade("head", 1)(a), trade("head", 1)(x)


def shards(
    block_in, cotangent, lengths,
    norm_gain, in_proj, conv_params, head_params, gate_gain, out_proj,
    norm_gain_momentum, in_proj_momentum, conv_momentum, head_momentum, gate_gain_momentum,
    out_proj_momentum,
    norm_gain_average, in_proj_average, conv_average, head_average, gate_gain_average,
    out_proj_average,
):
    seq_at, head_at = lax.axis_index("seq"), lax.axis_index("head")
    place = seq_at % GRP
    groups = lax.axis_size("seq") // GRP
    group = seq_at // GRP
    at = [place, head_at % 2, group, 0, head_at // 2, group > 0, group < groups - 1]
    at = jnp.concatenate([jnp.stack([jnp.asarray(v, jnp.int32) for v in at]), lengths])

    def turned(array):
        return jnp.transpose(array, (2, 1, 0))

    once = lengths[0] >= 0

    def apart(step):
        shapes = jax.eval_shape(step)
        return lax.cond(
            once, step, lambda: jax.tree.map(lambda s: jnp.zeros(s.shape, s.dtype), shapes)
        )

    anyspec = pl.BlockSpec(memory_space=pl.ANY)

    picked = pick(at, block_in, True)
    got = [picked[0]] + [trade("seq", b)(picked[b]) for b in (1, 2, 3)]
    w, wdt, low, send_bc, hp, vecs = call(
        prep_kernel, "prep", (1,),
        (turned(in_proj), out_proj, conv_params, head_params, norm_gain, gate_gain),
        [anyspec, whole((ZW, D)), whole((5, 1, 448)), whole((3, NH)), whole((D,)), whole((ZW,))],
        [sds((WROWS, D), BF16), sds((LANES, D), BF16), sds((ZW, D), BF16), sds((80, D), BF16),
         sds((8, LANES)), sds((8, D))],
        [whole((WROWS, D)), whole((LANES, D)), whole((ZW, D)), whole((80, D)), whole((8, LANES)), whole((8, D))],
        scratch=[pltpu.VMEM((COLS, D), F32), pltpu.VMEM((8, LANES), F32), pltpu.SemaphoreType.DMA],
        after=(picked[0],),
    )
    bcs = [send_bc] + [trade("head", b)(send_bc) for b in (1, 2, 3)]
    own, edge = stack(at, got, (w,))
    oth = trade("head", 1)(own)
    halo = moved(edge, GRP)
    cot_picked = pick(at, cotangent, False, (own,))
    cot_got = [cot_picked[0]] + [trade("seq", b)(cot_picked[b]) for b in (1, 2, 3)]

    def wblock(n, height):
        return pl.BlockSpec((height, D), lambda i, *_: (n, 0))

    nrm, z, info, rowc, logs = call(
        first_kernel, "first", (GRP,), (own, oth, vecs, w, wdt, hp),
        [slot(HALF), slot(HALF), whole((8, D)), wblock(0, ZW), whole((LANES, D)), whole((8, LANES))],
        [sds((TOK, D), BF16), sds((TOK, ZW)), sds((TOK, LANES)), sds((8, TOK)), sds((8, LANES))],
        [rows(D), rows(ZW), rows(LANES), pl.BlockSpec((8, BLK), lambda i, *_: (0, i)), whole((8, LANES))],
        scratch=[pltpu.VMEM((8, LANES), F32)], prefetch=at, flops=2 * TOK * D * 512, after=(halo, *bcs[1:]),
    )
    hspec = pl.BlockSpec((1, ZW, ST), lambda i, *_: (i, 0, 0))
    rowspec = pl.BlockSpec((8, BLK), lambda i, *_: (0, i))
    mx, px, xa, xdt, mo, po, bb, cc, hloc, fresh = call(
        mix_kernel, "mix", (GRP,), (nrm, halo, vecs, w, w, *bcs, conv_params, info),
        [rows(D), whole((16, D)), whole((8, D)), wblock(1, ZW), wblock(12, 2 * SW)]
        + [whole((80, D))] * 4 + [whole((5, 1, 448)), rows(LANES)],
        [sds((TOK, ZW)), sds((TOK, ZW)), sds((TOK, ZW)), sds((TOK, ZW), BF16), sds((TOK, 2 * SW)),
         sds((TOK, 2 * SW)), sds((TOK, ST), BF16), sds((TOK, ST), BF16), sds((GRP, ZW, ST)),
         sds((ZW, ST), BF16)],
        [rows(ZW), rows(ZW), rows(ZW), rows(ZW), rows(2 * SW), rows(2 * SW), rows(ST), rows(ST),
         hspec, whole((ZW, ST))],
        scratch=[pltpu.VMEM((2 * ST, D), BF16), pltpu.VMEM((8, 2 * ST), F32),
                 pltpu.VMEM((BLK + 8, ZW + 2 * ST), F32), pltpu.VMEM((BLK + 8, 2 * SW), F32),
                 pltpu.VMEM((ZW, ST), F32)],
        flops=2 * TOK * D * 704, prefetch=at,
    )
    hin = pieces_before(fresh, logs, 1)
    cot_own = stack(at, cot_got, (fresh,))[0]
    cot_oth = trade("head", 1)(cot_own)
    yl, dyn, w_live = call(
        local_kernel, "local", (GRP,),
        (xdt, xa, bb, cc, info, rowc, hloc, cot_own, cot_oth, low, vecs),
        [rows(ZW), rows(ZW), rows(ST), rows(ST), rows(LANES), rowspec, hspec, slot(HALF),
         slot(HALF), whole((ZW, D)), whole((8, D))],
        [sds((TOK, ZW)), sds((TOK, ZW)), sds((TOK, D), BF16)], [rows(ZW), rows(ZW), rows(D)],
        prefetch=at, flops=2 * TOK * (D * ZW + 4 * BLK * ZW),
    )
    y, sums = call(
        gate_kernel, "gate", (GRP,), (yl, cc, info, hin, z, dyn, vecs),
        [rows(ZW), rows(ST), rows(LANES), whole((ZW, ST)), rows(ZW), rows(ZW), whole((8, D))],
        [sds((TOK, ZW)), sds((8, TOK))], [rows(ZW), rowspec], prefetch=at, flops=2 * TOK * ST * ZW,
    )
    all_sums = [sums] + [trade("head", b)(sums) for b in (1, 2, 3)]
    half_slot = pl.BlockSpec((1, HALF, D), lambda i, at: (i ^ at[0], 0, 0))
    dy, dz, yn, pulled, g_gate, keep, send = call(
        ungate_kernel, "ungate", (GRP,), (y, z, dyn, *all_sums, info, cc, vecs, low),
        [rows(ZW)] * 3 + [rowspec] * 4 + [rows(LANES), rows(ST), whole((8, D)), whole((ZW, D))],
        [sds((TOK, ZW)), sds((TOK, ZW), BF16), sds((TOK, ZW), BF16), sds((ZW, ST), BF16), sds((8, ZW))]
        + [sds((GRP, HALF, D), BF16)] * 2,
        [rows(ZW), rows(ZW), rows(ZW), whole((ZW, ST)), whole((8, ZW))] + [half_slot] * 2,
        scratch=[pltpu.VMEM((ZW, ST), F32)], flops=2 * TOK * (ST + D) * ZW, prefetch=at,
    )
    grads1 = call(
        out_kernel, "out", (GRP,), (yn, w_live, nrm, dz), [rows(ZW), rows(D), rows(D), rows(ZW)],
        [sds((SEG1, D), BF16)] * 4, [whole((SEG1, D))] * 4,
        scratch=[pltpu.VMEM((2 * ZW, D), F32)], prefetch=at, flops=4 * TOK * D * ZW,
    )
    got1 = [trade("seq", b)(grads1[b]) for b in (1, 2, 3)]
    keep2, send2 = split_both(at, keep, trade("head", 1)(send), (grads1[0],))
    other2 = trade("head", 2)(send2)
    hback = pl.BlockSpec((1, ZW, ST), lambda i, *_: (GRP - 1 - i, 0, 0))

    after = pieces_before(pulled, logs, -1)
    dxi, dbi, dci, dcum, hall = call(
        inner_kernel, "inner", (GRP,), (xdt, bb, cc, info, rowc, dy, hloc, hin),
        [rows(ZW), rows(ST), rows(ST), rows(LANES), rowspec, rows(ZW), hspec, whole((ZW, ST))],
        [sds((TOK, ZW)), sds((TOK, ST)), sds((TOK, ST)), sds((TOK, LANES)), sds((GRP, ZW, ST))],
        [rows(ZW), rows(ST), rows(ST), rows(LANES), hspec], prefetch=at, after=(send2,),
    )
    dpx, halo_x, *dbc, draw, g_head = call(
        back_kernel, "back", (GRP,),
        (after, dxi, dbi, dci, dcum, hall, xa, px, bb, cc, info, dy, hp, vecs),
        [whole((ZW, ST)), rows_back(ZW), rows_back(ST), rows_back(ST), rows_back(LANES), hback,
         rows_back(ZW), rows_back(ZW), rows_back(ST), rows_back(ST), rows_back(LANES),
         rows_back(ZW), whole((8, LANES)), whole((8, D))],
        [sds((TOK, ZW)), sds((8, ZW))] + [sds((TOK // 2, LANES), BF16)] * 4 + [sds((TOK, LANES), BF16), sds((8, LANES))],
        [rows_back(ZW), whole((8, ZW))] + [rows_back(LANES, HALF)] * 4 + [rows_back(LANES), whole((8, LANES))],
        scratch=[pltpu.VMEM((ZW, ST), F32)], flops=2 * TOK * 4 * ST * ZW, prefetch=at,
    )
    quarters = quarter_add(keep2, other2, (g_head,))
    one, joint = whole((SEG1, D)), whole((SEG1 + QUART, D))
    mine1 = add_rows(SEG1, [grads1[0], *got1], (g_head,))

    def after_rows(width):
        last = TOK // 8 - 1
        return pl.BlockSpec((8, width), lambda i, *_: (min((i + 1) * (BLK // 8), last) if isinstance(i, int) else jnp.minimum((i + 1) * (BLK // 8), last), 0))

    final = GRP * SEG2
    half_rows = pl.BlockSpec((1, HALF, D), lambda i, at: (i ^ at[0], 0, 0))

    bc_got = [trade("head", b)(dbc[b]) for b in (1, 2, 3)]
    pb, end, acc = call(
        last_x_kernel, "last_x", (GRP,),
        (dpx, dpx, mx, conv_params, dz, draw, nrm, w, wdt),
        [rows(ZW), after_rows(ZW), rows(ZW), whole((5, 1, 448)), rows(ZW), rows(LANES),
         rows(D), whole((2 * ZW, D)), whole((LANES, D))],
        [sds((TOK, D)), sds((END, ZW)), sds((final, D))], [rows(D), whole((END, ZW)), whole((final, D))],
        scratch=[pltpu.VMEM((BLK + 8, ZW), F32)], prefetch=at, flops=4 * TOK * D * 2 * ZW, after=(mine1, quarters[0]),
    )
    dpo, halo_o = call(
        edge_kernel, "edge", (GRP,), (dbc[0], *bc_got, po, halo_x),
        [rows(LANES, HALF)] * 4 + [rows(2 * SW), whole((8, ZW))],
        [sds((TOK, 2 * SW)), sds((8, ZW + LANES))], [rows(2 * SW), whole((8, ZW + LANES))], after=(acc,),
    )
    halo_o = moved(halo_o, -GRP)
    total1 = across_groups(mine1, SEG1, (halo_o,))
    keep_b, send_b, *grads2 = call(
        last_o_kernel, "last_o", (GRP,),
        (dpo, dpo, halo_o, mo, conv_params, nrm, w, w, pb, vecs, g_gate, g_head, acc, end, mx),
        [rows(2 * SW), after_rows(2 * SW), whole((8, ZW + LANES)), rows(2 * SW), whole((5, 1, 448)), rows(D),
         wblock(12, 2 * SW), wblock(1, ZW), rows(D), whole((8, D)), whole((8, ZW)), whole((8, LANES)), whole((final, D)),
         whole((END, ZW)), pl.BlockSpec((END, ZW), lambda i, *_: (TOK // END - 1, 0))],
        [sds((GRP, HALF, D), BF16)] * 2 + [sds((SEG2, D), BF16)] * 4,
        [half_rows] * 2 + [whole((SEG2, D))] * 4,
        scratch=[pltpu.VMEM((BLK + 8, 2 * SW), F32), pltpu.VMEM((final, D), F32), pltpu.VMEM((BLK, D), F32)],
        prefetch=at, flops=4 * TOK * D * 2 * SW, after=(total1,),
    )

    def finish():
        keep3, send3 = split_both(at, keep_b, trade("head", 1)(send_b))
        quarters_b = quarter_add(keep3, trade("head", 2)(send3))
        mine2 = group_sum(grads2, SEG2, (quarters_b[0],))
        return quarters_b, mine2, quarter_home(quarters, (mine2,))

    quarters_b, mine2, own_out = apart(finish)
    x_out = trade("head", 2)(own_out)
    root = math.sqrt(TOK * lax.axis_size("seq"))
    mat = whole((ZW, D))
    turned3 = [turned(p) for p in (in_proj, in_proj_momentum, in_proj_average)]
    turned_shape = [sds((COLS, 1, D))] * 3
    buffers = [pltpu.VMEM((COLS, D), F32)] * 6 + [pltpu.SemaphoreType.DMA((5, 6))]
    hbm = pl.BlockSpec(memory_space=pltpu.HBM)

    def gather():
        own_grad = quarter_home(quarters_b)
        return own_grad, across_groups(mine2, SEG2, (own_grad,))

    own_grad, total2 = apart(gather)
    sums1 = all_quarters(total1)
    def spread_out():
        x_grad = trade("head", 2)(own_grad)
        core_grad, sums2 = trade("head", 1)(own_grad), all_quarters(total2)
        parts = (own_out, x_out, trade("head", 1)(own_out), trade("head", 1)(x_out))
        block_out, _ = home(home_out_kernel, "home_out", at, (block_in,), (None,), parts, BF16)
        return x_grad, core_grad, sums2, block_out

    x_grad, core_grad, sums2, block_out = apart(spread_out)
    grad_parts = (own_grad, x_grad, core_grad, trade("head", 1)(x_grad))

    quarter = whole((SEG2, D))
    small, norm = call(
        small_kernel, "small", (1,), sums2, [quarter] * 4, [sds((SMALL, D)), sds((8, D))],
        [whole((SMALL, D)), whole((8, D))], prefetch=at,
    )
    eight = whole((8, D))
    norm = call(
        add_small_kernel, "add_small", (1,), (norm, trade("head", 1)(norm)), [eight] * 2, [sds((8, D))], [eight]
    )[0]
    norms = [norm, trade("head", 2)(norm)]
    *in_half, done_b = call(
        functools.partial(update_b_kernel, rate=RATES[1] / root), "update_b", (1,),
        (*sums2, *turned3), [quarter] * 4 + [hbm] * 3, turned_shape, [hbm] * 3,
        scratch=[pltpu.VMEM((GRP * SEG2, D), F32)] + buffers, prefetch=at,
        after=(norm,), vmem=56, token=True,
    )
    input_grad, done_grad = home(
        home_grad_kernel, "home_grad", at, (block_in, cotangent, vecs), (None, None, (8, D)),
        grad_parts, F32, (done_b,),
    )
    out_w, out_m, out_a, *in_new, done_a = call(
        functools.partial(update_a_kernel, rate=RATES[5] / root, rate_in=RATES[1] / root), "update_a", (1,),
        (*sums1, out_proj, out_proj_momentum, out_proj_average, *turned3, *in_half),
        [one] * 4 + [mat] * 3 + [hbm] * 6, [sds((ZW, D))] * 3 + turned_shape,
        [mat] * 3 + [hbm] * 3, scratch=[pltpu.VMEM((2 * ZW, D), F32)] + buffers, prefetch=at,
        after=(done_grad,), aliases={11: 3, 12: 4, 13: 5}, vmem=56, token=True,
    )
    groups_of = (
        (norm_gain, norm_gain_momentum, norm_gain_average),
        (conv_params, conv_momentum, conv_average),
        (head_params, head_momentum, head_average),
        (gate_gain, gate_gain_momentum, gate_gain_average),
    )
    arrays = [a for three in groups_of for a in three]
    specs = [whole(a.shape) for a in arrays]
    new = call(
        functools.partial(update_small_kernel, rates=[r / root for r in RATES]), "update_small", (1,),
        (small, *norms, *arrays), [whole((SMALL, D))] + [whole((8, D))] * 2 + specs,
        [sds(a.shape) for a in arrays], specs, after=(done_a,),
    )
    ng3, cv3, hd3, gg3 = (tuple(new[3 * n : 3 * n + 3]) for n in range(4))
    in3 = tuple(turned(a) for a in in_new)
    return (block_out, input_grad, *ng3, *in3, *cv3, *hd3, *gg3, out_w, out_m, out_a)


def solution(mesh):
    act, vec, mat = P(None, "seq", None), P(), P(None, "head", None)
    weights = (vec, mat, mat, P(None, "head"), P("head"), P("head", None))
    outs = tuple(spec for spec in weights for _ in range(3))
    return jax.shard_map(
        shards,
        mesh=mesh,
        in_specs=(act, act, P(), *weights, *weights, *weights),
        out_specs=(act, act, *outs),
        check_vma=False,
    )
```

```python
import functools
import math

import jax
import jax.numpy as jnp
from jax import lax
from jax.experimental import pallas as pl
from jax.experimental.pallas import tpu as pltpu
from jax.sharding import PartitionSpec as P

HDIM = 64
CONV = 4
INNER = 1536
EPSILON = 1e-05
MOMENTUM = 0.5
AVERAGE = 0.5
RATES = (0.15, 0.1, 0.5, 0.05, 0.15, 0.02)
HIGHEST = lax.Precision.HIGHEST
F32 = jnp.float32
BF16 = jnp.bfloat16
VMEM = 14
GRP = 4
BLK = 256
HALF = BLK // 2
QUART = BLK // 4
D = 768
ZW = 384
NH = 6
ST = 128
SW = 32
LANES = 128
WCOLS = D // LANES
WROWS = 2 * ZW + 2 * SW
TOK = GRP * BLK
COLS = WROWS + NH
SEG1 = 2 * ZW // GRP
SEG2 = 120
BC_AT, DT_AT, TAP_AT, HD_AT, GG_AT, NG_AT = 384, 448, 456, 464, 472, 473


def nt(a, b, precision=None):
    return lax.dot_general(
        a, b, (((1,), (1,)), ((), ())), preferred_element_type=F32, precision=precision
    )


def nn(a, b, precision=None):
    return lax.dot_general(
        a, b, (((1,), (0,)), ((), ())), preferred_element_type=F32, precision=precision
    )


def tn(a, b, precision=None):
    return lax.dot_general(
        a, b, (((0,), (0,)), ((), ())), preferred_element_type=F32, precision=precision
    )


def iota(shape, dim):
    return lax.broadcasted_iota(jnp.int32, shape, dim)


def split3(value):
    high = value.astype(BF16).astype(F32)
    rest = value - high
    mid = rest.astype(BF16).astype(F32)
    return high, mid, rest - mid


def side_by_side(value, used):
    high, mid, low = split3(jnp.where(iota(value.shape, 1) < used, value, 0.0))
    return (high + pltpu.roll(mid, used, 1) + pltpu.roll(low, 2 * used, 1)).astype(BF16)


def widen(packed, kinds):
    lane, col = iota((LANES, ZW), 0), iota((LANES, ZW), 1)
    goals = [((lane % 32 == col // HDIM + 8 * k) & (lane < 96)).astype(BF16) for k in kinds]
    parts = side_by_side(packed, 32)
    return [nn(parts, goal) for goal in goals]


def head_sums(values):
    goal = (iota((ZW, LANES), 1) == iota((ZW, LANES), 0) // HDIM).astype(BF16)
    high = values.astype(BF16)
    return nn(high, goal) + nn((values - high.astype(F32)).astype(BF16), goal)


def running_sums(triangle, values):
    total = nn(triangle, side_by_side(values, 8))
    total = total + pltpu.roll(total, LANES - 8, 1) + pltpu.roll(total, LANES - 16, 1)
    return jnp.where(iota(total.shape, 1) < 8, total, 0.0)


def lane_mask(which):
    return (iota((1, LANES), 1) // HDIM == which).astype(BF16)


def triangle(lower):
    row, col = iota((BLK, BLK), 0), iota((BLK, BLK), 1)
    return (row >= col if lower else row <= col).astype(BF16)


def call(
    kernel, name, grid, ins, in_specs, outs, out_specs, scratch=(), prefetch=None, flops=0,
    aliases=None, after=(), vmem=VMEM, light=False, token=False,
):
    count = len(ins) + (prefetch is not None)
    results = len(outs)
    if grid == (GRP,) and name not in STREAMED:
        plain, pre, cuts = kernel, count - len(ins), list(in_specs) + list(out_specs)
        used = pre + len(cuts)

        def kernel(*refs):
            at = refs[:pre]

            def step(i):
                views = [part_of(r, c, i, at) for r, c in zip(refs[pre:used], cuts)]
                STEP.append(i)
                plain(*at, *views, *refs[used:])
                STEP.pop()

            def two_steps(k, carry):
                step(2 * k)
                step(2 * k + 1)
                return carry

            if name in BY_TWOS:
                lax.fori_loop(0, GRP // 2, two_steps, 0)
            else:
                for i in range(GRP):
                    step(i)

        grid = (1,)
        in_specs, out_specs = [whole(a.shape) for a in ins], [whole(a.shape) for a in outs]

    def body(*refs):
        rest = refs[count + len(after) :]
        if token:
            rest[results][...] = jnp.zeros((8, LANES), F32)
            rest = rest[:results] + rest[results + 1 :]
        kernel(*refs[:count], *rest)

    outs, out_specs = list(outs), list(out_specs)
    if token:
        outs.append(sds((8, LANES)))
        out_specs.append(whole((8, LANES)))
    nbytes = sum(math.prod(a.shape) * a.dtype.itemsize for a in (*ins, *outs))
    if light:
        flops, nbytes = 1024, 1024
    spec = pltpu.PrefetchScalarGridSpec(
        num_scalar_prefetch=0 if prefetch is None else 1,
        grid=grid,
        in_specs=list(in_specs) + [pl.BlockSpec(memory_space=pl.ANY)] * len(after),
        out_specs=out_specs,
        scratch_shapes=scratch,
    )
    return pl.pallas_call(
        body,
        grid_spec=spec,
        out_shape=outs,
        compiler_params=pltpu.CompilerParams(
            dimension_semantics=("arbitrary",) * len(grid), vmem_limit_bytes=vmem << 20
        ),
        cost_estimate=pl.CostEstimate(flops=flops, bytes_accessed=nbytes, transcendentals=0),
        input_output_aliases=aliases or {},
        name=name,
    )(*(() if prefetch is None else (prefetch,)), *ins, *after)


STEP = []
BY_TWOS = ("inner", )
STREAMED = ("home_out", "home_grad", "split", "gate", "edge", "last_x", )


def step_now():
    return STEP[-1] if STEP else pl.program_id(0)


def when(condition):
    if isinstance(condition, bool):
        return lambda body: body() if condition else None
    return pl.when(condition)


def part_of(ref, spec, i, at):
    size = spec.block_shape
    if size is None or tuple(size) == tuple(ref.shape):
        return ref
    cut = []
    for n, length, full in zip(spec.index_map(i, *at), size, ref.shape):
        if length == full:
            cut.append(slice(None))
        elif isinstance(n, int):
            cut.append(pl.ds(n * length, length))
        else:
            cut.append(pl.ds(pl.multiple_of(n * length, length), length))
    return ref.at[tuple(cut)]


def sds(shape, dtype=F32):
    return jax.ShapeDtypeStruct(shape, dtype)


def whole(shape):
    return pl.BlockSpec(shape, lambda *_: (0,) * len(shape))


def rows(width, height=BLK):
    return pl.BlockSpec((height, width), lambda i, *_: (i, 0))


def rows_back(width, height=BLK):
    return pl.BlockSpec((height, width), lambda i, *_: (GRP - 1 - i, 0))


def slot(height, width=D):
    return pl.BlockSpec((1, height, width), lambda i, at: (i ^ at[0], 0, 0))


def pick_kernel(at, *refs):
    for n, goal in enumerate(refs[2 * GRP :]):
        goal[0:HALF, :] = refs[n][0]
        if goal.shape[0] > HALF:
            goal[HALF:, :] = refs[GRP + n][0]


def pick(at, array, edge, after=()):
    def half_of(b):
        return pl.BlockSpec((1, HALF, D), lambda i, at: (at[0] ^ b, at[1], 0))

    def edge_of(b):
        return pl.BlockSpec((1, 16, D), lambda i, at: (at[0] ^ b, BLK // 16 - 1, 0))

    size = HALF + 16 * edge
    specs = [half_of(b) for b in range(GRP)] + [edge_of(b) for b in range(GRP)]
    return call(
        pick_kernel, "pick", (1,), (array,) * (2 * GRP), specs,
        [sds((size, D), BF16)] * GRP, [whole((size, D))] * GRP, prefetch=at, after=after,
    )


def stack_kernel(at, r0, r1, r2, r3, out_ref, *edge):
    refs = (r0, r1, r2, r3)
    for b, ref in enumerate(refs):
        out_ref[b] = ref[0:HALF, :]
    for goal in edge:
        for b, ref in enumerate(refs):

            @when(at[0] ^ b == GRP - 1)
            def _():
                goal[...] = ref[HALF:, :]


def stack(at, parts, after=()):
    size = parts[0].shape[0]
    outs, specs = [sds((GRP, HALF, D), BF16)], [whole((GRP, HALF, D))]
    if size > HALF:
        outs, specs = outs + [sds((16, D), BF16)], specs + [whole((16, D))]
    return call(
        stack_kernel, "stack", (1,), parts, [whole((size, D))] * GRP, outs, specs, prefetch=at, after=after
    )


def prep_kernel(
    win, wout, taps, heads, ng, gg,
    w_ref, wdt_ref, low_ref, send_ref, hp_ref, vec_ref, wide_w, scr, sem,
):
    copy = pltpu.make_async_copy(win.at[:, 0, :], wide_w, sem)
    copy.start()
    low_ref[...] = wout[...].astype(BF16)
    scr[...] = jnp.zeros_like(scr)
    scr[0:3, 0:NH] = heads[...]
    lanes = scr[...]
    for by in (8, 16, 32, 64):
        lanes = lanes + pltpu.roll(lanes, by, 1)
    hp_ref[...] = lanes
    vec_ref[...] = jnp.zeros_like(vec_ref)
    vec_ref[0:1, :] = ng[...].reshape(1, D)
    vec_ref[1:2, 0:ZW] = gg[...].reshape(1, ZW)
    vec_ref[2:3, 0:ZW] = widen(lanes, (0,))[0][2:3, :]
    copy.wait()
    w_ref[...] = wide_w[0:WROWS, :].astype(BF16)
    last = jnp.concatenate([wide_w[WROWS:, :], jnp.zeros((8 - NH, D), F32)], axis=0)
    wdt_ref[...] = jnp.concatenate([last] * 16, axis=0).astype(BF16)
    send_ref[0 : 2 * SW, :] = w_ref[2 * ZW : WROWS, :]
    own = taps[:, 0, :][:, ZW:]
    high = own.astype(BF16).astype(F32)
    mid = (own - high).astype(BF16).astype(F32)
    low = own - high - mid
    parts = jnp.concatenate([high, mid, low, jnp.zeros((1, 2 * SW), F32)], axis=0)
    send_ref[2 * SW :, :] = jnp.zeros((16, D), BF16)
    send_ref[2 * SW :, 0 : 2 * SW] = parts.astype(BF16)


def chunk_of(own_ref, oth_ref, core):
    own, oth = own_ref[0], oth_ref[0]
    first = core == 0
    return jnp.concatenate([jnp.where(first, own, oth), jnp.where(first, oth, own)], axis=0)


def normalise(x, gain):
    u = x.astype(F32)
    scale = lax.rsqrt(jnp.mean(u * u, axis=-1, keepdims=True) + EPSILON)
    return (u * scale * gain).astype(BF16)


def first_kernel(at, own, oth, vecs, wz, wdt, hp, nrm_ref, z_ref, info_ref, row_ref, tot_ref, cum):
    step = step_now()

    @when(step == 0)
    def _():
        cum[...] = jnp.zeros_like(cum)

    normed = normalise(chunk_of(own, oth, at[1]), vecs[0:1, :])
    nrm_ref[...] = normed
    z_ref[...] = nt(normed, wz[...])
    biased = nt(normed, wdt[...]) + hp[0:1, :]
    steps = jax.nn.softplus(biased)
    decays = -jnp.exp(hp[1:2, :]) * steps
    c = running_sums(triangle(True), decays)
    group = iota((BLK, LANES), 1) // 8
    info = jnp.where(group == 0, c, jnp.where(group == 1, steps, biased))
    moved_c = pltpu.roll(c, 24, 1) + cum[0:1, :]
    info_ref[...] = jnp.where(group == 3, moved_c, info)
    row_ref[...] = jnp.transpose(c)[0:8, :]
    cum[0:1, :] = moved_c[BLK - 1 : BLK, :]
    tot_ref[...] = jnp.broadcast_to(cum[0:1, :], (8, LANES))


def mix_kernel(
    at, nrm, halo, vecs, wx, wo, bc0, bc1, bc2, bc3, taps, info,
    mx_ref, px_ref, xa_ref, xdt_ref, mo_ref, po_ref, b_ref, c_ref, h_ref, s_ref,
    wbc, tbc, ext, exto, state,
):
    step = step_now()
    tap = taps[:, 0, :]

    @when(step == 0)
    def _():
        place = jnp.zeros((16, 2 * ST), F32)
        for b, buf in enumerate((bc0, bc1, bc2, bc3)):
            wbc[SW * b : SW * (b + 1), :] = buf[0:SW, :]
            wbc[ST + SW * b : ST + SW * (b + 1), :] = buf[SW : 2 * SW, :]
            at_row, at_col = iota((2 * SW, 2 * ST), 0), iota((2 * SW, 2 * ST), 1)
            goal = jnp.where(at_row < SW, SW * b + at_row, ST + SW * b + at_row - SW)
            put = (at_col == goal).astype(BF16)
            place = place + nn(buf[2 * SW :, 0 : 2 * SW], put)
        tbc[0:5, :] = place[0:5] + place[5:10] + place[10:15]
        before = normalise(jnp.where(at[5] > 0, halo[...], 0.0).astype(BF16), vecs[0:1, :])
        ext[0:8, 0:ZW] = nt(before, wx[...])[8:16]
        ext[0:8, ZW:] = nt(before, wbc[...])[8:16]
        exto[0:8, :] = nt(before, wo[...])[8:16]
        state[...] = jnp.zeros_like(state)

    normed = nrm[...]
    mixed = nt(normed, wx[...])
    mx_ref[...] = mixed
    ext[8:, 0:ZW] = mixed
    ext[8:, ZW:] = nt(normed, wbc[...])
    own = nt(normed, wo[...])
    mo_ref[...] = own
    exto[8:, :] = own
    pre = tap[4:5, 0:ZW]
    pre_bc = tbc[4:5, :]
    pre_o = tap[4:5, ZW:]
    for k in range(CONV):
        pre = pre + tap[k : k + 1, 0:ZW] * ext[5 + k : 5 + k + BLK, 0:ZW]
        pre_bc = pre_bc + tbc[k : k + 1, :] * ext[5 + k : 5 + k + BLK, ZW:]
        pre_o = pre_o + tap[k : k + 1, ZW:] * exto[5 + k : 5 + k + BLK, :]
    px_ref[...] = pre
    po_ref[...] = pre_o
    x = pre * jax.nn.sigmoid(pre)
    xa_ref[...] = x
    bc = (pre_bc * jax.nn.sigmoid(pre_bc)).astype(BF16)
    b_ref[...] = bc[:, 0:ST]
    c_ref[...] = bc[:, ST:]
    ext[0:8, :] = ext[BLK:, :]
    exto[0:8, :] = exto[BLK:, :]

    packed = info[...]
    c = packed[:, 0:LANES]
    keep = iota((BLK, LANES), 1) < 8
    tail = jnp.where(keep, jnp.exp(jnp.where(keep, c[BLK - 1 : BLK, :] - c, 0.0)), 0.0)
    tail_wide, dt_wide = widen(jnp.where(keep, tail, packed), (0, 1))
    xdt = x * dt_wide
    xdt_ref[...] = xdt.astype(BF16)
    fresh = tn((xdt * tail_wide).astype(BF16), bc[:, 0:ST])
    h_ref[0] = state[...]
    for h in range(NH):
        decay = jnp.exp(packed[BLK - 1 : BLK, h : h + 1])
        at = pl.ds(HDIM * h, HDIM)
        state[at, :] = decay * state[at, :] + fresh[HDIM * h : HDIM * (h + 1), :]
    s_ref[...] = state[...].astype(BF16)


def weights_of(h, packed, row, causal):
    diff = packed[:, h : h + 1] - row[h : h + 1, :]
    return jnp.where(causal, jnp.exp(jnp.where(causal, diff, 0.0)), 0.0)


def local_kernel(
    at, xdt, xa, b, c, info, row, hloc, own, oth, low, vecs, yl_ref, dyn_ref, w_ref
):
    step = step_now()
    packed = info[...]
    rowc = row[...]
    causal = iota((BLK, BLK), 0) >= iota((BLK, BLK), 1)
    scores = nt(c[...], b[...])
    c_exp = jnp.exp(jnp.where(iota((BLK, LANES), 1) < 8, packed, 0.0))
    carried = nt(c[...], hloc[0].astype(BF16)) * widen(c_exp, (0,))[0]
    carried = carried + vecs[2:3, 0:ZW] * xa[...]
    for p in range(NH // 2):
        x = xdt[:, LANES * p : LANES * (p + 1)]
        total = carried[:, LANES * p : LANES * (p + 1)]
        for q in range(2):
            weights = (weights_of(2 * p + q, packed, rowc, causal) * scores).astype(BF16)
            total = total + nn(weights, x * lane_mask(q))
        yl_ref[:, LANES * p : LANES * (p + 1)] = total
    place = (at[2] * GRP + step) * BLK + iota((BLK, 1), 0)
    live = place < at[7 + at[0]]
    w = jnp.where(live, chunk_of(own, oth, at[1]), 0.0).astype(BF16)
    w_ref[...] = w
    dyn_ref[...] = nt(w, low[...])


def gate_kernel(at, yl, c, info, hin, z, dyn, vecs, y_ref, sum_ref):
    packed = info[...]
    lane = iota((BLK, LANES), 1)
    cum = jnp.where(lane // 8 == 3, jnp.exp(jnp.where(lane // 8 == 3, packed, 0.0)), 0.0)
    entering = jnp.where(at[5] > 0, hin[...], 0.0).astype(BF16)
    y = yl[...] + nt(c[...], entering) * widen(cum, (3,))[0]
    y_ref[...] = y
    gate = z[...]
    g = y * (gate * jax.nn.sigmoid(gate))
    squares = jnp.sum(g * g, axis=-1, keepdims=True)
    inner = jnp.sum(dyn[...] * vecs[1:2, 0:ZW] * g, axis=-1, keepdims=True)
    both = jnp.where(lane == 0, squares, jnp.where(lane == 1, inner, 0.0))
    sum_ref[...] = jnp.transpose(both)[0:8, :]


def ungate_kernel(
    at, y, z, dyn, s0, s1, s2, s3, info, c, vecs, low,
    dy_ref, dz_ref, yn_ref, p_ref, gg_ref, keep_ref, send_ref, acc,
):
    step = step_now()

    @when(step == 0)
    def _():
        acc[...] = jnp.zeros_like(acc)
        gg_ref[...] = jnp.zeros_like(gg_ref)

    sums = s0[...] + s1[...] + s2[...] + s3[...]
    sums = jnp.transpose(jnp.concatenate([sums, jnp.zeros((LANES - 8, BLK), F32)], axis=0))
    q = lax.rsqrt(sums[:, 0:1] / INNER + EPSILON)
    mean = sums[:, 1:2] * q / INNER
    gate = z[...]
    sigma = jax.nn.sigmoid(gate)
    silu = gate * sigma
    out = y[...]
    g = out * silu
    n = g * q
    d = dyn[...]
    gg = vecs[1:2, 0:ZW]
    d_g = q * (d * gg - n * mean)
    d_y = d_g * silu
    dy_ref[...] = d_y
    dz_ref[...] = (d_g * out * sigma * (1.0 + gate * (1.0 - sigma))).astype(BF16)
    yn = (n * gg).astype(BF16)
    yn_ref[...] = yn
    halves(nn(yn, low[...]).astype(BF16), at[1], keep_ref, send_ref)
    gg_ref[0:1, :] += jnp.sum(d * n, axis=0, keepdims=True)
    packed = info[...]
    lane = iota((BLK, LANES), 1)
    cum = jnp.where(lane // 8 == 3, jnp.exp(jnp.where(lane // 8 == 3, packed, 0.0)), 0.0)
    acc[...] += tn((d_y * widen(cum, (3,))[0]).astype(BF16), c[...])
    p_ref[...] = acc[...].astype(BF16)


def halves(value, core, keep_ref, send_ref):
    low, high = value[0:HALF], value[HALF:]
    first = core == 0
    keep_ref[0] = jnp.where(first, low, high)
    send_ref[0] = jnp.where(first, high, low)


def out_kernel(
    at, yn, w, nrm, dz, g0, g1, g2, g3, acc
):
    step = step_now()

    @when(step == 0)
    def _():
        acc[...] = jnp.zeros_like(acc)

    acc[0:ZW, :] += tn(dz[...], nrm[...])
    acc[ZW:, :] += tn(yn[...], w[...])

    @when(step == GRP - 1)
    def _():
        for b, ref in enumerate((g0, g1, g2, g3)):
            start = pl.multiple_of((at[0] ^ b) * SEG1, SEG1)
            ref[...] = acc[pl.ds(start, SEG1), :].astype(BF16)


def inner_kernel(
    at, xdt, b, c, info, row, dy, hloc, hin, dxi_ref, dbi_ref, dci_ref, dcum_ref, hall_ref
):
    packed = info[...]
    rowc = row[...]
    lane = iota((BLK, LANES), 1)
    causal = iota((BLK, BLK), 0) >= iota((BLK, BLK), 1)
    bb, cc = b[...], c[...]
    scores = nt(cc, bb)
    d_scores = jnp.zeros((BLK, BLK), F32)
    d_cum = jnp.zeros((BLK, LANES), F32)
    columns = jnp.zeros((8, BLK), F32)
    row8 = iota((8, BLK), 0)
    dyv = dy[...]
    for p in range(NH // 2):
        x = xdt[:, LANES * p : LANES * (p + 1)]
        d = dyv[:, LANES * p : LANES * (p + 1)].astype(BF16)
        total = jnp.zeros((BLK, LANES), F32)
        for q in range(2):
            h = 2 * p + q
            spans = weights_of(h, packed, rowc, causal)
            d_h = d * lane_mask(q)
            d_spans = nt(d_h, x) * spans
            d_scores = d_scores + d_spans
            both = (d_spans * scores).astype(BF16)
            d_cum = d_cum + nn(both, (lane == h).astype(BF16))
            columns = columns + nn((row8 == h).astype(BF16), both)
            total = total + tn((spans * scores).astype(BF16), d_h)
        dxi_ref[:, LANES * p : LANES * (p + 1)] = total
    columns = jnp.concatenate([columns, jnp.zeros((LANES - 8, BLK), F32)], axis=0)
    d_cum = d_cum - jnp.transpose(columns)
    low_scores = d_scores.astype(BF16)
    c_exp = jnp.exp(jnp.where(lane < 8, packed, 0.0))
    c_wide = widen(c_exp, (0,))[0]
    base = packed[0:1, 24:32] - packed[0:1, 0:8]
    for h in range(NH):
        here = pl.ds(HDIM * h, HDIM)
        grown = jnp.exp(base[:, h : h + 1]) * hin[here, :].astype(F32)
        grown = jnp.where(at[5] > 0, grown, 0.0)
        hall_ref[0, here, :] = hloc[0, here, :] + grown
    entering = hall_ref[0].astype(BF16)
    carried = nt(cc, entering) * c_wide
    d_cum = d_cum + head_sums(dyv * carried)
    dcum_ref[...] = d_cum
    dci_ref[...] = nn(low_scores, bb) + nn((dyv * c_wide).astype(BF16), entering)
    dbi_ref[...] = tn(low_scores, cc)


def back_kernel(
    at, after, dxi, dbi, dci, dcum, hall, xa, px, b, c, info, dy, hp, vecs,
    dpx_ref, halo_ref, o0, o1, o2, o3, draw_ref, hg_ref, state,
):
    step = step_now()

    @when(step == 0)
    def _():
        state[...] = jnp.where(at[6] > 0, after[...].astype(F32), 0.0)
        hg_ref[...] = jnp.zeros_like(hg_ref)

    packed = info[...]
    lane = iota((BLK, LANES), 1)
    first = lane < 8
    c_last = packed[BLK - 1 : BLK, :]
    tail = jnp.where(first, jnp.exp(jnp.where(first, c_last - packed, 0.0)), 0.0)
    c_exp = jnp.where(first, jnp.exp(jnp.where(first, packed, 0.0)), 0.0)
    mixed = jnp.where(first, tail, jnp.where(lane < 16, packed, pltpu.roll(c_exp, 16, 1)))
    tail_wide, dt_wide, c_wide = widen(mixed, (0, 1, 2))
    x = xa[...]
    xdt = x * dt_wide
    d_y = dy[...]
    bb, cc = b[...], c[...]
    low_state = state[...].astype(BF16)
    d_tail = nt(bb, low_state) * tail_wide
    tails = head_sums(xdt * d_tail)
    d_xdt = dxi[...] + d_tail
    d_b = dbi[...] + nn((xdt * tail_wide).astype(BF16), low_state)
    d_c = dci[...]
    ending = jnp.sum(tails, axis=0, keepdims=True)
    lane1 = iota((1, LANES), 1)
    for h in range(NH):
        here = pl.ds(HDIM * h, HDIM)
        inner = jnp.sum(state[here, :] * hall[0, here, :], axis=(0, 1), keepdims=True)
        ending = ending + jnp.where(lane1 == h, inner * jnp.exp(c_last[:, h : h + 1]), 0.0)
    d_cum = dcum[...] - tails
    d_cum = d_cum + jnp.where(iota((BLK, LANES), 0) == BLK - 1, ending, 0.0)
    d_a = running_sums(triangle(False), d_cum)
    fresh = tn((d_y * c_wide).astype(BF16), cc)
    for h in range(NH):
        here = pl.ds(HDIM * h, HDIM)
        decay = jnp.exp(c_last[:, h : h + 1])
        state[here, :] = decay * state[here, :] + fresh[HDIM * h : HDIM * (h + 1), :]
    rate = -jnp.exp(hp[1:2, :])
    d_dt = head_sums(x * d_xdt) + rate * d_a
    biased = pltpu.roll(packed, LANES - 16, 1)
    steps = pltpu.roll(packed, LANES - 8, 1)
    used = lane < NH
    d_raw = jnp.where(used, d_dt * jax.nn.sigmoid(jnp.where(used, biased, 0.0)), 0.0)
    draw_ref[...] = d_raw.astype(BF16)
    hg_ref[0:1, :] += jnp.sum(d_raw, axis=0, keepdims=True)
    g_rate = jnp.where(used, d_a * rate * jnp.where(used, steps, 0.0), 0.0)
    hg_ref[1:2, :] += jnp.sum(g_rate, axis=0, keepdims=True)
    hg_ref[2:3, :] += jnp.sum(head_sums(d_y * x), axis=0, keepdims=True)
    d_x = d_xdt * dt_wide + vecs[2:3, 0:ZW] * d_y
    pre = px[...]
    sigma = jax.nn.sigmoid(pre)
    d_pre = d_x * sigma * (1.0 + pre * (1.0 - sigma))
    dpx_ref[...] = d_pre
    halo_ref[...] = d_pre[0:8]
    for s, ref in enumerate((o0, o1, o2, o3)):
        for n, value in enumerate((d_b, d_c)):
            mine = value[:, SW * s : SW * (s + 1)].astype(BF16)
            ref[:, SW * n : SW * (n + 1)] = mine[0:HALF]
            ref[:, SW * (n + 2) : SW * (n + 3)] = mine[HALF:]


def edge_kernel(o0, r1, r2, r3, po, halo_x, dpo_ref, halo_ref):
    d = o0[...].astype(F32) + r1[...].astype(F32) + r2[...].astype(F32) + r3[...].astype(F32)
    d = jnp.concatenate([d[:, 0 : 2 * SW], d[:, 2 * SW :]], axis=0)
    pre = po[...]
    sigma = jax.nn.sigmoid(pre)
    d = d * sigma * (1.0 + pre * (1.0 - sigma))
    dpo_ref[...] = d

    @when(step_now() == 0)
    def _():
        halo_ref[:, X_LANES] = halo_x[...]
        halo_ref[:, ZW:] = jnp.zeros((8, LANES), F32)
        halo_ref[:, O_LANES] = d[0:8]


def unconvolve(acc, ext, d_pre, follows, values, tap, lanes):
    ext[0:BLK, :] = d_pre
    ext[BLK:, :] = follows
    total = jnp.zeros(d_pre.shape, F32)
    for k in range(CONV):
        shifted = ext[3 - k : 3 - k + BLK, :]
        total = total + tap[k : k + 1, lanes] * shifted
        acc[TAP_AT + k : TAP_AT + k + 1, lanes] += jnp.sum(values * shifted, axis=0, keepdims=True)
    acc[TAP_AT + CONV : TAP_AT + CONV + 1, lanes] += jnp.sum(d_pre, axis=0, keepdims=True)
    return total


X_LANES, O_LANES = slice(0, ZW), slice(ZW, ZW + 2 * SW)


END = 16


def last_x_kernel(
    at, dpx, nx, mx, taps, dz, draw, nrm, w, wdt, pb_ref, end_ref, acc, ext
):
    step = step_now()

    @when(step == 0)
    def _():
        acc[...] = jnp.zeros_like(acc)

    follows = jnp.where(step < GRP - 1, nx[...], 0.0)
    d_mx = unconvolve(acc, ext, dpx[...], follows, mx[...], taps[:, 0, :], X_LANES)
    end_ref[...] = d_mx[BLK - END :, :]
    late = (step == GRP - 1) & (iota((BLK, 1), 0) >= BLK - END)
    p_x = jnp.where(late, 0.0, d_mx).astype(BF16)
    p_t = draw[...]
    pb_ref[...] = nn(dz[...], w[0:ZW, :]) + nn(p_x, w[ZW:, :]) + nn(p_t, wdt[...])
    normed = nrm[...]
    acc[0:ZW, :] += tn(p_x, normed)
    acc[DT_AT : DT_AT + 8, :] += tn(p_t, normed)[0:8]


def last_o_kernel(
    at, dpo, no, halo, mo, taps, nrm, w, wx, pb, vecs, gg, hg, acc_in, end, mxe,
    keep_ref, send_ref, g0, g1, g2, g3, ext, acc, wide_pb,
):
    step = step_now()

    @when(step == 0)
    def _():
        acc[...] = acc_in[...]
        acc[HD_AT : HD_AT + 8, 0:LANES] = hg[...]
        acc[GG_AT : GG_AT + 1, 0:ZW] = gg[0:1, :]

    after = jnp.where(at[6] > 0, halo[...], 0.0)
    follows = jnp.where(step < GRP - 1, no[...], after[:, O_LANES])
    p_o = unconvolve(acc, ext, dpo[...], follows, mo[...], taps[:, 0, :], O_LANES).astype(BF16)
    wide_pb[...] = pb[...] + nn(p_o, w[...])
    normed = nrm[...]

    @when(step == GRP - 1)
    def _():
        rows_after = jnp.concatenate([jnp.zeros((END, ZW), F32), after[:, X_LANES]], axis=0)
        total = end[...]
        for k in range(CONV):
            shifted = rows_after[3 - k : 3 - k + END, :]
            total = total + taps[k : k + 1, 0, X_LANES] * shifted
            grad = jnp.sum(mxe[...] * shifted, axis=0, keepdims=True)
            acc[TAP_AT + k : TAP_AT + k + 1, X_LANES] += grad
        p_x = total.astype(BF16)
        wide_pb[BLK - END :, :] += nn(p_x, wx[...])
        acc[0:ZW, :] += tn(p_x, normed[BLK - END :, :])

    back = wide_pb[...]
    halves(back.astype(BF16), at[1], keep_ref, send_ref)
    acc[NG_AT : NG_AT + 1, :] += jnp.sum(back * normed.astype(F32), axis=0, keepdims=True)
    acc[BC_AT:DT_AT, :] += tn(p_o, normed)

    @when(step == GRP - 1)
    def _():
        acc[NG_AT : NG_AT + 1, :] = acc[NG_AT : NG_AT + 1, :] / vecs[0:1, :]
        for b, ref in enumerate((g0, g1, g2, g3)):
            start = pl.multiple_of((at[0] ^ b) * SEG2, 8)
            ref[...] = acc[pl.ds(start, SEG2), :].astype(BF16)


def split_kernel(at, keep, other, keep_ref, send_ref):
    value = keep[0].astype(F32) + other[0].astype(F32)
    low, high = value[0:QUART], value[QUART:]
    first = at[4] == 0
    keep_ref[0] = jnp.where(first, low, high)
    send_ref[0] = jnp.where(first, high, low).astype(BF16)


def add_kernel(keep, other, r0, r1, r2, r3):
    for b, ref in enumerate((r0, r1, r2, r3)):
        ref[...] = (keep[b] + other[b].astype(F32)).astype(BF16)


def sum_kernel(*refs):
    total = refs[0][...].astype(F32)
    for ref in refs[1:-1]:
        total = total + ref[...].astype(F32)
    refs[-1][...] = total.astype(refs[-1].dtype)


def place_quarters(at, b, parts, scr):
    core, xbit = at[1], at[4]
    for n, ref in enumerate(parts):
        half = core if n < 2 else 1 - core
        quarter = xbit if n % 2 == 0 else 1 - xbit
        start = pl.multiple_of(half * HALF + quarter * QUART, QUART)
        scr[pl.ds(start, QUART), :] = ref[0]


def home_out_kernel(at, block, a, x, ac, xc, out_ref, scr):
    step = step_now()
    place_quarters(at, step, (a, x, ac, xc), scr)
    place = (at[2] * GRP + at[0]) * BLK + iota((BLK, 1), 0)
    live = place < at[7 + step]
    total = block[0].astype(F32) + scr[...].astype(F32)
    out_ref[0] = jnp.where(live, total, 0.0).astype(BF16)


def home_grad_kernel(at, block, cot, vecs, a, x, ac, xc, out_ref, scr):
    step = step_now()
    place_quarters(at, step, (a, x, ac, xc), scr)
    place = (at[2] * GRP + at[0]) * BLK + iota((BLK, 1), 0)
    live = place < at[7 + step]
    u = block[0].astype(F32)
    scale = lax.rsqrt(jnp.mean(u * u, axis=-1, keepdims=True) + EPSILON)
    m = u * scale
    f = scr[...].astype(F32) * vecs[0:1, :]
    inner = jnp.mean(f * m, axis=-1, keepdims=True)
    out_ref[0] = scale * (f - m * inner) + jnp.where(live, cot[0].astype(F32), 0.0)


def home(kernel, name, at, arrays, specs, parts, dtype, after=()):
    full = pl.BlockSpec((1, BLK, D), lambda i, *_: (i, 0, 0))
    part = pl.BlockSpec((1, QUART, D), lambda i, at: (i ^ at[0], 0, 0))
    specs = [full if s is None else whole(s) for s in specs]
    return call(
        kernel, name, (GRP,), (*arrays, *parts), specs + [part] * 4, [sds((GRP, BLK, D), dtype)],
        [full], scratch=[pltpu.VMEM((BLK, D), BF16)], prefetch=at, after=after, token=True,
    )


def advance(weight, gradient, moment, average, rate):
    moment_new = MOMENTUM * moment + gradient
    weight_new = weight - rate * (gradient + MOMENTUM * moment_new)
    average_new = AVERAGE * average + (1.0 - AVERAGE) * weight_new
    return (weight_new, moment_new, average_new)


def stepped(grad, grad_at, weights, outs, blocks, buffers, sems, rate):
    ins, done = buffers[:3], buffers[3:]

    def reads(n):
        start, size = blocks[n]
        return [
            pltpu.make_async_copy(
                w.at[pl.ds(start, size), 0, :], buf.at[pl.ds(start, size), :], sems.at[n, j]
            )
            for j, (w, buf) in enumerate(zip(weights, ins))
        ]

    def writes(n):
        start, size = blocks[n]
        return [
            pltpu.make_async_copy(
                buf.at[pl.ds(start, size), :], o.at[pl.ds(start, size), 0, :], sems.at[n, 3 + j]
            )
            for j, (o, buf) in enumerate(zip(outs, done))
        ]

    for n in range(len(blocks)):
        for copy in reads(n):
            copy.start()
    for n, (start, size) in enumerate(blocks):
        for copy in reads(n):
            copy.wait()
        cut = 16 if size % 16 == 0 else size

        def some(k, carry):
            here = pl.ds(pl.multiple_of(start + k * cut, 8), cut)
            there = pl.ds(pl.multiple_of(grad_at(n) + k * cut, 8), cut)
            new = advance(ins[0][here, :], grad[there, :], ins[1][here, :], ins[2][here, :], rate)
            for buf, value in zip(done, new):
                buf[here, :] = value
            return carry

        lax.fori_loop(0, size // cut, some, 0)
        for copy in writes(n):
            copy.start()
    for n in range(len(blocks)):
        for copy in writes(n):
            copy.wait()


Z_BLOCKS = tuple((96 * n, 96) for n in range(4))
X_BLOCKS = tuple((ZW + 96 * n, 96) for n in range(4)) + ((2 * ZW, COLS - 2 * ZW),)


def update_a_kernel(
    at, g0, g1, g2, g3, w, m, a, wi, mi, ai, x0, x1, x2, w_ref, m_ref, a_ref, wo, mo, ao,
    grad, b0, b1, b2, b3, b4, b5, sems, *, rate, rate_in,
):
    for b, ref in enumerate((g0, g1, g2, g3)):
        grad[pl.ds(pl.multiple_of((at[0] ^ b) * SEG1, SEG1), SEG1), :] = ref[0:SEG1, :].astype(F32)
    stepped(
        grad, lambda n: 96 * n, (wi, mi, ai), (wo, mo, ao), Z_BLOCKS,
        (b0, b1, b2, b3, b4, b5), sems, rate_in,
    )
    w_ref[...], m_ref[...], a_ref[...] = advance(w[...], grad[ZW:, :], m[...], a[...], rate)


def update_b_kernel(
    at, g0, g1, g2, g3, wi, mi, ai, wo, mo, ao,
    grad, b0, b1, b2, b3, b4, b5, sems, *, rate,
):
    for b, ref in enumerate((g0, g1, g2, g3)):
        start = pl.multiple_of((at[0] ^ b) * SEG2, 8)
        grad[pl.ds(start, SEG2), :] = ref[...].astype(F32)
    stepped(
        grad, lambda n: 96 * n, (wi, mi, ai), (wo, mo, ao), X_BLOCKS,
        (b0, b1, b2, b3, b4, b5), sems, rate,
    )


SMALL = GRP * SEG2 - TAP_AT


def small_kernel(at, g0, g1, g2, g3, small_ref, norm_ref):
    for b, ref in enumerate((g0, g1, g2, g3)):

        @when(at[0] ^ b == GRP - 1)
        def _():
            small_ref[...] = ref[SEG2 - SMALL :, :].astype(F32)
            norm_ref[...] = ref[SEG2 - 8 :, :].astype(F32)


def add_small_kernel(a, b, out_ref):
    out_ref[...] = a[...] + b[...]


def update_small_kernel(
    small, n0, n1, ng, ngm, nga, cv, cvm, cva, hd, hdm, hda, gg, ggm, gga, *outs, rates
):
    ng_o, cv_o, hd_o, gg_o = (outs[3 * n : 3 * n + 3] for n in range(4))
    at_norm = NG_AT - TAP_AT - (SMALL - 8)
    norms = [n[at_norm : at_norm + 1, :] for n in (n0, n1)]
    grad = (norms[0] + norms[1]).reshape(D)
    for ref, new in zip(ng_o, advance(ng[...], grad, ngm[...], nga[...], rates[0])):
        ref[...] = new
    grad = small[0:5, 0 : ZW + 2 * SW]
    old = [a[:, 0, :] for a in (cv, cvm, cva)]
    for ref, new in zip(cv_o, advance(old[0], grad, old[1], old[2], rates[2])):
        ref[:, 0, :] = new
    at_head = HD_AT - TAP_AT
    grad = small[at_head : at_head + 3, 0:NH]
    for ref, new in zip(hd_o, advance(hd[...], grad, hdm[...], hda[...], rates[3])):
        ref[...] = new
    at_gate = GG_AT - TAP_AT
    grad = small[at_gate : at_gate + 1, 0:ZW].reshape(ZW)
    for ref, new in zip(gg_o, advance(gg[...], grad, ggm[...], gga[...], rates[4])):
        ref[...] = new


def trade(axis, flip):
    count = lax.axis_size(axis)
    pairs = [(i, i ^ flip) for i in range(count)]
    return lambda array: lax.ppermute(array, axis, pairs)


def moved(array, by):
    count = lax.axis_size("seq")
    if count == 2 * abs(by):
        return trade("seq", abs(by))(array)
    pairs = [(i, i + by) for i in range(count) if 0 <= i + by < count]
    return lax.ppermute(array, "seq", pairs)


def grow(decay, state):
    return jnp.repeat(decay[0, 24 : 24 + NH], HDIM)[:, None] * state


def pieces_before(state, logs, way):
    count = lax.axis_size("seq") // GRP
    found = moved(state, way * GRP)
    by = 1
    if count > 2:
        there = lax.axis_index("seq") // GRP
        decay = moved(jnp.exp(logs), way * GRP)
        total = found.astype(F32)
        while by < count - 1:
            inside = (there >= by) if way > 0 else (there + by < count)
            earlier = moved(total.astype(BF16), way * GRP * by).astype(F32)
            total = jnp.where(inside, grow(decay, earlier) + total, total)
            decay = decay * moved(decay, way * GRP * by)
            by *= 2
        found = total.astype(BF16)
    return found


def group_sum(parts, height, after=()):
    return add_rows(height, [parts[0]] + [trade("seq", b)(parts[b]) for b in (1, 2, 3)], after)


def add_rows(height, arrays, after=()):
    spec = whole((height, D))
    out = [sds((height, D), BF16)]
    return call(sum_kernel, "sum", (1,), arrays, [spec] * len(arrays), out, [spec], after=after)[0]


def across_groups(mine, height, after=()):
    by = GRP
    while by < lax.axis_size("seq"):
        mine = add_rows(height, [mine, trade("seq", by)(mine)], after)
        by *= 2
    return mine


def all_quarters(mine):
    return [mine] + [trade("seq", b)(mine) for b in (1, 2, 3)]


def slot_of(height):
    return pl.BlockSpec((1, height, D), lambda i, at: (i, 0, 0))


def split_both(at, keep, other, after=()):
    return call(
        split_kernel, "split", (GRP,), (keep, other), [slot_of(HALF)] * 2,
        [sds((GRP, QUART, D)), sds((GRP, QUART, D), BF16)], [slot_of(QUART)] * 2,
        prefetch=at, after=after,
    )


def quarter_add(keep, other, after=()):
    every = whole((GRP, QUART, D))
    return call(
        add_kernel, "add", (1,), (keep, other), [every] * 2,
        [sds((QUART, D), BF16)] * 4, [whole((QUART, D))] * 4, after=after,
    )


def join_kernel(r0, r1, r2, r3, out_ref):
    for b, ref in enumerate((r0, r1, r2, r3)):
        out_ref[b] = ref[ref.shape[0] - QUART :, :]


def quarter_home(parts, after=()):
    return join([parts[0]] + [trade("seq", b)(parts[b]) for b in (1, 2, 3)], after)


def join(got, after=()):
    return call(
        join_kernel, "join", (1,), got, [whole(a.shape) for a in got],
        [sds((GRP, QUART, D), BF16)], [whole((GRP, QUART, D))], after=after,
    )[0]


def all_home(a):
    x = trade("head", 2)(a)
    return a, x, trade("head", 1)(a), trade("head", 1)(x)


def shards(
    block_in, cotangent, lengths,
    norm_gain, in_proj, conv_params, head_params, gate_gain, out_proj,
    norm_gain_momentum, in_proj_momentum, conv_momentum, head_momentum, gate_gain_momentum,
    out_proj_momentum,
    norm_gain_average, in_proj_average, conv_average, head_average, gate_gain_average,
    out_proj_average,
):
    seq_at, head_at = lax.axis_index("seq"), lax.axis_index("head")
    place = seq_at % GRP
    groups = lax.axis_size("seq") // GRP
    group = seq_at // GRP
    at = [place, head_at % 2, group, 0, head_at // 2, group > 0, group < groups - 1]
    at = jnp.concatenate([jnp.stack([jnp.asarray(v, jnp.int32) for v in at]), lengths])

    def turned(array):
        return jnp.transpose(array, (2, 1, 0))

    once = lengths[0] >= 0

    def apart(step):
        shapes = jax.eval_shape(step)
        return lax.cond(
            once, step, lambda: jax.tree.map(lambda s: jnp.zeros(s.shape, s.dtype), shapes)
        )

    anyspec = pl.BlockSpec(memory_space=pl.ANY)

    picked = pick(at, block_in, True)
    got = [picked[0]] + [trade("seq", b)(picked[b]) for b in (1, 2, 3)]
    w, wdt, low, send_bc, hp, vecs = call(
        prep_kernel, "prep", (1,),
        (turned(in_proj), out_proj, conv_params, head_params, norm_gain, gate_gain),
        [anyspec, whole((ZW, D)), whole((5, 1, 448)), whole((3, NH)), whole((D,)), whole((ZW,))],
        [sds((WROWS, D), BF16), sds((LANES, D), BF16), sds((ZW, D), BF16), sds((80, D), BF16),
         sds((8, LANES)), sds((8, D))],
        [whole((WROWS, D)), whole((LANES, D)), whole((ZW, D)), whole((80, D)), whole((8, LANES)), whole((8, D))],
        scratch=[pltpu.VMEM((COLS, D), F32), pltpu.VMEM((8, LANES), F32), pltpu.SemaphoreType.DMA],
        after=(picked[0],),
    )
    bcs = [send_bc] + [trade("head", b)(send_bc) for b in (1, 2, 3)]
    own, edge = stack(at, got, (w,))
    oth = trade("head", 1)(own)
    halo = moved(edge, GRP)
    cot_picked = pick(at, cotangent, False, (own,))
    cot_got = [cot_picked[0]] + [trade("seq", b)(cot_picked[b]) for b in (1, 2, 3)]

    def wblock(n, height):
        return pl.BlockSpec((height, D), lambda i, *_: (n, 0))

    nrm, z, info, rowc, logs = call(
        first_kernel, "first", (GRP,), (own, oth, vecs, w, wdt, hp),
        [slot(HALF), slot(HALF), whole((8, D)), wblock(0, ZW), whole((LANES, D)), whole((8, LANES))],
        [sds((TOK, D), BF16), sds((TOK, ZW)), sds((TOK, LANES)), sds((8, TOK)), sds((8, LANES))],
        [rows(D), rows(ZW), rows(LANES), pl.BlockSpec((8, BLK), lambda i, *_: (0, i)), whole((8, LANES))],
        scratch=[pltpu.VMEM((8, LANES), F32)], prefetch=at, flops=2 * TOK * D * 512, after=(halo, *bcs[1:]),
    )
    hspec = pl.BlockSpec((1, ZW, ST), lambda i, *_: (i, 0, 0))
    rowspec = pl.BlockSpec((8, BLK), lambda i, *_: (0, i))
    mx, px, xa, xdt, mo, po, bb, cc, hloc, fresh = call(
        mix_kernel, "mix", (GRP,), (nrm, halo, vecs, w, w, *bcs, conv_params, info),
        [rows(D), whole((16, D)), whole((8, D)), wblock(1, ZW), wblock(12, 2 * SW)]
        + [whole((80, D))] * 4 + [whole((5, 1, 448)), rows(LANES)],
        [sds((TOK, ZW)), sds((TOK, ZW)), sds((TOK, ZW)), sds((TOK, ZW), BF16), sds((TOK, 2 * SW)),
         sds((TOK, 2 * SW)), sds((TOK, ST), BF16), sds((TOK, ST), BF16), sds((GRP, ZW, ST)),
         sds((ZW, ST), BF16)],
        [rows(ZW), rows(ZW), rows(ZW), rows(ZW), rows(2 * SW), rows(2 * SW), rows(ST), rows(ST),
         hspec, whole((ZW, ST))],
        scratch=[pltpu.VMEM((2 * ST, D), BF16), pltpu.VMEM((8, 2 * ST), F32),
                 pltpu.VMEM((BLK + 8, ZW + 2 * ST), F32), pltpu.VMEM((BLK + 8, 2 * SW), F32),
                 pltpu.VMEM((ZW, ST), F32)],
        flops=2 * TOK * D * 704, prefetch=at,
    )
    hin = pieces_before(fresh, logs, 1)
    cot_own = stack(at, cot_got, (fresh,))[0]
    cot_oth = trade("head", 1)(cot_own)
    yl, dyn, w_live = call(
        local_kernel, "local", (GRP,),
        (xdt, xa, bb, cc, info, rowc, hloc, cot_own, cot_oth, low, vecs),
        [rows(ZW), rows(ZW), rows(ST), rows(ST), rows(LANES), rowspec, hspec, slot(HALF),
         slot(HALF), whole((ZW, D)), whole((8, D))],
        [sds((TOK, ZW)), sds((TOK, ZW)), sds((TOK, D), BF16)], [rows(ZW), rows(ZW), rows(D)],
        prefetch=at, flops=2 * TOK * (D * ZW + 4 * BLK * ZW),
    )
    y, sums = call(
        gate_kernel, "gate", (GRP,), (yl, cc, info, hin, z, dyn, vecs),
        [rows(ZW), rows(ST), rows(LANES), whole((ZW, ST)), rows(ZW), rows(ZW), whole((8, D))],
        [sds((TOK, ZW)), sds((8, TOK))], [rows(ZW), rowspec], prefetch=at, flops=2 * TOK * ST * ZW,
    )
    all_sums = [sums] + [trade("head", b)(sums) for b in (1, 2, 3)]
    half_slot = pl.BlockSpec((1, HALF, D), lambda i, at: (i ^ at[0], 0, 0))
    dy, dz, yn, pulled, g_gate, keep, send = call(
        ungate_kernel, "ungate", (GRP,), (y, z, dyn, *all_sums, info, cc, vecs, low),
        [rows(ZW)] * 3 + [rowspec] * 4 + [rows(LANES), rows(ST), whole((8, D)), whole((ZW, D))],
        [sds((TOK, ZW)), sds((TOK, ZW), BF16), sds((TOK, ZW), BF16), sds((ZW, ST), BF16), sds((8, ZW))]
        + [sds((GRP, HALF, D), BF16)] * 2,
        [rows(ZW), rows(ZW), rows(ZW), whole((ZW, ST)), whole((8, ZW))] + [half_slot] * 2,
        scratch=[pltpu.VMEM((ZW, ST), F32)], flops=2 * TOK * (ST + D) * ZW, prefetch=at,
    )
    grads1 = call(
        out_kernel, "out", (GRP,), (yn, w_live, nrm, dz), [rows(ZW), rows(D), rows(D), rows(ZW)],
        [sds((SEG1, D), BF16)] * 4, [whole((SEG1, D))] * 4,
        scratch=[pltpu.VMEM((2 * ZW, D), F32)], prefetch=at, flops=4 * TOK * D * ZW,
    )
    got1 = [trade("seq", b)(grads1[b]) for b in (1, 2, 3)]
    keep2, send2 = split_both(at, keep, trade("head", 1)(send), (grads1[0],))
    other2 = trade("head", 2)(send2)
    hback = pl.BlockSpec((1, ZW, ST), lambda i, *_: (GRP - 1 - i, 0, 0))

    after = pieces_before(pulled, logs, -1)
    dxi, dbi, dci, dcum, hall = call(
        inner_kernel, "inner", (GRP,), (xdt, bb, cc, info, rowc, dy, hloc, hin),
        [rows(ZW), rows(ST), rows(ST), rows(LANES), rowspec, rows(ZW), hspec, whole((ZW, ST))],
        [sds((TOK, ZW)), sds((TOK, ST)), sds((TOK, ST)), sds((TOK, LANES)), sds((GRP, ZW, ST))],
        [rows(ZW), rows(ST), rows(ST), rows(LANES), hspec], prefetch=at, after=(send2,),
    )
    dpx, halo_x, *dbc, draw, g_head = call(
        back_kernel, "back", (GRP,),
        (after, dxi, dbi, dci, dcum, hall, xa, px, bb, cc, info, dy, hp, vecs),
        [whole((ZW, ST)), rows_back(ZW), rows_back(ST), rows_back(ST), rows_back(LANES), hback,
         rows_back(ZW), rows_back(ZW), rows_back(ST), rows_back(ST), rows_back(LANES),
         rows_back(ZW), whole((8, LANES)), whole((8, D))],
        [sds((TOK, ZW)), sds((8, ZW))] + [sds((TOK // 2, LANES), BF16)] * 4 + [sds((TOK, LANES), BF16), sds((8, LANES))],
        [rows_back(ZW), whole((8, ZW))] + [rows_back(LANES, HALF)] * 4 + [rows_back(LANES), whole((8, LANES))],
        scratch=[pltpu.VMEM((ZW, ST), F32)], flops=2 * TOK * 4 * ST * ZW, prefetch=at,
    )
    quarters = quarter_add(keep2, other2, (g_head,))
    one, joint = whole((SEG1, D)), whole((SEG1 + QUART, D))

    def after_rows(width):
        last = TOK // 8 - 1
        return pl.BlockSpec((8, width), lambda i, *_: (min((i + 1) * (BLK // 8), last) if isinstance(i, int) else jnp.minimum((i + 1) * (BLK // 8), last), 0))

    final = GRP * SEG2
    half_rows = pl.BlockSpec((1, HALF, D), lambda i, at: (i ^ at[0], 0, 0))

    bc_got = [trade("head", b)(dbc[b]) for b in (1, 2, 3)]
    pb, end, acc = call(
        last_x_kernel, "last_x", (GRP,),
        (dpx, dpx, mx, conv_params, dz, draw, nrm, w, wdt),
        [rows(ZW), after_rows(ZW), rows(ZW), whole((5, 1, 448)), rows(ZW), rows(LANES),
         rows(D), whole((2 * ZW, D)), whole((LANES, D))],
        [sds((TOK, D)), sds((END, ZW)), sds((final, D))], [rows(D), whole((END, ZW)), whole((final, D))],
        scratch=[pltpu.VMEM((BLK + 8, ZW), F32)], prefetch=at, flops=4 * TOK * D * 2 * ZW, after=(quarters[0],),
    )
    dpo, halo_o = call(
        edge_kernel, "edge", (GRP,), (dbc[0], *bc_got, po, halo_x),
        [rows(LANES, HALF)] * 4 + [rows(2 * SW), whole((8, ZW))],
        [sds((TOK, 2 * SW)), sds((8, ZW + LANES))], [rows(2 * SW), whole((8, ZW + LANES))], after=(acc,),
    )
    halo_o = moved(halo_o, -GRP)
    mine1 = add_rows(SEG1, [grads1[0], *got1], (halo_o,))
    keep_b, send_b, *grads2 = call(
        last_o_kernel, "last_o", (GRP,),
        (dpo, dpo, halo_o, mo, conv_params, nrm, w, w, pb, vecs, g_gate, g_head, acc, end, mx),
        [rows(2 * SW), after_rows(2 * SW), whole((8, ZW + LANES)), rows(2 * SW), whole((5, 1, 448)), rows(D),
         wblock(12, 2 * SW), wblock(1, ZW), rows(D), whole((8, D)), whole((8, ZW)), whole((8, LANES)), whole((final, D)),
         whole((END, ZW)), pl.BlockSpec((END, ZW), lambda i, *_: (TOK // END - 1, 0))],
        [sds((GRP, HALF, D), BF16)] * 2 + [sds((SEG2, D), BF16)] * 4,
        [half_rows] * 2 + [whole((SEG2, D))] * 4,
        scratch=[pltpu.VMEM((BLK + 8, 2 * SW), F32), pltpu.VMEM((final, D), F32), pltpu.VMEM((BLK, D), F32)],
        prefetch=at, flops=4 * TOK * D * 2 * SW, after=(mine1,),
    )

    def finish():
        keep3, send3 = split_both(at, keep_b, trade("head", 1)(send_b))
        quarters_b = quarter_add(keep3, trade("head", 2)(send3))
        mine2 = group_sum(grads2, SEG2, (quarters_b[0],))
        own = quarter_home(quarters, (mine2,))
        return quarters_b, mine2, own, across_groups(mine1, SEG1, (own,))

    quarters_b, mine2, own_out, total1 = apart(finish)
    x_out = trade("head", 2)(own_out)
    root = math.sqrt(TOK * lax.axis_size("seq"))
    mat = whole((ZW, D))
    turned3 = [turned(p) for p in (in_proj, in_proj_momentum, in_proj_average)]
    turned_shape = [sds((COLS, 1, D))] * 3
    buffers = [pltpu.VMEM((COLS, D), F32)] * 6 + [pltpu.SemaphoreType.DMA((5, 6))]
    hbm = pl.BlockSpec(memory_space=pltpu.HBM)

    def gather():
        own_grad = quarter_home(quarters_b)
        return own_grad, across_groups(mine2, SEG2, (own_grad,))

    own_grad, total2 = apart(gather)
    sums1 = all_quarters(total1)
    def spread_out():
        x_grad = trade("head", 2)(own_grad)
        core_grad, sums2 = trade("head", 1)(own_grad), all_quarters(total2)
        parts = (own_out, x_out, trade("head", 1)(own_out), trade("head", 1)(x_out))
        block_out, _ = home(home_out_kernel, "home_out", at, (block_in,), (None,), parts, BF16)
        return x_grad, core_grad, sums2, block_out

    x_grad, core_grad, sums2, block_out = apart(spread_out)
    grad_parts = (own_grad, x_grad, core_grad, trade("head", 1)(x_grad))

    quarter = whole((SEG2, D))
    small, norm = call(
        small_kernel, "small", (1,), sums2, [quarter] * 4, [sds((SMALL, D)), sds((8, D))],
        [whole((SMALL, D)), whole((8, D))], prefetch=at,
    )
    eight = whole((8, D))
    norm = call(
        add_small_kernel, "add_small", (1,), (norm, trade("head", 1)(norm)), [eight] * 2, [sds((8, D))], [eight]
    )[0]
    norms = [norm, trade("head", 2)(norm)]
    *in_half, done_b = call(
        functools.partial(update_b_kernel, rate=RATES[1] / root), "update_b", (1,),
        (*sums2, *turned3), [quarter] * 4 + [hbm] * 3, turned_shape, [hbm] * 3,
        scratch=[pltpu.VMEM((GRP * SEG2, D), F32)] + buffers, prefetch=at,
        after=(norm,), vmem=56, token=True,
    )
    input_grad, done_grad = home(
        home_grad_kernel, "home_grad", at, (block_in, cotangent, vecs), (None, None, (8, D)),
        grad_parts, F32, (done_b,),
    )
    out_w, out_m, out_a, *in_new, done_a = call(
        functools.partial(update_a_kernel, rate=RATES[5] / root, rate_in=RATES[1] / root), "update_a", (1,),
        (*sums1, out_proj, out_proj_momentum, out_proj_average, *turned3, *in_half),
        [one] * 4 + [mat] * 3 + [hbm] * 6, [sds((ZW, D))] * 3 + turned_shape,
        [mat] * 3 + [hbm] * 3, scratch=[pltpu.VMEM((2 * ZW, D), F32)] + buffers, prefetch=at,
        after=(done_grad,), aliases={11: 3, 12: 4, 13: 5}, vmem=56, token=True,
    )
    groups_of = (
        (norm_gain, norm_gain_momentum, norm_gain_average),
        (conv_params, conv_momentum, conv_average),
        (head_params, head_momentum, head_average),
        (gate_gain, gate_gain_momentum, gate_gain_average),
    )
    arrays = [a for three in groups_of for a in three]
    specs = [whole(a.shape) for a in arrays]
    new = call(
        functools.partial(update_small_kernel, rates=[r / root for r in RATES]), "update_small", (1,),
        (small, *norms, *arrays), [whole((SMALL, D))] + [whole((8, D))] * 2 + specs,
        [sds(a.shape) for a in arrays], specs, after=(done_a,),
    )
    ng3, cv3, hd3, gg3 = (tuple(new[3 * n : 3 * n + 3]) for n in range(4))
    in3 = tuple(turned(a) for a in in_new)
    return (block_out, input_grad, *ng3, *in3, *cv3, *hd3, *gg3, out_w, out_m, out_a)


def solution(mesh):
    act, vec, mat = P(None, "seq", None), P(), P(None, "head", None)
    weights = (vec, mat, mat, P(None, "head"), P("head"), P("head", None))
    outs = tuple(spec for spec in weights for _ in range(3))
    return jax.shard_map(
        shards,
        mesh=mesh,
        in_specs=(act, act, P(), *weights, *weights, *weights),
        out_specs=(act, act, *outs),
        check_vma=False,
    )
```

```python
import functools
import math

import jax
import jax.numpy as jnp
from jax import lax
from jax.experimental import pallas as pl
from jax.experimental.pallas import tpu as pltpu
from jax.sharding import PartitionSpec as P

HDIM = 64
CONV = 4
INNER = 1536
EPSILON = 1e-05
MOMENTUM = 0.5
AVERAGE = 0.5
RATES = (0.15, 0.1, 0.5, 0.05, 0.15, 0.02)
HIGHEST = lax.Precision.HIGHEST
F32 = jnp.float32
BF16 = jnp.bfloat16
VMEM = 14
GRP = 4
BLK = 256
HALF = BLK // 2
QUART = BLK // 4
D = 768
ZW = 384
NH = 6
ST = 128
SW = 32
LANES = 128
WCOLS = D // LANES
WROWS = 2 * ZW + 2 * SW
TOK = GRP * BLK
COLS = WROWS + NH
SEG1 = 2 * ZW // GRP
SEG2 = 120
BC_AT, DT_AT, TAP_AT, HD_AT, GG_AT, NG_AT = 384, 448, 456, 464, 472, 473


def nt(a, b, precision=None):
    return lax.dot_general(
        a, b, (((1,), (1,)), ((), ())), preferred_element_type=F32, precision=precision
    )


def nn(a, b, precision=None):
    return lax.dot_general(
        a, b, (((1,), (0,)), ((), ())), preferred_element_type=F32, precision=precision
    )


def tn(a, b, precision=None):
    return lax.dot_general(
        a, b, (((0,), (0,)), ((), ())), preferred_element_type=F32, precision=precision
    )


def iota(shape, dim):
    return lax.broadcasted_iota(jnp.int32, shape, dim)


def split3(value):
    high = value.astype(BF16).astype(F32)
    rest = value - high
    mid = rest.astype(BF16).astype(F32)
    return high, mid, rest - mid


def side_by_side(value, used):
    high, mid, low = split3(jnp.where(iota(value.shape, 1) < used, value, 0.0))
    return (high + pltpu.roll(mid, used, 1) + pltpu.roll(low, 2 * used, 1)).astype(BF16)


def widen(packed, kinds):
    lane, col = iota((LANES, ZW), 0), iota((LANES, ZW), 1)
    goals = [((lane % 32 == col // HDIM + 8 * k) & (lane < 96)).astype(BF16) for k in kinds]
    parts = side_by_side(packed, 32)
    return [nn(parts, goal) for goal in goals]


def head_sums(values):
    goal = (iota((ZW, LANES), 1) == iota((ZW, LANES), 0) // HDIM).astype(BF16)
    high = values.astype(BF16)
    return nn(high, goal) + nn((values - high.astype(F32)).astype(BF16), goal)


def running_sums(triangle, values):
    total = nn(triangle, side_by_side(values, 8))
    total = total + pltpu.roll(total, LANES - 8, 1) + pltpu.roll(total, LANES - 16, 1)
    return jnp.where(iota(total.shape, 1) < 8, total, 0.0)


def lane_mask(which):
    return (iota((1, LANES), 1) // HDIM == which).astype(BF16)


def triangle(lower):
    row, col = iota((BLK, BLK), 0), iota((BLK, BLK), 1)
    return (row >= col if lower else row <= col).astype(BF16)


def call(
    kernel, name, grid, ins, in_specs, outs, out_specs, scratch=(), prefetch=None, flops=0,
    aliases=None, after=(), vmem=VMEM, light=False, token=False,
):
    count = len(ins) + (prefetch is not None)
    results = len(outs)
    if grid == (GRP,) and name not in STREAMED:
        plain, pre, cuts = kernel, count - len(ins), list(in_specs) + list(out_specs)
        used = pre + len(cuts)

        def kernel(*refs):
            at = refs[:pre]

            def step(i):
                views = [part_of(r, c, i, at) for r, c in zip(refs[pre:used], cuts)]
                STEP.append(i)
                plain(*at, *views, *refs[used:])
                STEP.pop()

            def two_steps(k, carry):
                step(2 * k)
                step(2 * k + 1)
                return carry

            if name in BY_TWOS:
                lax.fori_loop(0, GRP // 2, two_steps, 0)
            else:
                for i in range(GRP):
                    step(i)

        grid = (1,)
        in_specs, out_specs = [whole(a.shape) for a in ins], [whole(a.shape) for a in outs]

    def body(*refs):
        rest = refs[count + len(after) :]
        if token:
            rest[results][...] = jnp.zeros((8, LANES), F32)
            rest = rest[:results] + rest[results + 1 :]
        kernel(*refs[:count], *rest)

    outs, out_specs = list(outs), list(out_specs)
    if token:
        outs.append(sds((8, LANES)))
        out_specs.append(whole((8, LANES)))
    nbytes = sum(math.prod(a.shape) * a.dtype.itemsize for a in (*ins, *outs))
    if light:
        flops, nbytes = 1024, 1024
    spec = pltpu.PrefetchScalarGridSpec(
        num_scalar_prefetch=0 if prefetch is None else 1,
        grid=grid,
        in_specs=list(in_specs) + [token_spec(a) for a in after],
        out_specs=out_specs,
        scratch_shapes=scratch,
    )
    return pl.pallas_call(
        body,
        grid_spec=spec,
        out_shape=outs,
        compiler_params=pltpu.CompilerParams(
            dimension_semantics=("arbitrary",) * len(grid), vmem_limit_bytes=vmem << 20
        ),
        cost_estimate=pl.CostEstimate(flops=flops, bytes_accessed=nbytes, transcendentals=0),
        input_output_aliases=aliases or {},
        name=name,
    )(*(() if prefetch is None else (prefetch,)), *ins, *after)


def token_spec(array):
    return whole((8, LANES)) if array.shape == (8, LANES) else pl.BlockSpec(memory_space=pl.ANY)


STEP = []
BY_TWOS = ("inner", )
STREAMED = ("home_out", "home_grad", "split", "gate", "edge", "last_x", )


def step_now():
    return STEP[-1] if STEP else pl.program_id(0)


def when(condition):
    if isinstance(condition, bool):
        return lambda body: body() if condition else None
    return pl.when(condition)


def part_of(ref, spec, i, at):
    size = spec.block_shape
    if size is None or tuple(size) == tuple(ref.shape):
        return ref
    cut = []
    for n, length, full in zip(spec.index_map(i, *at), size, ref.shape):
        if length == full:
            cut.append(slice(None))
        elif isinstance(n, int):
            cut.append(pl.ds(n * length, length))
        else:
            cut.append(pl.ds(pl.multiple_of(n * length, length), length))
    return ref.at[tuple(cut)]


def sds(shape, dtype=F32):
    return jax.ShapeDtypeStruct(shape, dtype)


def whole(shape):
    return pl.BlockSpec(shape, lambda *_: (0,) * len(shape))


def rows(width, height=BLK):
    return pl.BlockSpec((height, width), lambda i, *_: (i, 0))


def rows_back(width, height=BLK):
    return pl.BlockSpec((height, width), lambda i, *_: (GRP - 1 - i, 0))


def slot(height, width=D):
    return pl.BlockSpec((1, height, width), lambda i, at: (i ^ at[0], 0, 0))


def pick_kernel(at, *refs):
    for n, goal in enumerate(refs[2 * GRP :]):
        goal[0:HALF, :] = refs[n][0]
        if goal.shape[0] > HALF:
            goal[HALF:, :] = refs[GRP + n][0]


def pick(at, array, edge, after=()):
    def half_of(b):
        return pl.BlockSpec((1, HALF, D), lambda i, at: (at[0] ^ b, at[1], 0))

    def edge_of(b):
        return pl.BlockSpec((1, 16, D), lambda i, at: (at[0] ^ b, BLK // 16 - 1, 0))

    size = HALF + 16 * edge
    specs = [half_of(b) for b in range(GRP)] + [edge_of(b) for b in range(GRP)]
    return call(
        pick_kernel, "pick", (1,), (array,) * (2 * GRP), specs,
        [sds((size, D), BF16)] * GRP, [whole((size, D))] * GRP, prefetch=at, after=after,
    )


def stack_kernel(at, r0, r1, r2, r3, out_ref, *edge):
    refs = (r0, r1, r2, r3)
    for b, ref in enumerate(refs):
        out_ref[b] = ref[0:HALF, :]
    for goal in edge:
        for b, ref in enumerate(refs):

            @when(at[0] ^ b == GRP - 1)
            def _():
                goal[...] = ref[HALF:, :]


def stack(at, parts, after=()):
    size = parts[0].shape[0]
    outs, specs = [sds((GRP, HALF, D), BF16)], [whole((GRP, HALF, D))]
    if size > HALF:
        outs, specs = outs + [sds((16, D), BF16)], specs + [whole((16, D))]
    return call(
        stack_kernel, "stack", (1,), parts, [whole((size, D))] * GRP, outs, specs, prefetch=at, after=after
    )


def prep_kernel(
    win, wout, taps, heads, ng, gg,
    w_ref, wdt_ref, low_ref, send_ref, hp_ref, vec_ref, wide_w, scr, sem,
):
    copy = pltpu.make_async_copy(win.at[:, 0, :], wide_w, sem)
    copy.start()
    low_ref[...] = wout[...].astype(BF16)
    scr[...] = jnp.zeros_like(scr)
    scr[0:3, 0:NH] = heads[...]
    lanes = scr[...]
    for by in (8, 16, 32, 64):
        lanes = lanes + pltpu.roll(lanes, by, 1)
    hp_ref[...] = lanes
    vec_ref[...] = jnp.zeros_like(vec_ref)
    vec_ref[0:1, :] = ng[...].reshape(1, D)
    vec_ref[1:2, 0:ZW] = gg[...].reshape(1, ZW)
    vec_ref[2:3, 0:ZW] = widen(lanes, (0,))[0][2:3, :]
    copy.wait()
    w_ref[...] = wide_w[0:WROWS, :].astype(BF16)
    last = jnp.concatenate([wide_w[WROWS:, :], jnp.zeros((8 - NH, D), F32)], axis=0)
    wdt_ref[...] = jnp.concatenate([last] * 16, axis=0).astype(BF16)
    send_ref[0 : 2 * SW, :] = w_ref[2 * ZW : WROWS, :]
    own = taps[:, 0, :][:, ZW:]
    high = own.astype(BF16).astype(F32)
    mid = (own - high).astype(BF16).astype(F32)
    low = own - high - mid
    parts = jnp.concatenate([high, mid, low, jnp.zeros((1, 2 * SW), F32)], axis=0)
    send_ref[2 * SW :, :] = jnp.zeros((16, D), BF16)
    send_ref[2 * SW :, 0 : 2 * SW] = parts.astype(BF16)


def chunk_of(own_ref, oth_ref, core):
    own, oth = own_ref[0], oth_ref[0]
    first = core == 0
    return jnp.concatenate([jnp.where(first, own, oth), jnp.where(first, oth, own)], axis=0)


def normalise(x, gain):
    u = x.astype(F32)
    scale = lax.rsqrt(jnp.mean(u * u, axis=-1, keepdims=True) + EPSILON)
    return (u * scale * gain).astype(BF16)


def first_kernel(at, own, oth, vecs, wz, wdt, hp, nrm_ref, z_ref, info_ref, row_ref, tot_ref, cum):
    step = step_now()

    @when(step == 0)
    def _():
        cum[...] = jnp.zeros_like(cum)

    normed = normalise(chunk_of(own, oth, at[1]), vecs[0:1, :])
    nrm_ref[...] = normed
    z_ref[...] = nt(normed, wz[...])
    biased = nt(normed, wdt[...]) + hp[0:1, :]
    steps = jax.nn.softplus(biased)
    decays = -jnp.exp(hp[1:2, :]) * steps
    c = running_sums(triangle(True), decays)
    group = iota((BLK, LANES), 1) // 8
    info = jnp.where(group == 0, c, jnp.where(group == 1, steps, biased))
    moved_c = pltpu.roll(c, 24, 1) + cum[0:1, :]
    info_ref[...] = jnp.where(group == 3, moved_c, info)
    row_ref[...] = jnp.transpose(c)[0:8, :]
    cum[0:1, :] = moved_c[BLK - 1 : BLK, :]
    tot_ref[...] = jnp.broadcast_to(cum[0:1, :], (8, LANES))


def mix_kernel(
    at, nrm, halo, vecs, wx, wo, bc0, bc1, bc2, bc3, taps, info,
    mx_ref, px_ref, xa_ref, xdt_ref, mo_ref, po_ref, b_ref, c_ref, h_ref, s_ref,
    wbc, tbc, ext, exto, state,
):
    step = step_now()
    tap = taps[:, 0, :]

    @when(step == 0)
    def _():
        place = jnp.zeros((16, 2 * ST), F32)
        for b, buf in enumerate((bc0, bc1, bc2, bc3)):
            wbc[SW * b : SW * (b + 1), :] = buf[0:SW, :]
            wbc[ST + SW * b : ST + SW * (b + 1), :] = buf[SW : 2 * SW, :]
            at_row, at_col = iota((2 * SW, 2 * ST), 0), iota((2 * SW, 2 * ST), 1)
            goal = jnp.where(at_row < SW, SW * b + at_row, ST + SW * b + at_row - SW)
            put = (at_col == goal).astype(BF16)
            place = place + nn(buf[2 * SW :, 0 : 2 * SW], put)
        tbc[0:5, :] = place[0:5] + place[5:10] + place[10:15]
        before = normalise(jnp.where(at[5] > 0, halo[...], 0.0).astype(BF16), vecs[0:1, :])
        ext[0:8, 0:ZW] = nt(before, wx[...])[8:16]
        ext[0:8, ZW:] = nt(before, wbc[...])[8:16]
        exto[0:8, :] = nt(before, wo[...])[8:16]
        state[...] = jnp.zeros_like(state)

    normed = nrm[...]
    mixed = nt(normed, wx[...])
    mx_ref[...] = mixed
    ext[8:, 0:ZW] = mixed
    ext[8:, ZW:] = nt(normed, wbc[...])
    own = nt(normed, wo[...])
    mo_ref[...] = own
    exto[8:, :] = own
    pre = tap[4:5, 0:ZW]
    pre_bc = tbc[4:5, :]
    pre_o = tap[4:5, ZW:]
    for k in range(CONV):
        pre = pre + tap[k : k + 1, 0:ZW] * ext[5 + k : 5 + k + BLK, 0:ZW]
        pre_bc = pre_bc + tbc[k : k + 1, :] * ext[5 + k : 5 + k + BLK, ZW:]
        pre_o = pre_o + tap[k : k + 1, ZW:] * exto[5 + k : 5 + k + BLK, :]
    px_ref[...] = pre
    po_ref[...] = pre_o
    x = pre * jax.nn.sigmoid(pre)
    xa_ref[...] = x
    bc = (pre_bc * jax.nn.sigmoid(pre_bc)).astype(BF16)
    b_ref[...] = bc[:, 0:ST]
    c_ref[...] = bc[:, ST:]
    ext[0:8, :] = ext[BLK:, :]
    exto[0:8, :] = exto[BLK:, :]

    packed = info[...]
    c = packed[:, 0:LANES]
    keep = iota((BLK, LANES), 1) < 8
    tail = jnp.where(keep, jnp.exp(jnp.where(keep, c[BLK - 1 : BLK, :] - c, 0.0)), 0.0)
    tail_wide, dt_wide = widen(jnp.where(keep, tail, packed), (0, 1))
    xdt = x * dt_wide
    xdt_ref[...] = xdt.astype(BF16)
    fresh = tn((xdt * tail_wide).astype(BF16), bc[:, 0:ST])
    h_ref[0] = state[...]
    for h in range(NH):
        decay = jnp.exp(packed[BLK - 1 : BLK, h : h + 1])
        at = pl.ds(HDIM * h, HDIM)
        state[at, :] = decay * state[at, :] + fresh[HDIM * h : HDIM * (h + 1), :]
    s_ref[...] = state[...].astype(BF16)


def weights_of(h, packed, row, causal):
    diff = packed[:, h : h + 1] - row[h : h + 1, :]
    return jnp.where(causal, jnp.exp(jnp.where(causal, diff, 0.0)), 0.0)


def local_kernel(
    at, xdt, xa, b, c, info, row, hloc, own, oth, low, vecs, yl_ref, dyn_ref, w_ref
):
    step = step_now()
    packed = info[...]
    rowc = row[...]
    causal = iota((BLK, BLK), 0) >= iota((BLK, BLK), 1)
    scores = nt(c[...], b[...])
    c_exp = jnp.exp(jnp.where(iota((BLK, LANES), 1) < 8, packed, 0.0))
    carried = nt(c[...], hloc[0].astype(BF16)) * widen(c_exp, (0,))[0]
    carried = carried + vecs[2:3, 0:ZW] * xa[...]
    for p in range(NH // 2):
        x = xdt[:, LANES * p : LANES * (p + 1)]
        total = carried[:, LANES * p : LANES * (p + 1)]
        for q in range(2):
            weights = (weights_of(2 * p + q, packed, rowc, causal) * scores).astype(BF16)
            total = total + nn(weights, x * lane_mask(q))
        yl_ref[:, LANES * p : LANES * (p + 1)] = total
    place = (at[2] * GRP + step) * BLK + iota((BLK, 1), 0)
    live = place < at[7 + at[0]]
    w = jnp.where(live, chunk_of(own, oth, at[1]), 0.0).astype(BF16)
    w_ref[...] = w
    dyn_ref[...] = nt(w, low[...])


def gate_kernel(at, yl, c, info, hin, z, dyn, vecs, y_ref, sum_ref):
    packed = info[...]
    lane = iota((BLK, LANES), 1)
    cum = jnp.where(lane // 8 == 3, jnp.exp(jnp.where(lane // 8 == 3, packed, 0.0)), 0.0)
    entering = jnp.where(at[5] > 0, hin[...], 0.0).astype(BF16)
    y = yl[...] + nt(c[...], entering) * widen(cum, (3,))[0]
    y_ref[...] = y
    gate = z[...]
    g = y * (gate * jax.nn.sigmoid(gate))
    squares = jnp.sum(g * g, axis=-1, keepdims=True)
    inner = jnp.sum(dyn[...] * vecs[1:2, 0:ZW] * g, axis=-1, keepdims=True)
    both = jnp.where(lane == 0, squares, jnp.where(lane == 1, inner, 0.0))
    sum_ref[...] = jnp.transpose(both)[0:8, :]


def ungate_kernel(
    at, y, z, dyn, s0, s1, s2, s3, info, c, vecs, low,
    dy_ref, dz_ref, yn_ref, p_ref, gg_ref, keep_ref, send_ref, acc,
):
    step = step_now()

    @when(step == 0)
    def _():
        acc[...] = jnp.zeros_like(acc)
        gg_ref[...] = jnp.zeros_like(gg_ref)

    sums = s0[...] + s1[...] + s2[...] + s3[...]
    sums = jnp.transpose(jnp.concatenate([sums, jnp.zeros((LANES - 8, BLK), F32)], axis=0))
    q = lax.rsqrt(sums[:, 0:1] / INNER + EPSILON)
    mean = sums[:, 1:2] * q / INNER
    gate = z[...]
    sigma = jax.nn.sigmoid(gate)
    silu = gate * sigma
    out = y[...]
    g = out * silu
    n = g * q
    d = dyn[...]
    gg = vecs[1:2, 0:ZW]
    d_g = q * (d * gg - n * mean)
    d_y = d_g * silu
    dy_ref[...] = d_y
    dz_ref[...] = (d_g * out * sigma * (1.0 + gate * (1.0 - sigma))).astype(BF16)
    yn = (n * gg).astype(BF16)
    yn_ref[...] = yn
    halves(nn(yn, low[...]).astype(BF16), at[1], keep_ref, send_ref)
    gg_ref[0:1, :] += jnp.sum(d * n, axis=0, keepdims=True)
    packed = info[...]
    lane = iota((BLK, LANES), 1)
    cum = jnp.where(lane // 8 == 3, jnp.exp(jnp.where(lane // 8 == 3, packed, 0.0)), 0.0)
    acc[...] += tn((d_y * widen(cum, (3,))[0]).astype(BF16), c[...])
    p_ref[...] = acc[...].astype(BF16)


def halves(value, core, keep_ref, send_ref):
    low, high = value[0:HALF], value[HALF:]
    first = core == 0
    keep_ref[0] = jnp.where(first, low, high)
    send_ref[0] = jnp.where(first, high, low)


def out_kernel(
    at, yn, w, nrm, dz, g0, g1, g2, g3, acc
):
    step = step_now()

    @when(step == 0)
    def _():
        acc[...] = jnp.zeros_like(acc)

    acc[0:ZW, :] += tn(dz[...], nrm[...])
    acc[ZW:, :] += tn(yn[...], w[...])

    @when(step == GRP - 1)
    def _():
        for b, ref in enumerate((g0, g1, g2, g3)):
            start = pl.multiple_of((at[0] ^ b) * SEG1, SEG1)
            ref[...] = acc[pl.ds(start, SEG1), :].astype(BF16)


def inner_kernel(
    at, xdt, b, c, info, row, dy, hloc, hin, dxi_ref, dbi_ref, dci_ref, dcum_ref, hall_ref
):
    packed = info[...]
    rowc = row[...]
    lane = iota((BLK, LANES), 1)
    causal = iota((BLK, BLK), 0) >= iota((BLK, BLK), 1)
    bb, cc = b[...], c[...]
    scores = nt(cc, bb)
    d_scores = jnp.zeros((BLK, BLK), F32)
    d_cum = jnp.zeros((BLK, LANES), F32)
    columns = jnp.zeros((8, BLK), F32)
    row8 = iota((8, BLK), 0)
    dyv = dy[...]
    for p in range(NH // 2):
        x = xdt[:, LANES * p : LANES * (p + 1)]
        d = dyv[:, LANES * p : LANES * (p + 1)].astype(BF16)
        total = jnp.zeros((BLK, LANES), F32)
        for q in range(2):
            h = 2 * p + q
            spans = weights_of(h, packed, rowc, causal)
            d_h = d * lane_mask(q)
            d_spans = nt(d_h, x) * spans
            d_scores = d_scores + d_spans
            both = (d_spans * scores).astype(BF16)
            d_cum = d_cum + nn(both, (lane == h).astype(BF16))
            columns = columns + nn((row8 == h).astype(BF16), both)
            total = total + tn((spans * scores).astype(BF16), d_h)
        dxi_ref[:, LANES * p : LANES * (p + 1)] = total
    columns = jnp.concatenate([columns, jnp.zeros((LANES - 8, BLK), F32)], axis=0)
    d_cum = d_cum - jnp.transpose(columns)
    low_scores = d_scores.astype(BF16)
    c_exp = jnp.exp(jnp.where(lane < 8, packed, 0.0))
    c_wide = widen(c_exp, (0,))[0]
    base = packed[0:1, 24:32] - packed[0:1, 0:8]
    for h in range(NH):
        here = pl.ds(HDIM * h, HDIM)
        grown = jnp.exp(base[:, h : h + 1]) * hin[here, :].astype(F32)
        grown = jnp.where(at[5] > 0, grown, 0.0)
        hall_ref[0, here, :] = hloc[0, here, :] + grown
    entering = hall_ref[0].astype(BF16)
    carried = nt(cc, entering) * c_wide
    d_cum = d_cum + head_sums(dyv * carried)
    dcum_ref[...] = d_cum
    dci_ref[...] = nn(low_scores, bb) + nn((dyv * c_wide).astype(BF16), entering)
    dbi_ref[...] = tn(low_scores, cc)


def back_kernel(
    at, after, dxi, dbi, dci, dcum, hall, xa, px, b, c, info, dy, hp, vecs,
    dpx_ref, halo_ref, o0, o1, o2, o3, draw_ref, hg_ref, state,
):
    step = step_now()

    @when(step == 0)
    def _():
        state[...] = jnp.where(at[6] > 0, after[...].astype(F32), 0.0)
        hg_ref[...] = jnp.zeros_like(hg_ref)

    packed = info[...]
    lane = iota((BLK, LANES), 1)
    first = lane < 8
    c_last = packed[BLK - 1 : BLK, :]
    tail = jnp.where(first, jnp.exp(jnp.where(first, c_last - packed, 0.0)), 0.0)
    c_exp = jnp.where(first, jnp.exp(jnp.where(first, packed, 0.0)), 0.0)
    mixed = jnp.where(first, tail, jnp.where(lane < 16, packed, pltpu.roll(c_exp, 16, 1)))
    tail_wide, dt_wide, c_wide = widen(mixed, (0, 1, 2))
    x = xa[...]
    xdt = x * dt_wide
    d_y = dy[...]
    bb, cc = b[...], c[...]
    low_state = state[...].astype(BF16)
    d_tail = nt(bb, low_state) * tail_wide
    tails = head_sums(xdt * d_tail)
    d_xdt = dxi[...] + d_tail
    d_b = dbi[...] + nn((xdt * tail_wide).astype(BF16), low_state)
    d_c = dci[...]
    ending = jnp.sum(tails, axis=0, keepdims=True)
    lane1 = iota((1, LANES), 1)
    for h in range(NH):
        here = pl.ds(HDIM * h, HDIM)
        inner = jnp.sum(state[here, :] * hall[0, here, :], axis=(0, 1), keepdims=True)
        ending = ending + jnp.where(lane1 == h, inner * jnp.exp(c_last[:, h : h + 1]), 0.0)
    d_cum = dcum[...] - tails
    d_cum = d_cum + jnp.where(iota((BLK, LANES), 0) == BLK - 1, ending, 0.0)
    d_a = running_sums(triangle(False), d_cum)
    fresh = tn((d_y * c_wide).astype(BF16), cc)
    for h in range(NH):
        here = pl.ds(HDIM * h, HDIM)
        decay = jnp.exp(c_last[:, h : h + 1])
        state[here, :] = decay * state[here, :] + fresh[HDIM * h : HDIM * (h + 1), :]
    rate = -jnp.exp(hp[1:2, :])
    d_dt = head_sums(x * d_xdt) + rate * d_a
    biased = pltpu.roll(packed, LANES - 16, 1)
    steps = pltpu.roll(packed, LANES - 8, 1)
    used = lane < NH
    d_raw = jnp.where(used, d_dt * jax.nn.sigmoid(jnp.where(used, biased, 0.0)), 0.0)
    draw_ref[...] = d_raw.astype(BF16)
    hg_ref[0:1, :] += jnp.sum(d_raw, axis=0, keepdims=True)
    g_rate = jnp.where(used, d_a * rate * jnp.where(used, steps, 0.0), 0.0)
    hg_ref[1:2, :] += jnp.sum(g_rate, axis=0, keepdims=True)
    hg_ref[2:3, :] += jnp.sum(head_sums(d_y * x), axis=0, keepdims=True)
    d_x = d_xdt * dt_wide + vecs[2:3, 0:ZW] * d_y
    pre = px[...]
    sigma = jax.nn.sigmoid(pre)
    d_pre = d_x * sigma * (1.0 + pre * (1.0 - sigma))
    dpx_ref[...] = d_pre
    halo_ref[...] = d_pre[0:8]
    for s, ref in enumerate((o0, o1, o2, o3)):
        for n, value in enumerate((d_b, d_c)):
            mine = value[:, SW * s : SW * (s + 1)].astype(BF16)
            ref[:, SW * n : SW * (n + 1)] = mine[0:HALF]
            ref[:, SW * (n + 2) : SW * (n + 3)] = mine[HALF:]


def edge_kernel(o0, r1, r2, r3, po, halo_x, dpo_ref, halo_ref):
    d = o0[...].astype(F32) + r1[...].astype(F32) + r2[...].astype(F32) + r3[...].astype(F32)
    d = jnp.concatenate([d[:, 0 : 2 * SW], d[:, 2 * SW :]], axis=0)
    pre = po[...]
    sigma = jax.nn.sigmoid(pre)
    d = d * sigma * (1.0 + pre * (1.0 - sigma))
    dpo_ref[...] = d

    @when(step_now() == 0)
    def _():
        halo_ref[:, X_LANES] = halo_x[...]
        halo_ref[:, ZW:] = jnp.zeros((8, LANES), F32)
        halo_ref[:, O_LANES] = d[0:8]


def unconvolve(acc, ext, d_pre, follows, values, tap, lanes):
    ext[0:BLK, :] = d_pre
    ext[BLK:, :] = follows
    total = jnp.zeros(d_pre.shape, F32)
    for k in range(CONV):
        shifted = ext[3 - k : 3 - k + BLK, :]
        total = total + tap[k : k + 1, lanes] * shifted
        acc[TAP_AT + k : TAP_AT + k + 1, lanes] += jnp.sum(values * shifted, axis=0, keepdims=True)
    acc[TAP_AT + CONV : TAP_AT + CONV + 1, lanes] += jnp.sum(d_pre, axis=0, keepdims=True)
    return total


X_LANES, O_LANES = slice(0, ZW), slice(ZW, ZW + 2 * SW)


END = 16


def last_x_kernel(
    at, dpx, nx, mx, taps, dz, draw, nrm, w, wdt, pb_ref, end_ref, acc, ext
):
    step = step_now()

    @when(step == 0)
    def _():
        acc[...] = jnp.zeros_like(acc)

    follows = jnp.where(step < GRP - 1, nx[...], 0.0)
    d_mx = unconvolve(acc, ext, dpx[...], follows, mx[...], taps[:, 0, :], X_LANES)
    end_ref[...] = d_mx[BLK - END :, :]
    late = (step == GRP - 1) & (iota((BLK, 1), 0) >= BLK - END)
    p_x = jnp.where(late, 0.0, d_mx).astype(BF16)
    p_t = draw[...]
    pb_ref[...] = nn(dz[...], w[0:ZW, :]) + nn(p_x, w[ZW:, :]) + nn(p_t, wdt[...])
    normed = nrm[...]
    acc[0:ZW, :] += tn(p_x, normed)
    acc[DT_AT : DT_AT + 8, :] += tn(p_t, normed)[0:8]


def last_o_kernel(
    at, dpo, no, halo, mo, taps, nrm, w, wx, pb, vecs, gg, hg, acc_in, end, mxe,
    keep_ref, send_ref, g0, g1, g2, g3, ext, acc, wide_pb,
):
    step = step_now()

    @when(step == 0)
    def _():
        acc[...] = acc_in[...]
        acc[HD_AT : HD_AT + 8, 0:LANES] = hg[...]
        acc[GG_AT : GG_AT + 1, 0:ZW] = gg[0:1, :]

    after = jnp.where(at[6] > 0, halo[...], 0.0)
    follows = jnp.where(step < GRP - 1, no[...], after[:, O_LANES])
    p_o = unconvolve(acc, ext, dpo[...], follows, mo[...], taps[:, 0, :], O_LANES).astype(BF16)
    wide_pb[...] = pb[...] + nn(p_o, w[...])
    normed = nrm[...]

    @when(step == GRP - 1)
    def _():
        rows_after = jnp.concatenate([jnp.zeros((END, ZW), F32), after[:, X_LANES]], axis=0)
        total = end[...]
        for k in range(CONV):
            shifted = rows_after[3 - k : 3 - k + END, :]
            total = total + taps[k : k + 1, 0, X_LANES] * shifted
            grad = jnp.sum(mxe[...] * shifted, axis=0, keepdims=True)
            acc[TAP_AT + k : TAP_AT + k + 1, X_LANES] += grad
        p_x = total.astype(BF16)
        wide_pb[BLK - END :, :] += nn(p_x, wx[...])
        acc[0:ZW, :] += tn(p_x, normed[BLK - END :, :])

    back = wide_pb[...]
    halves(back.astype(BF16), at[1], keep_ref, send_ref)
    acc[NG_AT : NG_AT + 1, :] += jnp.sum(back * normed.astype(F32), axis=0, keepdims=True)
    acc[BC_AT:DT_AT, :] += tn(p_o, normed)

    @when(step == GRP - 1)
    def _():
        acc[NG_AT : NG_AT + 1, :] = acc[NG_AT : NG_AT + 1, :] / vecs[0:1, :]
        for b, ref in enumerate((g0, g1, g2, g3)):
            start = pl.multiple_of((at[0] ^ b) * SEG2, 8)
            ref[...] = acc[pl.ds(start, SEG2), :].astype(BF16)


def split_kernel(at, keep, other, keep_ref, send_ref):
    value = keep[0].astype(F32) + other[0].astype(F32)
    low, high = value[0:QUART], value[QUART:]
    first = at[4] == 0
    keep_ref[0] = jnp.where(first, low, high)
    send_ref[0] = jnp.where(first, high, low).astype(BF16)


def add_kernel(keep, other, r0, r1, r2, r3):
    for b, ref in enumerate((r0, r1, r2, r3)):
        ref[...] = (keep[b] + other[b].astype(F32)).astype(BF16)


def sum_kernel(*refs):
    total = refs[0][...].astype(F32)
    for ref in refs[1:-1]:
        total = total + ref[...].astype(F32)
    refs[-1][...] = total.astype(refs[-1].dtype)


def place_quarters(at, b, parts, scr):
    core, xbit = at[1], at[4]
    for n, ref in enumerate(parts):
        half = core if n < 2 else 1 - core
        quarter = xbit if n % 2 == 0 else 1 - xbit
        start = pl.multiple_of(half * HALF + quarter * QUART, QUART)
        scr[pl.ds(start, QUART), :] = ref[0]


def home_out_kernel(at, block, a, x, ac, xc, out_ref, scr):
    step = step_now()
    place_quarters(at, step, (a, x, ac, xc), scr)
    place = (at[2] * GRP + at[0]) * BLK + iota((BLK, 1), 0)
    live = place < at[7 + step]
    total = block[0].astype(F32) + scr[...].astype(F32)
    out_ref[0] = jnp.where(live, total, 0.0).astype(BF16)


def home_grad_kernel(at, block, cot, vecs, a, x, ac, xc, out_ref, scr):
    step = step_now()
    place_quarters(at, step, (a, x, ac, xc), scr)
    place = (at[2] * GRP + at[0]) * BLK + iota((BLK, 1), 0)
    live = place < at[7 + step]
    u = block[0].astype(F32)
    scale = lax.rsqrt(jnp.mean(u * u, axis=-1, keepdims=True) + EPSILON)
    m = u * scale
    f = scr[...].astype(F32) * vecs[0:1, :]
    inner = jnp.mean(f * m, axis=-1, keepdims=True)
    out_ref[0] = scale * (f - m * inner) + jnp.where(live, cot[0].astype(F32), 0.0)


def home(kernel, name, at, arrays, specs, parts, dtype, after=()):
    full = pl.BlockSpec((1, BLK, D), lambda i, *_: (i, 0, 0))
    part = pl.BlockSpec((1, QUART, D), lambda i, at: (i ^ at[0], 0, 0))
    specs = [full if s is None else whole(s) for s in specs]
    return call(
        kernel, name, (GRP,), (*arrays, *parts), specs + [part] * 4, [sds((GRP, BLK, D), dtype)],
        [full], scratch=[pltpu.VMEM((BLK, D), BF16)], prefetch=at, after=after, token=True,
    )


def advance(weight, gradient, moment, average, rate):
    moment_new = MOMENTUM * moment + gradient
    weight_new = weight - rate * (gradient + MOMENTUM * moment_new)
    average_new = AVERAGE * average + (1.0 - AVERAGE) * weight_new
    return (weight_new, moment_new, average_new)


def stepped(grad, grad_at, weights, outs, blocks, buffers, sems, rate):
    ins, done = buffers[:3], buffers[3:]

    def reads(n):
        start, size = blocks[n]
        return [
            pltpu.make_async_copy(
                w.at[pl.ds(start, size), 0, :], buf.at[pl.ds(start, size), :], sems.at[n, j]
            )
            for j, (w, buf) in enumerate(zip(weights, ins))
        ]

    def writes(n):
        start, size = blocks[n]
        return [
            pltpu.make_async_copy(
                buf.at[pl.ds(start, size), :], o.at[pl.ds(start, size), 0, :], sems.at[n, 3 + j]
            )
            for j, (o, buf) in enumerate(zip(outs, done))
        ]

    for n in range(len(blocks)):
        for copy in reads(n):
            copy.start()
    for n, (start, size) in enumerate(blocks):
        for copy in reads(n):
            copy.wait()
        cut = 16 if size % 16 == 0 else size

        def some(k, carry):
            here = pl.ds(pl.multiple_of(start + k * cut, 8), cut)
            there = pl.ds(pl.multiple_of(grad_at(n) + k * cut, 8), cut)
            new = advance(ins[0][here, :], grad[there, :], ins[1][here, :], ins[2][here, :], rate)
            for buf, value in zip(done, new):
                buf[here, :] = value
            return carry

        lax.fori_loop(0, size // cut, some, 0)
        for copy in writes(n):
            copy.start()
    for n in range(len(blocks)):
        for copy in writes(n):
            copy.wait()


Z_BLOCKS = tuple((96 * n, 96) for n in range(4))
X_BLOCKS = tuple((ZW + 96 * n, 96) for n in range(4)) + ((2 * ZW, COLS - 2 * ZW),)


def update_a_kernel(
    at, g0, g1, g2, g3, w, m, a, wi, mi, ai, x0, x1, x2, w_ref, m_ref, a_ref, wo, mo, ao,
    grad, b0, b1, b2, b3, b4, b5, sems, *, rate, rate_in,
):
    for b, ref in enumerate((g0, g1, g2, g3)):
        grad[pl.ds(pl.multiple_of((at[0] ^ b) * SEG1, SEG1), SEG1), :] = ref[0:SEG1, :].astype(F32)
    stepped(
        grad, lambda n: 96 * n, (wi, mi, ai), (wo, mo, ao), Z_BLOCKS,
        (b0, b1, b2, b3, b4, b5), sems, rate_in,
    )
    w_ref[...], m_ref[...], a_ref[...] = advance(w[...], grad[ZW:, :], m[...], a[...], rate)


def update_b_kernel(
    at, g0, g1, g2, g3, wi, mi, ai, wo, mo, ao,
    grad, b0, b1, b2, b3, b4, b5, sems, *, rate,
):
    for b, ref in enumerate((g0, g1, g2, g3)):
        start = pl.multiple_of((at[0] ^ b) * SEG2, 8)
        grad[pl.ds(start, SEG2), :] = ref[...].astype(F32)
    stepped(
        grad, lambda n: 96 * n, (wi, mi, ai), (wo, mo, ao), X_BLOCKS,
        (b0, b1, b2, b3, b4, b5), sems, rate,
    )


SMALL = GRP * SEG2 - TAP_AT


def small_kernel(at, g0, g1, g2, g3, small_ref, norm_ref):
    for b, ref in enumerate((g0, g1, g2, g3)):

        @when(at[0] ^ b == GRP - 1)
        def _():
            small_ref[...] = ref[SEG2 - SMALL :, :].astype(F32)
            norm_ref[...] = ref[SEG2 - 8 :, :].astype(F32)


def add_small_kernel(a, b, out_ref):
    out_ref[...] = a[...] + b[...]


def update_small_kernel(
    small, n0, n1, ng, ngm, nga, cv, cvm, cva, hd, hdm, hda, gg, ggm, gga, *outs, rates
):
    ng_o, cv_o, hd_o, gg_o = (outs[3 * n : 3 * n + 3] for n in range(4))
    at_norm = NG_AT - TAP_AT - (SMALL - 8)
    norms = [n[at_norm : at_norm + 1, :] for n in (n0, n1)]
    grad = (norms[0] + norms[1]).reshape(D)
    for ref, new in zip(ng_o, advance(ng[...], grad, ngm[...], nga[...], rates[0])):
        ref[...] = new
    grad = small[0:5, 0 : ZW + 2 * SW]
    old = [a[:, 0, :] for a in (cv, cvm, cva)]
    for ref, new in zip(cv_o, advance(old[0], grad, old[1], old[2], rates[2])):
        ref[:, 0, :] = new
    at_head = HD_AT - TAP_AT
    grad = small[at_head : at_head + 3, 0:NH]
    for ref, new in zip(hd_o, advance(hd[...], grad, hdm[...], hda[...], rates[3])):
        ref[...] = new
    at_gate = GG_AT - TAP_AT
    grad = small[at_gate : at_gate + 1, 0:ZW].reshape(ZW)
    for ref, new in zip(gg_o, advance(gg[...], grad, ggm[...], gga[...], rates[4])):
        ref[...] = new


def trade(axis, flip):
    count = lax.axis_size(axis)
    pairs = [(i, i ^ flip) for i in range(count)]
    return lambda array: lax.ppermute(array, axis, pairs)


def moved(array, by):
    count = lax.axis_size("seq")
    if count == 2 * abs(by):
        return trade("seq", abs(by))(array)
    pairs = [(i, i + by) for i in range(count) if 0 <= i + by < count]
    return lax.ppermute(array, "seq", pairs)


def grow(decay, state):
    return jnp.repeat(decay[0, 24 : 24 + NH], HDIM)[:, None] * state


def pieces_before(state, logs, way):
    count = lax.axis_size("seq") // GRP
    found = moved(state, way * GRP)
    by = 1
    if count > 2:
        there = lax.axis_index("seq") // GRP
        decay = moved(jnp.exp(logs), way * GRP)
        total = found.astype(F32)
        while by < count - 1:
            inside = (there >= by) if way > 0 else (there + by < count)
            earlier = moved(total.astype(BF16), way * GRP * by).astype(F32)
            total = jnp.where(inside, grow(decay, earlier) + total, total)
            decay = decay * moved(decay, way * GRP * by)
            by *= 2
        found = total.astype(BF16)
    return found


def group_sum(parts, height, after=()):
    return add_rows(height, [parts[0]] + [trade("seq", b)(parts[b]) for b in (1, 2, 3)], after)


def add_rows(height, arrays, after=()):
    spec = whole((height, D))
    out = [sds((height, D), BF16)]
    return call(sum_kernel, "sum", (1,), arrays, [spec] * len(arrays), out, [spec], after=after)[0]


def across_groups(mine, height, after=()):
    by = GRP
    while by < lax.axis_size("seq"):
        mine = add_rows(height, [mine, trade("seq", by)(mine)], after)
        by *= 2
    return mine


def all_quarters(mine):
    return [mine] + [trade("seq", b)(mine) for b in (1, 2, 3)]


def slot_of(height):
    return pl.BlockSpec((1, height, D), lambda i, at: (i, 0, 0))


def split_both(at, keep, other, after=()):
    return call(
        split_kernel, "split", (GRP,), (keep, other), [slot_of(HALF)] * 2,
        [sds((GRP, QUART, D)), sds((GRP, QUART, D), BF16)], [slot_of(QUART)] * 2,
        prefetch=at, after=after,
    )


def quarter_add(keep, other, after=()):
    every = whole((GRP, QUART, D))
    return call(
        add_kernel, "add", (1,), (keep, other), [every] * 2,
        [sds((QUART, D), BF16)] * 4, [whole((QUART, D))] * 4, after=after,
    )


def join_kernel(r0, r1, r2, r3, out_ref):
    for b, ref in enumerate((r0, r1, r2, r3)):
        out_ref[b] = ref[ref.shape[0] - QUART :, :]


def quarter_home(parts, after=()):
    return join([parts[0]] + [trade("seq", b)(parts[b]) for b in (1, 2, 3)], after)


def join(got, after=()):
    return call(
        join_kernel, "join", (1,), got, [whole(a.shape) for a in got],
        [sds((GRP, QUART, D), BF16)], [whole((GRP, QUART, D))], after=after,
    )[0]


def all_home(a):
    x = trade("head", 2)(a)
    return a, x, trade("head", 1)(a), trade("head", 1)(x)


def shards(
    block_in, cotangent, lengths,
    norm_gain, in_proj, conv_params, head_params, gate_gain, out_proj,
    norm_gain_momentum, in_proj_momentum, conv_momentum, head_momentum, gate_gain_momentum,
    out_proj_momentum,
    norm_gain_average, in_proj_average, conv_average, head_average, gate_gain_average,
    out_proj_average,
):
    seq_at, head_at = lax.axis_index("seq"), lax.axis_index("head")
    place = seq_at % GRP
    groups = lax.axis_size("seq") // GRP
    group = seq_at // GRP
    at = [place, head_at % 2, group, 0, head_at // 2, group > 0, group < groups - 1]
    at = jnp.concatenate([jnp.stack([jnp.asarray(v, jnp.int32) for v in at]), lengths])

    def turned(array):
        return jnp.transpose(array, (2, 1, 0))

    once = lengths[0] >= 0

    def apart(step):
        shapes = jax.eval_shape(step)
        return lax.cond(
            once, step, lambda: jax.tree.map(lambda s: jnp.zeros(s.shape, s.dtype), shapes)
        )

    anyspec = pl.BlockSpec(memory_space=pl.ANY)

    picked = pick(at, block_in, True)
    got = [picked[0]] + [trade("seq", b)(picked[b]) for b in (1, 2, 3)]
    w, wdt, low, send_bc, hp, vecs = call(
        prep_kernel, "prep", (1,),
        (turned(in_proj), out_proj, conv_params, head_params, norm_gain, gate_gain),
        [anyspec, whole((ZW, D)), whole((5, 1, 448)), whole((3, NH)), whole((D,)), whole((ZW,))],
        [sds((WROWS, D), BF16), sds((LANES, D), BF16), sds((ZW, D), BF16), sds((80, D), BF16),
         sds((8, LANES)), sds((8, D))],
        [whole((WROWS, D)), whole((LANES, D)), whole((ZW, D)), whole((80, D)), whole((8, LANES)), whole((8, D))],
        scratch=[pltpu.VMEM((COLS, D), F32), pltpu.VMEM((8, LANES), F32), pltpu.SemaphoreType.DMA],
        after=(picked[0],),
    )
    bcs = [send_bc] + [trade("head", b)(send_bc) for b in (1, 2, 3)]
    own, edge = stack(at, got, (w,))
    oth = trade("head", 1)(own)
    halo = moved(edge, GRP)
    cot_picked = pick(at, cotangent, False, (own,))
    cot_got = [cot_picked[0]] + [trade("seq", b)(cot_picked[b]) for b in (1, 2, 3)]

    def wblock(n, height):
        return pl.BlockSpec((height, D), lambda i, *_: (n, 0))

    nrm, z, info, rowc, logs = call(
        first_kernel, "first", (GRP,), (own, oth, vecs, w, wdt, hp),
        [slot(HALF), slot(HALF), whole((8, D)), wblock(0, ZW), whole((LANES, D)), whole((8, LANES))],
        [sds((TOK, D), BF16), sds((TOK, ZW)), sds((TOK, LANES)), sds((8, TOK)), sds((8, LANES))],
        [rows(D), rows(ZW), rows(LANES), pl.BlockSpec((8, BLK), lambda i, *_: (0, i)), whole((8, LANES))],
        scratch=[pltpu.VMEM((8, LANES), F32)], prefetch=at, flops=2 * TOK * D * 512, after=(halo, *bcs[1:]),
    )
    hspec = pl.BlockSpec((1, ZW, ST), lambda i, *_: (i, 0, 0))
    rowspec = pl.BlockSpec((8, BLK), lambda i, *_: (0, i))
    mx, px, xa, xdt, mo, po, bb, cc, hloc, fresh = call(
        mix_kernel, "mix", (GRP,), (nrm, halo, vecs, w, w, *bcs, conv_params, info),
        [rows(D), whole((16, D)), whole((8, D)), wblock(1, ZW), wblock(12, 2 * SW)]
        + [whole((80, D))] * 4 + [whole((5, 1, 448)), rows(LANES)],
        [sds((TOK, ZW)), sds((TOK, ZW)), sds((TOK, ZW)), sds((TOK, ZW), BF16), sds((TOK, 2 * SW)),
         sds((TOK, 2 * SW)), sds((TOK, ST), BF16), sds((TOK, ST), BF16), sds((GRP, ZW, ST)),
         sds((ZW, ST), BF16)],
        [rows(ZW), rows(ZW), rows(ZW), rows(ZW), rows(2 * SW), rows(2 * SW), rows(ST), rows(ST),
         hspec, whole((ZW, ST))],
        scratch=[pltpu.VMEM((2 * ST, D), BF16), pltpu.VMEM((8, 2 * ST), F32),
                 pltpu.VMEM((BLK + 8, ZW + 2 * ST), F32), pltpu.VMEM((BLK + 8, 2 * SW), F32),
                 pltpu.VMEM((ZW, ST), F32)],
        flops=2 * TOK * D * 704, prefetch=at,
    )
    hin = pieces_before(fresh, logs, 1)
    cot_own = stack(at, cot_got, (fresh,))[0]
    cot_oth = trade("head", 1)(cot_own)
    yl, dyn, w_live = call(
        local_kernel, "local", (GRP,),
        (xdt, xa, bb, cc, info, rowc, hloc, cot_own, cot_oth, low, vecs),
        [rows(ZW), rows(ZW), rows(ST), rows(ST), rows(LANES), rowspec, hspec, slot(HALF),
         slot(HALF), whole((ZW, D)), whole((8, D))],
        [sds((TOK, ZW)), sds((TOK, ZW)), sds((TOK, D), BF16)], [rows(ZW), rows(ZW), rows(D)],
        prefetch=at, flops=2 * TOK * (D * ZW + 4 * BLK * ZW),
    )
    y, sums = call(
        gate_kernel, "gate", (GRP,), (yl, cc, info, hin, z, dyn, vecs),
        [rows(ZW), rows(ST), rows(LANES), whole((ZW, ST)), rows(ZW), rows(ZW), whole((8, D))],
        [sds((TOK, ZW)), sds((8, TOK))], [rows(ZW), rowspec], prefetch=at, flops=2 * TOK * ST * ZW,
    )
    all_sums = [sums] + [trade("head", b)(sums) for b in (1, 2, 3)]
    half_slot = pl.BlockSpec((1, HALF, D), lambda i, at: (i ^ at[0], 0, 0))
    dy, dz, yn, pulled, g_gate, keep, send = call(
        ungate_kernel, "ungate", (GRP,), (y, z, dyn, *all_sums, info, cc, vecs, low),
        [rows(ZW)] * 3 + [rowspec] * 4 + [rows(LANES), rows(ST), whole((8, D)), whole((ZW, D))],
        [sds((TOK, ZW)), sds((TOK, ZW), BF16), sds((TOK, ZW), BF16), sds((ZW, ST), BF16), sds((8, ZW))]
        + [sds((GRP, HALF, D), BF16)] * 2,
        [rows(ZW), rows(ZW), rows(ZW), whole((ZW, ST)), whole((8, ZW))] + [half_slot] * 2,
        scratch=[pltpu.VMEM((ZW, ST), F32)], flops=2 * TOK * (ST + D) * ZW, prefetch=at,
    )
    grads1 = call(
        out_kernel, "out", (GRP,), (yn, w_live, nrm, dz), [rows(ZW), rows(D), rows(D), rows(ZW)],
        [sds((SEG1, D), BF16)] * 4, [whole((SEG1, D))] * 4,
        scratch=[pltpu.VMEM((2 * ZW, D), F32)], prefetch=at, flops=4 * TOK * D * ZW,
    )
    got1 = [trade("seq", b)(grads1[b]) for b in (1, 2, 3)]
    keep2, send2 = split_both(at, keep, trade("head", 1)(send), (grads1[0],))
    other2 = trade("head", 2)(send2)
    hback = pl.BlockSpec((1, ZW, ST), lambda i, *_: (GRP - 1 - i, 0, 0))

    after = pieces_before(pulled, logs, -1)
    dxi, dbi, dci, dcum, hall = call(
        inner_kernel, "inner", (GRP,), (xdt, bb, cc, info, rowc, dy, hloc, hin),
        [rows(ZW), rows(ST), rows(ST), rows(LANES), rowspec, rows(ZW), hspec, whole((ZW, ST))],
        [sds((TOK, ZW)), sds((TOK, ST)), sds((TOK, ST)), sds((TOK, LANES)), sds((GRP, ZW, ST))],
        [rows(ZW), rows(ST), rows(ST), rows(LANES), hspec], prefetch=at, after=(send2,),
    )
    dpx, halo_x, *dbc, draw, g_head = call(
        back_kernel, "back", (GRP,),
        (after, dxi, dbi, dci, dcum, hall, xa, px, bb, cc, info, dy, hp, vecs),
        [whole((ZW, ST)), rows_back(ZW), rows_back(ST), rows_back(ST), rows_back(LANES), hback,
         rows_back(ZW), rows_back(ZW), rows_back(ST), rows_back(ST), rows_back(LANES),
         rows_back(ZW), whole((8, LANES)), whole((8, D))],
        [sds((TOK, ZW)), sds((8, ZW))] + [sds((TOK // 2, LANES), BF16)] * 4 + [sds((TOK, LANES), BF16), sds((8, LANES))],
        [rows_back(ZW), whole((8, ZW))] + [rows_back(LANES, HALF)] * 4 + [rows_back(LANES), whole((8, LANES))],
        scratch=[pltpu.VMEM((ZW, ST), F32)], flops=2 * TOK * 4 * ST * ZW, prefetch=at,
    )
    quarters = quarter_add(keep2, other2, (g_head,))
    one, joint = whole((SEG1, D)), whole((SEG1 + QUART, D))

    def after_rows(width):
        last = TOK // 8 - 1
        return pl.BlockSpec((8, width), lambda i, *_: (min((i + 1) * (BLK // 8), last) if isinstance(i, int) else jnp.minimum((i + 1) * (BLK // 8), last), 0))

    final = GRP * SEG2
    half_rows = pl.BlockSpec((1, HALF, D), lambda i, at: (i ^ at[0], 0, 0))

    bc_got = [trade("head", b)(dbc[b]) for b in (1, 2, 3)]
    pb, end, acc = call(
        last_x_kernel, "last_x", (GRP,),
        (dpx, dpx, mx, conv_params, dz, draw, nrm, w, wdt),
        [rows(ZW), after_rows(ZW), rows(ZW), whole((5, 1, 448)), rows(ZW), rows(LANES),
         rows(D), whole((2 * ZW, D)), whole((LANES, D))],
        [sds((TOK, D)), sds((END, ZW)), sds((final, D))], [rows(D), whole((END, ZW)), whole((final, D))],
        scratch=[pltpu.VMEM((BLK + 8, ZW), F32)], prefetch=at, flops=4 * TOK * D * 2 * ZW, after=(quarters[0],),
    )
    dpo, halo_o = call(
        edge_kernel, "edge", (GRP,), (dbc[0], *bc_got, po, halo_x),
        [rows(LANES, HALF)] * 4 + [rows(2 * SW), whole((8, ZW))],
        [sds((TOK, 2 * SW)), sds((8, ZW + LANES))], [rows(2 * SW), whole((8, ZW + LANES))], after=(acc,),
    )
    halo_o = moved(halo_o, -GRP)
    mine1 = add_rows(SEG1, [grads1[0], *got1], (halo_o,))
    keep_b, send_b, *grads2 = call(
        last_o_kernel, "last_o", (GRP,),
        (dpo, dpo, halo_o, mo, conv_params, nrm, w, w, pb, vecs, g_gate, g_head, acc, end, mx),
        [rows(2 * SW), after_rows(2 * SW), whole((8, ZW + LANES)), rows(2 * SW), whole((5, 1, 448)), rows(D),
         wblock(12, 2 * SW), wblock(1, ZW), rows(D), whole((8, D)), whole((8, ZW)), whole((8, LANES)), whole((final, D)),
         whole((END, ZW)), pl.BlockSpec((END, ZW), lambda i, *_: (TOK // END - 1, 0))],
        [sds((GRP, HALF, D), BF16)] * 2 + [sds((SEG2, D), BF16)] * 4,
        [half_rows] * 2 + [whole((SEG2, D))] * 4,
        scratch=[pltpu.VMEM((BLK + 8, 2 * SW), F32), pltpu.VMEM((final, D), F32), pltpu.VMEM((BLK, D), F32)],
        prefetch=at, flops=4 * TOK * D * 2 * SW, after=(mine1,),
    )

    def finish():
        keep3, send3 = split_both(at, keep_b, trade("head", 1)(send_b))
        quarters_b = quarter_add(keep3, trade("head", 2)(send3))
        mine2 = group_sum(grads2, SEG2, (quarters_b[0],))
        own = quarter_home(quarters, (mine2,))
        return quarters_b, mine2, own, across_groups(mine1, SEG1, (own,))

    quarters_b, mine2, own_out, total1 = apart(finish)
    x_out = trade("head", 2)(own_out)
    root = math.sqrt(TOK * lax.axis_size("seq"))
    mat = whole((ZW, D))
    turned3 = [turned(p) for p in (in_proj, in_proj_momentum, in_proj_average)]
    turned_shape = [sds((COLS, 1, D))] * 3
    buffers = [pltpu.VMEM((COLS, D), F32)] * 6 + [pltpu.SemaphoreType.DMA((5, 6))]
    hbm = pl.BlockSpec(memory_space=pltpu.HBM)

    def gather():
        own_grad = quarter_home(quarters_b)
        return own_grad, across_groups(mine2, SEG2, (own_grad,))

    own_grad, total2 = apart(gather)
    sums1 = all_quarters(total1)
    def spread_out():
        x_grad = trade("head", 2)(own_grad)
        core_grad, sums2 = trade("head", 1)(own_grad), all_quarters(total2)
        parts = (own_out, x_out, trade("head", 1)(own_out), trade("head", 1)(x_out))
        block_out, _ = home(home_out_kernel, "home_out", at, (block_in,), (None,), parts, BF16)
        return x_grad, core_grad, sums2, block_out

    x_grad, core_grad, sums2, block_out = apart(spread_out)
    grad_parts = (own_grad, x_grad, core_grad, trade("head", 1)(x_grad))

    quarter = whole((SEG2, D))
    small, norm, done_small = call(
        small_kernel, "small", (1,), sums2, [quarter] * 4, [sds((SMALL, D)), sds((8, D))],
        [whole((SMALL, D)), whole((8, D))], prefetch=at, token=True,
    )
    *in_half, done_b = call(
        functools.partial(update_b_kernel, rate=RATES[1] / root), "update_b", (1,),
        (*sums2, *turned3), [quarter] * 4 + [hbm] * 3, turned_shape, [hbm] * 3,
        scratch=[pltpu.VMEM((GRP * SEG2, D), F32)] + buffers, prefetch=at,
        after=(done_small,), vmem=56, token=True,
    )
    eight = whole((8, D))
    norm = call(
        add_small_kernel, "add_small", (1,), (norm, trade("head", 1)(norm)), [eight] * 2, [sds((8, D))], [eight],
        after=(done_b,),
    )[0]
    norms = [norm, trade("head", 2)(norm)]
    input_grad, done_grad = home(
        home_grad_kernel, "home_grad", at, (block_in, cotangent, vecs), (None, None, (8, D)),
        grad_parts, F32, (done_b,),
    )
    out_w, out_m, out_a, *in_new, done_a = call(
        functools.partial(update_a_kernel, rate=RATES[5] / root, rate_in=RATES[1] / root), "update_a", (1,),
        (*sums1, out_proj, out_proj_momentum, out_proj_average, *turned3, *in_half),
        [one] * 4 + [mat] * 3 + [hbm] * 6, [sds((ZW, D))] * 3 + turned_shape,
        [mat] * 3 + [hbm] * 3, scratch=[pltpu.VMEM((2 * ZW, D), F32)] + buffers, prefetch=at,
        after=(done_grad,), aliases={11: 3, 12: 4, 13: 5}, vmem=56, token=True,
    )
    groups_of = (
        (norm_gain, norm_gain_momentum, norm_gain_average),
        (conv_params, conv_momentum, conv_average),
        (head_params, head_momentum, head_average),
        (gate_gain, gate_gain_momentum, gate_gain_average),
    )
    arrays = [a for three in groups_of for a in three]
    specs = [whole(a.shape) for a in arrays]
    new = call(
        functools.partial(update_small_kernel, rates=[r / root for r in RATES]), "update_small", (1,),
        (small, *norms, *arrays), [whole((SMALL, D))] + [whole((8, D))] * 2 + specs,
        [sds(a.shape) for a in arrays], specs, after=(done_a,),
    )
    ng3, cv3, hd3, gg3 = (tuple(new[3 * n : 3 * n + 3]) for n in range(4))
    in3 = tuple(turned(a) for a in in_new)
    return (block_out, input_grad, *ng3, *in3, *cv3, *hd3, *gg3, out_w, out_m, out_a)


def solution(mesh):
    act, vec, mat = P(None, "seq", None), P(), P(None, "head", None)
    weights = (vec, mat, mat, P(None, "head"), P("head"), P("head", None))
    outs = tuple(spec for spec in weights for _ in range(3))
    return jax.shard_map(
        shards,
        mesh=mesh,
        in_specs=(act, act, P(), *weights, *weights, *weights),
        out_specs=(act, act, *outs),
        check_vma=False,
    )
```
